128 devices in a mesh: dp: 8 (over z_lo, x), ctx: 16 (over z_hi, y, core).
Axes of the slice: x: 4, y: 4, z: 4 (z_hi: 2, z_lo: 2; z = z_hi * 2 + z_lo), core: 2. Of those that a mesh axis runs over, the one named last changes fastest.
Arguments:
- queries: bfloat16 [8, 8192, 2048], P('dp', 'ctx'), may hold values from -216 to 216
- key_rows: bfloat16 [8, 8192, 2048], P('dp', 'ctx'), may hold values from -8 to 8
- value_rows: bfloat16 [8, 8192, 2048], P('dp', 'ctx'), may hold values from -6 to 6
- document_ids: int32 [8, 8192], P('dp', 'ctx'), may hold values from 0 to 7, never falling along the last dimension, each value on 1 to 2048 neighbouring positions
- dilation_offsets: int32 [4, 16], replicated, may hold values from 0 to 1023
Outputs:
- attended: bfloat16 [8, 8192, 2048], P('dp', 'ctx')
The draws below stay inside these ranges and needn't reach their ends.
All inputs are finite; a program needn't handle non-finite values.
Results may differ from the reference program's by a relative error of at most 0.0035.
Values may be sent and summed in bfloat16 or wider, within the bound.
A program may use at most 192 MiB of HBM per device.

```python
import math
import jax
import jax.numpy as jnp
import numpy as np
from jax import lax

H = 16
ROWS = 512
LEVELS = 4
SEQS = 8
LENGTH = 8192
HH = 2048
N_CTX = 16


def pair_base(key):
    return jnp.clip(jax.random.normal(key, (SEQS, LENGTH, HH), jnp.float32), -6.0, 6.0)


def draw_key_rows(key, part):
    base = pair_base(key)
    return base.astype(jnp.bfloat16)


def draw_queries(key, part):
    key = jax.random.fold_in(key, 5)
    own_rows = jnp.clip(jax.random.normal(key, (SEQS, LENGTH, HH), jnp.float32), -6.0, 6.0)
    return own_rows.astype(jnp.bfloat16)


def set_ends(values, own_key, low, top_value):
    dims = values.shape
    spot = [jax.random.randint(jax.random.fold_in(own_key, axis), (), 0, dims[axis]) for axis in range(len(dims))]
    values = values.at[tuple(spot)].set(low)
    longest = dims.index(max(dims))
    spot[longest] = (spot[longest] + 1) % dims[longest]
    return values.at[tuple(spot)].set(top_value)


def level_of(rng, extent, split, low, largest):
    def one(position, shards_of):
        steps = jax.random.uniform(jax.random.fold_in(jax.random.fold_in(rng, 6), position), (shards_of,), jnp.float32, low / len(split), largest / len(split))
        return jnp.repeat(jnp.exp(steps), extent[position] // shards_of).reshape((-1,) + (1,) * (len(extent) - position - 1))

    loudness = one(*split[0])
    for cut in split[1:]:
        loudness = loudness * one(*cut)
    return loudness


def profile(number_of, total, limit, slope):
    weights = [(1 << 20) // math.isqrt(grade ** slope) + 1 for grade in range(2, number_of + 1)]
    surplus, given = total - limit - (number_of - 1), [1] * (number_of - 1)
    while surplus > 0:
        free = [i for i in range(number_of - 1) if given[i] < limit]
        whole, budget = sum([weights[i] for i in free]), surplus
        for i in free:
            more = min(limit - given[i], max(1, budget * weights[i] // whole), surplus)
            given[i] = given[i] + more
            surplus = surplus - more
    return np.array([limit] + given)


def uneven(stream_key, count, total, limit, skew):
    if count == 2:
        one = jax.random.randint(stream_key, (), max(1, total - limit), min(limit, total - 1) + 1)
        return jnp.stack([one, total - one])
    sizes = jnp.asarray(profile(count, total, limit, skew), jnp.int32)
    couples = (count - 1) // 2
    giver, taker = sizes[1:1 + 2 * couples:2], sizes[2:2 + 2 * couples:2]
    slack = jnp.minimum(giver - 1, limit - taker)
    passed = jax.random.randint(jax.random.fold_in(stream_key, 1), (couples,), 0, 1 << 20) % (slack + 1)
    sizes = sizes.at[1:1 + 2 * couples:2].set(giver - passed).at[2:2 + 2 * couples:2].set(taker + passed)
    return sizes[jax.random.permutation(jax.random.fold_in(stream_key, 2), count)]


def centred(stream_key, shape, deviation, limit, shards=(), held_as=jnp.bfloat16):
    array = deviation * jax.random.normal(stream_key, shape, jnp.float32)
    if shards:
        array = array * level_of(stream_key, shape, shards, -0.22, 0.18)
    return jnp.clip(array, -limit, limit).astype(held_as)


def setup_inputs(seed: int = 0) -> dict:
    key_list = jax.random.split(jax.random.key(seed), 6)
    queries = draw_queries(jax.random.fold_in(key_list[5], 71), 0)
    key_rows = draw_key_rows(jax.random.fold_in(key_list[5], 71), 0)
    value_rows = centred(key_list[2], (SEQS, LENGTH, HH), 1.0, 6.0, ((0, 8), (1, 16)))
    document_ids = jax.vmap(lambda own: jnp.searchsorted(jnp.cumsum(uneven(own, N_CTX // 2, LENGTH, 4 * ROWS, 1)), jnp.arange(LENGTH), side="right"))(jax.random.split(key_list[3], SEQS)).reshape((SEQS, LENGTH)).astype(jnp.int32)
    dilation_offsets = set_ends(jax.random.randint(key_list[4], (LEVELS, H), 0, 1024), jax.random.fold_in(key_list[4], 1), 0, 1023).astype(jnp.int32)
    return dict(queries=queries, key_rows=key_rows, value_rows=value_rows, document_ids=document_ids, dilation_offsets=dilation_offsets)


def softmax_terms(query_block, key_block, value_block, allowed, scaling):
    scores = jnp.einsum('...qd,...kd->...qk', query_block.astype(jnp.float32), key_block.astype(jnp.float32)) * scaling
    scores = jnp.where(allowed, scores, -1e+30)
    maxima = lax.optimization_barrier(jnp.max(scores, axis=-1))
    weights = jnp.exp(scores - maxima[..., None])
    totals = lax.optimization_barrier(jnp.sum(weights, axis=-1))
    rounded = lax.optimization_barrier(weights.astype(jnp.bfloat16)).astype(jnp.float32)
    accumulated = jnp.einsum('...qk,...kd->...qd', rounded, value_block.astype(jnp.float32))
    return (maxima, totals, accumulated)

def join_terms(old_terms, new_terms):
    old_max, old_tot, old_acc = old_terms
    new_max, new_tot, new_acc = new_terms
    highest = jnp.maximum(old_max, new_max)
    old_scale = jnp.exp(old_max - highest)
    new_scale = jnp.exp(new_max - highest)
    return (highest, old_tot * old_scale + new_tot * new_scale, old_acc * old_scale[..., None] + new_acc * new_scale[..., None])

def pick_rows(head_major, shifts, span_size):
    heads = head_major.shape[0]
    row_count = head_major.shape[1]
    view = head_major.reshape((heads, row_count // span_size, span_size) + head_major.shape[2:])
    index_shape = (heads, 1, 1) + (1,) * (head_major.ndim - 2)
    return jnp.take_along_axis(view, shifts.reshape(index_shape), axis=2)[:, :, 0]

def put_rows(old_rows, new_rows, shifts, span_size):
    heads = old_rows.shape[0]
    row_count = old_rows.shape[1]
    view = old_rows.reshape((heads, row_count // span_size, span_size) + old_rows.shape[2:])
    chosen = jnp.arange(span_size, dtype=jnp.int32)[None, :] == shifts[:, None]
    chosen = chosen.reshape((heads, 1, span_size) + (1,) * (old_rows.ndim - 2))
    return jnp.where(chosen, new_rows[:, :, None], view).reshape(old_rows.shape)

def to_heads(rows_in, heads):
    length = rows_in.shape[0]
    return rows_in.reshape(length, heads, -1).transpose(1, 0, 2)

def one_pack(pack, dilation_offsets):
    q_rows, k_rows, v_rows, docs = pack
    heads = dilation_offsets.shape[1]
    length = q_rows.shape[0]
    width = q_rows.shape[1] // heads
    scaling = 1.0 / math.sqrt(width)
    q_heads = to_heads(q_rows, heads)
    k_heads = to_heads(k_rows, heads)
    v_heads = to_heads(v_rows, heads)
    half_rows = ROWS // 2
    blocks = length // half_rows
    causal_half = jnp.arange(half_rows)[:, None] >= jnp.arange(half_rows)[None, :]

    def local_block(block_number):
        begin_at = block_number * half_rows
        doc_block = lax.dynamic_slice_in_dim(docs, begin_at, half_rows, 0)
        allowed = causal_half & (doc_block[:, None] == doc_block[None, :])
        return softmax_terms(lax.dynamic_slice_in_dim(q_heads, begin_at, half_rows, 1), lax.dynamic_slice_in_dim(k_heads, begin_at, half_rows, 1), lax.dynamic_slice_in_dim(v_heads, begin_at, half_rows, 1), allowed[None], scaling)
    terms = lax.map(local_block, jnp.arange(blocks, dtype=jnp.int32))
    state = (jnp.moveaxis(terms[0], 0, 1).reshape(heads, length), jnp.moveaxis(terms[1], 0, 1).reshape(heads, length), jnp.moveaxis(terms[2], 0, 1).reshape(heads, length, width))
    causal_full = jnp.arange(ROWS)[:, None] >= jnp.arange(ROWS)[None, :]
    head_docs = jnp.broadcast_to(docs[None, :], (heads, length))
    for level_num in range(LEVELS):
        span_size = N_CTX >> LEVELS - 1 - level_num
        segments = N_CTX // span_size
        shifts = jnp.remainder(dilation_offsets[level_num], span_size).astype(jnp.int32)
        sel_q = pick_rows(q_heads, shifts, span_size).reshape(heads, segments, ROWS, width)
        sel_k = pick_rows(k_heads, shifts, span_size).reshape(heads, segments, ROWS, width)
        sel_v = pick_rows(v_heads, shifts, span_size).reshape(heads, segments, ROWS, width)
        sel_doc = pick_rows(head_docs, shifts, span_size).reshape(heads, segments, ROWS)

        def dilated_block(segment_number):
            doc_block = lax.dynamic_index_in_dim(sel_doc, segment_number, 1, False)
            allowed = causal_full[None] & (doc_block[:, :, None] == doc_block[:, None, :])
            return softmax_terms(lax.dynamic_index_in_dim(sel_q, segment_number, 1, False), lax.dynamic_index_in_dim(sel_k, segment_number, 1, False), lax.dynamic_index_in_dim(sel_v, segment_number, 1, False), allowed, scaling)
        level_terms = lax.map(dilated_block, jnp.arange(segments, dtype=jnp.int32))
        level_terms = (jnp.moveaxis(level_terms[0], 0, 1).reshape(heads, length // span_size), jnp.moveaxis(level_terms[1], 0, 1).reshape(heads, length // span_size), jnp.moveaxis(level_terms[2], 0, 1).reshape(heads, length // span_size, width))
        old_sel = tuple((pick_rows(member, shifts, span_size) for member in state))
        joined = join_terms(old_sel, level_terms)
        state = tuple((put_rows(member, fresh, shifts, span_size) for member, fresh in zip(state, joined)))
    result = state[2] / state[1][..., None]
    return result.transpose(1, 0, 2).reshape(length, heads * width).astype(jnp.bfloat16)

def reference(queries, key_rows, value_rows, document_ids, dilation_offsets):
    return lax.map(lambda pack: one_pack(pack, dilation_offsets), (queries, key_rows, value_rows, document_ids))
```

```python
import math

import jax
import jax.numpy as jnp
from jax import lax
from jax.experimental import pallas as pl
from jax.experimental.pallas import tpu as pltpu
from jax.sharding import PartitionSpec as P

MESH = pl.DeviceIdType.MESH
F32, BF16, I32 = jnp.float32, jnp.bfloat16, jnp.int32
HEADS, HALF, ROWS, DIM, CHUNK = 16, 8, 512, 128, 256
SEL, FAR, FAR3 = 240, 112, 48
REGIONS = ((0, 128, 1), (128, 64, 2), (192, 32, 3), (224, 16, 4))
NEG = -1e30
SCALE2 = math.log2(math.e) / math.sqrt(DIM)


def nt(a, b):
    return lax.dot_general(a, b, (((1,), (1,)), ((), ())), preferred_element_type=F32)


def nn(a, b):
    return jnp.dot(a, b, preferred_element_type=F32)


def split3(x):
    first = x.astype(BF16)
    rest = x - first.astype(F32)
    second = rest.astype(BF16)
    third = (rest - second.astype(F32)).astype(BF16)
    return jnp.concatenate([first, second, third], axis=0)


def fold3(x):
    n = x.shape[0] // 3
    return (x[2 * n :] + x[n : 2 * n]) + x[:n]


def iota(shape, dim):
    return lax.broadcasted_iota(I32, shape, dim)


def attend(q, k, v, bias):
    s = nt(q, k)
    if bias is not None:
        s = bias(s)
    top = jnp.max(s, axis=1, keepdims=True)
    w = jnp.exp2((s - top) * SCALE2).astype(BF16)
    both = nn(w, jnp.concatenate([v, jnp.ones_like(v)], axis=1))
    total = both[:, DIM:]
    return both[:, :DIM] / total, top * SCALE2 + jnp.log2(total)


def kernel(
    q_hbm, k_hbm, v_hbm, docs_ref, off_ref, out_hbm,
    qv, kv, vv, ov,
    cq, ck, cv, sq, sk, sv, q1in, q2in, pbuf,
    ob, oo_in, os1, os2, or1, or2, o0,
    st_own, st1, st2, lse0,
    ls_own, ls1, ls2, lo_in, lr1, lr2,
    docs_all, ot_q, ot_k, base_m, causal, bias0, al_own, al_far, a0,
    load_sem, store_sem, d_send, d_recv, x_send, x_recv,
    q1_send, q1_recv, q2_send, q2_recv, o1_send, o1_recv, o2_send, o2_recv,
    oo_send, oo_recv, l_send, l_recv,
):
    me = lax.axis_index("ctx")
    dp = lax.axis_index("dp")
    c = me // 2
    j = me % 2

    def device(steps, core):
        return (dp, ((c + steps + 8) % 8) * 2 + core)

    def remote(src, dst, send, recv, to):
        return pltpu.make_async_remote_copy(
            src_ref=src, dst_ref=dst, send_sem=send, recv_sem=recv, device_id=to, device_id_type=MESH
        )

    loads = [
        pltpu.make_async_copy(src.at[0], dst, load_sem.at[i])
        for i, (src, dst) in enumerate(((q_hbm, qv), (k_hbm, kv), (v_hbm, vv)))
    ]
    for load in loads:
        load.start()

    def clear(h, _):
        or1[h] = jnp.zeros(or1.shape[1:], BF16)
        or2[h] = jnp.zeros(or2.shape[1:], BF16)
        return 0

    lax.fori_loop(0, HEADS, clear, 0)

    def clear_pads(t, _):
        for b in range(2):
            oo_in[t, b, SEL:] = jnp.zeros((CHUNK - SEL, DIM), BF16)
            for d in range(2):
                ob[d, t, b, SEL:] = jnp.zeros((CHUNK - SEL, DIM), BF16)
        return 0

    lax.fori_loop(0, HALF, clear_pads, 0)

    barrier = pltpu.get_barrier_semaphore()
    greeted = [(0, 1 - j)] + [(g, core) for g in (-2, -1, 1, 2) for core in (0, 1)]
    for g, core in greeted:
        pl.semaphore_signal(barrier, inc=1, device_id=device(g, core), device_id_type=MESH)
    pl.semaphore_wait(barrier, len(greeted))

    docs_sent = [(0, 1 - j)] + [(-g, core) for g in (1, 2) for core in (0, 1)]
    docs_copies = [
        remote(docs_ref, docs_all.at[2 * -g + j], d_send.at[i], d_recv.at[2 * -g + j], device(g, core))
        for i, (g, core) in enumerate(docs_sent)
    ]
    for copy in docs_copies:
        copy.start()
    docs_all[j] = docs_ref[...]

    for first, count, bits in REGIONS:
        base_m[first : first + count] = iota((count, CHUNK), 1) - (iota((count, CHUNK), 0) << bits)
    causal[...] = jnp.where(iota((CHUNK, CHUNK), 1) <= iota((CHUNK, CHUNK), 0), 0.0, NEG)
    eye = jnp.where(iota((CHUNK, CHUNK), 1) == iota((CHUNK, CHUNK), 0), 1.0, 0.0).astype(BF16)
    for b in range(2):
        same = docs_ref[:, b * CHUNK : (b + 1) * CHUNK] == iota((DIM, CHUNK), 0)
        q_one = nt(eye, jnp.where(same, 1.0, 0.0).astype(BF16)).astype(BF16)
        k_one = nt(eye, jnp.where(same, 0.0, NEG).astype(BF16)).astype(BF16)
        bias0[b] = nt(q_one, k_one) + causal[...]

    for load in loads:
        load.wait()

    def q1_cases(chip):
        return (((chip >= 1) & (chip % 2 == 1), 0), ((chip >= 1) & (chip % 2 == 0), 64))

    def q2_cases(chip):
        return (((chip >= 2) & (chip % 4 >= 2), 0), ((chip >= 2) & (chip % 4 < 2), 32))

    def q1_copy(src, t, d, low, send, core):
        return remote(
            src.at[:, pl.ds(128 + low, FAR - low)],
            q1in.at[t, pl.ds(2 * d, 2), pl.ds(low, FAR - low)],
            q1_send.at[send, t], q1_recv.at[d, t], device(-1, core),
        )

    def q2_copy(src, t, d, low, send, core):
        return remote(
            src.at[:, pl.ds(192 + low, FAR3 - low)],
            q2in.at[t, pl.ds(2 * d, 2), pl.ds(low, FAR3 - low)],
            q2_send.at[send, t], q2_recv.at[d, t], device(-2, core),
        )

    def q_sources(t):
        return ((sq.at[t], 0, 1 - j), (cq.at[t, pl.ds(2 * j, 2)], 1, j))

    def each_q_send(t, which, do):
        src, send, core = q_sources(t)[which]
        for present, low in q1_cases(c):

            @pl.when(present)
            def _():
                do(q1_copy(src, t, j, low, send, core))

        for present, low in q2_cases(c):

            @pl.when(present)
            def _():
                do(q2_copy(src, t, j, low, send, core))

    def exchange(t):
        return [
            remote(
                src.at[t], dst.at[t, pl.ds(2 * j, 2)], x_send.at[i, t], x_recv.at[i, t], device(0, 1 - j)
            )
            for i, (src, dst) in enumerate(((sq, cq), (sk, ck), (sv, cv)))
        ]

    def picker(h):
        parts = []
        for level, (first, count, bits) in enumerate(REGIONS):
            shift = off_ref[level, h] & ((1 << bits) - 1)
            parts.append(jnp.where(base_m[first : first + count] == shift, 1.0, 0.0))
        return jnp.concatenate(parts, axis=0).astype(BF16)

    def columns(ref, h):
        return ref[:, pl.ds(pl.multiple_of(h * DIM, DIM), DIM)]

    def select(pick, ref, h):
        x = columns(ref, h)
        both = nn(pick, jnp.concatenate([x[:CHUNK], x[CHUNK:]], axis=1)).astype(BF16)
        return both[:, :DIM], both[:, DIM:]

    def select_head(t, _):
        for which in range(2):
            h = HALF * (1 - j) + t if which == 0 else HALF * j + t
            pick = picker(h)
            if which == 1:
                pbuf[t] = pick
            for ref, mine, theirs in ((qv, cq, sq), (kv, ck, sk), (vv, cv, sv)):
                for b, part in enumerate(select(pick, ref, h)):
                    if which == 0:
                        theirs[t, b] = part
                    else:
                        mine[t, 2 * j + b] = part
                if ref is qv:
                    each_q_send(t, which, lambda copy: copy.start())
            if which == 0:
                for copy in exchange(t):
                    copy.start()
        return 0

    lax.fori_loop(0, HALF, select_head, 0)

    for i, slot in enumerate((1 - j, 2, 3, 4, 5)):
        remote(docs_ref, docs_all.at[slot], d_send.at[i], d_recv.at[slot], device(0, 1 - j)).wait_recv()
    for b in range(2):
        span = slice(b * CHUNK, (b + 1) * CHUNK)
        ones = [
            jnp.where(docs_all[g, :, span] == iota((8, CHUNK), 0), 1.0, 0.0) for g in range(6)
        ] + [jnp.zeros((DIM - 48, CHUNK), F32)]
        ot_q[b * DIM : (b + 1) * DIM] = jnp.concatenate(ones, axis=0).astype(BF16)
        for d in range(2):
            same = docs_all[d, :, span] == (iota((DIM, CHUNK), 0) & 7)
            ot_k[d, b * DIM : (b + 1) * DIM] = jnp.where(same, 0.0, NEG).astype(BF16)

    lane = iota((1, DIM), 1)

    def keep(ref, index, rows, t, value):
        old = ref[index + (rows,)]
        ref[index + (rows,)] = jnp.where(lane == t, value, old)

    def ret_copies(t, g, low, d):
        if g == 1:
            rows = pl.ds(low, FAR - low)
            return remote(
                os1.at[d, t, :, rows], or1.at[HALF * j + t, :, rows],
                o1_send.at[d, t], o1_recv.at[j, t], device(1, d),
            )
        return remote(
            os2.at[d, t, :, pl.ds(low, FAR3 - low)],
            or2.at[HALF * j + t, :, pl.ds(64 + low, FAR3 - low)],
            o2_send.at[d, t], o2_recv.at[j, t], device(2, d),
        )

    def partner_out(t):
        return remote(
            ob.at[1 - j, t, :, pl.ds(0, SEL)], oo_in.at[t, :, pl.ds(0, SEL)],
            oo_send.at[t], oo_recv.at[t], device(0, 1 - j),
        )

    def local_head(h):
        q, k, v = columns(qv, h), columns(kv, h), columns(vv, h)
        for b in range(2):
            span = slice(b * CHUNK, (b + 1) * CHUNK)
            o, lse = attend(q[span], k[span], v[span], lambda s: s + bias0[b])
            o0[h, span] = o
            keep(lse0, (), span, h, lse)

    def level_head(t, _):
        for copy in exchange(t):
            copy.wait_recv()
        pick = pbuf[t]
        dq = nt(pick, ot_q[...]).astype(BF16)
        dk = [nt(pick, ot_k[d]).astype(BF16) for d in range(2)]

        def rows_of(piece, level):
            first, count, _ = REGIONS[level]
            return jnp.concatenate([piece(d, b, first, count) for d in range(2) for b in range(2)], axis=0)

        def q_docs(g, level):
            def piece(d, b, first, count):
                mark = jnp.where((lane >> 3) == 2 * g + d, 1.0, 0.0).astype(BF16)
                return dq[first : first + count, b * DIM : (b + 1) * DIM] * mark

            return rows_of(piece, level)

        def keys(level):
            k = rows_of(lambda d, b, first, count: ck[t, 2 * d + b, first : first + count], level)
            kd = rows_of(lambda d, b, first, count: dk[d][first : first + count, b * DIM : (b + 1) * DIM], level)
            v = rows_of(lambda d, b, first, count: cv[t, 2 * d + b, first : first + count], level)
            return jnp.concatenate([k, kd], axis=1), v

        held = [keys(level) for level in range(4)]

        def put(o, lse, level, out, stats, shift, stats_shift):
            first, count, _ = REGIONS[level]
            for d in range(2):
                for b in range(2):
                    rows = slice((2 * d + b) * count, (2 * d + b + 1) * count)
                    spot = slice(first - shift, first - shift + count)
                    out[d, t, b, spot] = o[rows].astype(BF16)
                    place = slice(first - stats_shift, first - stats_shift + count)
                    keep(stats, (d, b), place, t, lse[rows])

        for level in range(4):
            q = rows_of(lambda d, b, first, count: cq[t, 2 * d + b, first : first + count], level)
            q = jnp.concatenate([q, q_docs(0, level)], axis=1)
            k, v = held[level]
            n = q.shape[0]
            if level == 0:
                early = attend(q[:CHUNK], k[:CHUNK], v[:CHUNK], lambda s: s + causal[...])
                late = attend(
                    q[CHUNK:], k, v,
                    lambda s: jnp.concatenate([s[:, :CHUNK], s[:, CHUNK:] + causal[...]], axis=1),
                )
                o, lse = [jnp.concatenate(pair, axis=0) for pair in zip(early, late)]
            else:
                o, lse = attend(q, k, v, lambda s: s + causal[:n, :n])
            put(o, lse, level, ob, st_own, 0, 0)
        partner_out(t).start()

        local_head(2 * t)
        local_head(2 * t + 1)

        def visit(g, level):
            def piece(d, b, first, count):
                if g == 1:
                    return q1in[t, 2 * d + b, first - 128 : first - 128 + count]
                return q2in[t, 2 * d + b, first - 192 : first - 192 + count]

            q = jnp.concatenate([rows_of(piece, level), q_docs(g, level)], axis=1)
            o, lse = attend(q, *held[level], None)
            if g == 1:
                put(o, lse, level, os1, st1, 128, 128)
            else:
                put(o, lse, level, os2, st2, 192, 128)

        for present, low in q2_cases(c + 2):

            @pl.when(present & (c <= 5))
            def _():
                for d in range(2):
                    q2_copy(sq.at[t], t, d, low, 0, 0).wait_recv()
                for level in (2, 3) if low == 0 else (3,):
                    visit(2, level)
                for d in range(2):
                    ret_copies(t, 2, low, d).start()

        for present, low in q1_cases(c + 1):

            @pl.when(present & (c <= 6))
            def _():
                for d in range(2):
                    q1_copy(sq.at[t], t, d, low, 0, 0).wait_recv()
                for level in (1, 2, 3) if low == 0 else (2, 3):
                    visit(1, level)
                for d in range(2):
                    ret_copies(t, 1, low, d).start()

        return 0

    lax.fori_loop(0, HALF, level_head, 0)

    for d in range(2):
        for b in range(2):
            ls_own[d, b] = st_own[d, b].T[:HALF]
            ls1[d, b] = st1[d, b].T[:HALF]
            ls2[d, b] = st2[d, b].T[:HALF]
    l_own = remote(ls_own.at[1 - j], lo_in, l_send.at[0], l_recv.at[0], device(0, 1 - j))
    l_own.start()

    def far_stats(g, d):
        if g == 1:
            return remote(ls1.at[d], lr1.at[j], l_send.at[1 + d], l_recv.at[1 + j], device(1, d))
        return remote(ls2.at[d], lr2.at[j], l_send.at[3 + d], l_recv.at[3 + j], device(2, d))

    for g in (1, 2):

        @pl.when(c <= 7 - g)
        def _():
            for d in range(2):
                far_stats(g, d).start()

    l_own.wait_recv()
    for g in (1, 2):

        @pl.when(c >= g)
        def _():
            for i in range(2):
                copy = (
                    remote(ls1.at[0], lr1.at[i], l_send.at[1], l_recv.at[1 + i], device(1, 0))
                    if g == 1
                    else remote(ls2.at[0], lr2.at[i], l_send.at[3], l_recv.at[3 + i], device(2, 0))
                )
                copy.wait_recv()

    mine = ls_own[j]
    theirs = lo_in[...]
    lower = jnp.where(j == 0, mine, theirs)
    upper = jnp.where(j == 0, theirs, mine)
    wide = iota((1, CHUNK), 1)
    own = jnp.concatenate([lower[0], upper[0], lower[1], upper[1]], axis=0)
    own = jnp.where(wide < SEL, own, NEG)
    yes2, yes3, yes4 = (c % 2 == 1, c % 4 >= 1, c >= 1)
    two3, two4 = (c % 4 >= 2, c >= 2)

    def limits(l2, l3, l4):
        return (
            ((lane < 64) & l2)
            | ((lane >= 64) & (lane < 96) & l3)
            | ((lane >= 96) & (lane < FAR) & l4)
        )

    def far(ref, valid):
        x = jnp.concatenate([ref[0, 0], ref[1, 0], ref[0, 1], ref[1, 1]], axis=0)
        return jnp.where(valid, x, NEG)

    far1 = far(lr1, limits(yes2, yes3, yes4))
    far2 = far(lr2, limits(False, two3, two4))
    none = jnp.full((2 * HEADS, DIM), NEG, F32)
    far1w = jnp.concatenate([none, far1], axis=1)
    far2w = jnp.concatenate([none, far2], axis=1)
    top = jnp.maximum(own, jnp.maximum(far1w, far2w))
    lse_sel = top + jnp.log2(jnp.exp2(own - top) + jnp.exp2(far1w - top) + jnp.exp2(far2w - top))

    head = iota((HEADS, CHUNK), 0)
    spot = iota((HEADS, CHUNK), 1)
    tall = iota((CHUNK, CHUNK), 0)
    spread, chosen = [], []
    for level, (first, count, bits) in enumerate(REGIONS):
        hit = ((iota((CHUNK, CHUNK), 1) >> bits) == tall - first) & (tall >= first) & (tall < first + count)
        spread.append(jnp.where(hit, 1.0, 0.0).astype(BF16))
        shifts = jnp.zeros((HEADS, CHUNK), I32)
        for h in range(HEADS):
            shifts = jnp.where(head == h, off_ref[level, h] & ((1 << bits) - 1), shifts)
        pick = (spot & ((1 << bits) - 1)) == shifts
        chosen.append(jnp.concatenate([pick, pick], axis=0))
    zeroth = lse0[...].T
    parts = [jnp.concatenate([zeroth[:HEADS, :CHUNK], zeroth[:HEADS, CHUNK:]], axis=0)]
    sel3 = split3(lse_sel)
    for level in range(4):
        parts.append(jnp.where(chosen[level], fold3(nn(sel3, spread[level])), NEG))
    top = parts[0]
    for part in parts[1:]:
        top = jnp.maximum(top, part)
    total = jnp.exp2(parts[0] - top)
    for part in parts[1:]:
        total = total + jnp.exp2(part - top)
    lse = top + jnp.log2(total)
    back = jnp.zeros((2 * HEADS, CHUNK), F32)
    for level in range(4):
        back = back + fold3(nt(split3(jnp.where(chosen[level], lse, 0.0)), spread[level]))
    al_own[...] = jnp.exp2(own - back)
    al_far[:, :DIM] = jnp.exp2(far1 - back[:, DIM:])
    al_far[:, DIM:] = jnp.exp2(far2 - back[:, DIM:])
    pad = jnp.zeros((DIM - HEADS, CHUNK), F32)
    for b in range(2):
        across = jnp.concatenate([lse[b * HEADS : (b + 1) * HEADS], pad], axis=0).T
        span = slice(b * CHUNK, (b + 1) * CHUNK)
        a0[span] = jnp.exp2(lse0[span] - across)

    def out_copy(h):
        span = pl.ds(pl.multiple_of(h * DIM, DIM), DIM)
        return pltpu.make_async_copy(ov.at[:, span], out_hbm.at[0, :, span], store_sem.at[h])

    column = iota((CHUNK, CHUNK), 0)
    own_first = jnp.where(wide < 128, 0, jnp.where(wide < 192, 128, jnp.where(wide < 224, 192, 224)))
    own_bits = jnp.where(wide < 128, 1, jnp.where(wide < 192, 2, jnp.where(wide < 224, 3, 4)))
    own_base = column - ((wide - own_first) << own_bits)
    wrapped = (wide & (DIM - 1)) + DIM
    far_first = jnp.where(wrapped < 192, 128, jnp.where(wrapped < 224, 192, 224))
    far_bits = jnp.where(wrapped < 192, 2, jnp.where(wrapped < 224, 3, 4))
    far_base = column - ((wrapped - far_first) << far_bits)

    def finish_head(t, _):
        partner_out(t).wait_recv()
        for present, low in q1_cases(c):

            @pl.when(present)
            def _():
                rows = pl.ds(low, FAR - low)
                for i in range(2):
                    remote(
                        os1.at[0, t, :, rows], or1.at[HALF * i + t, :, rows],
                        o1_send.at[0, t], o1_recv.at[i, t], device(1, 0),
                    ).wait_recv()

        for present, low in q2_cases(c):

            @pl.when(present)
            def _():
                for i in range(2):
                    remote(
                        os2.at[0, t, :, pl.ds(low, FAR3 - low)],
                        or2.at[HALF * i + t, :, pl.ds(64 + low, FAR3 - low)],
                        o2_send.at[0, t], o2_recv.at[i, t], device(2, 0),
                    ).wait_recv()

        for which in range(2):
            h = HALF * j + t if which == 0 else HALF * (1 - j) + t
            o1, o2, o3, o4 = [off_ref[i, h] & (2 << i) - 1 for i in range(4)]
            own_shift = jnp.where(wide < 128, o1, jnp.where(wide < 192, o2, jnp.where(wide < 224, o3, o4)))
            far_shift = jnp.where(wrapped < 192, o2, jnp.where(wrapped < 224, o3, o4))
            own_hit = own_base == own_shift
            far_hit = far_base == far_shift
            for b in range(2):
                span = slice(b * CHUNK, (b + 1) * CHUNK)
                own_w = jnp.where(own_hit, al_own[pl.ds(b * HEADS + h, 1), :], 0.0).astype(BF16)
                far_w = jnp.where(far_hit, al_far[pl.ds(b * HEADS + h, 1), :], 0.0).astype(BF16)
                o_own = ob[j, t, b] if which == 0 else oo_in[t, b]
                o_far = jnp.concatenate([or1[h, b], or2[h, b]], axis=0)
                mixed = nn(own_w, o_own) + nn(far_w, o_far)
                scale = jnp.sum(jnp.where(lane == h, a0[span], 0.0), axis=1, keepdims=True)
                ov[span, pl.ds(pl.multiple_of(h * DIM, DIM), DIM)] = (mixed + scale * o0[h, span]).astype(BF16)
            out_copy(h).start()
        return 0

    lax.fori_loop(0, HALF, finish_head, 0)

    for copy in docs_copies:
        copy.wait_send()
    l_own.wait_send()
    for g in (1, 2):

        @pl.when(c <= 7 - g)
        def _():
            for d in range(2):
                far_stats(g, d).wait_send()

    def drain(t, _):
        for which in range(2):
            each_q_send(t, which, lambda copy: copy.wait_send())
        for copy in exchange(t):
            copy.wait_send()
        partner_out(t).wait_send()
        for present, low in q2_cases(c + 2):

            @pl.when(present & (c <= 5))
            def _():
                for d in range(2):
                    ret_copies(t, 2, low, d).wait_send()

        for present, low in q1_cases(c + 1):

            @pl.when(present & (c <= 6))
            def _():
                for d in range(2):
                    ret_copies(t, 1, low, d).wait_send()

        out_copy(2 * t).wait()
        out_copy(2 * t + 1).wait()
        return 0

    lax.fori_loop(0, HALF, drain, 0)


def on_device(queries, key_rows, value_rows, document_ids, dilation_offsets):
    any_space = pl.BlockSpec(memory_space=pl.ANY)
    dma = pltpu.SemaphoreType.DMA

    def vmem(*shape, kind=BF16):
        return pltpu.VMEM(shape, kind)

    return pl.pallas_call(
        kernel,
        out_shape=jax.ShapeDtypeStruct((1, ROWS, HEADS * DIM), BF16),
        in_specs=[
            any_space, any_space, any_space,
            pl.BlockSpec(memory_space=pltpu.VMEM),
            pl.BlockSpec(memory_space=pltpu.SMEM),
        ],
        out_specs=any_space,
        scratch_shapes=[
            vmem(ROWS, HEADS * DIM), vmem(ROWS, HEADS * DIM), vmem(ROWS, HEADS * DIM), vmem(ROWS, HEADS * DIM),
            vmem(HALF, 4, SEL, DIM), vmem(HALF, 4, SEL, DIM), vmem(HALF, 4, SEL, DIM),
            vmem(HALF, 2, SEL, DIM), vmem(HALF, 2, SEL, DIM), vmem(HALF, 2, SEL, DIM),
            vmem(HALF, 4, FAR, DIM), vmem(HALF, 4, FAR3, DIM), vmem(HALF, SEL, CHUNK),
            vmem(2, HALF, 2, CHUNK, DIM), vmem(HALF, 2, CHUNK, DIM),
            vmem(2, HALF, 2, FAR, DIM), vmem(2, HALF, 2, FAR3, DIM),
            vmem(HEADS, 2, DIM, DIM), vmem(HEADS, 2, DIM, DIM), vmem(HEADS, ROWS, DIM, kind=F32),
            vmem(2, 2, CHUNK, DIM, kind=F32), vmem(2, 2, DIM, DIM, kind=F32), vmem(2, 2, DIM, DIM, kind=F32),
            vmem(ROWS, DIM, kind=F32),
            vmem(2, 2, HALF, CHUNK, kind=F32), vmem(2, 2, HALF, DIM, kind=F32), vmem(2, 2, HALF, DIM, kind=F32),
            vmem(2, HALF, CHUNK, kind=F32), vmem(2, 2, HALF, DIM, kind=F32), vmem(2, 2, HALF, DIM, kind=F32),
            vmem(6, 1, ROWS, kind=I32), vmem(2 * DIM, CHUNK), vmem(2, 2 * DIM, CHUNK),
            vmem(SEL, CHUNK, kind=I32), vmem(CHUNK, CHUNK, kind=F32), vmem(2, CHUNK, CHUNK, kind=F32),
            vmem(2 * HEADS, CHUNK, kind=F32), vmem(2 * HEADS, CHUNK, kind=F32), vmem(ROWS, DIM, kind=F32),
            dma((3,)), dma((HEADS,)), dma((5,)), dma((6,)), dma((3, HALF)), dma((3, HALF)),
            dma((2, HALF)), dma((2, HALF)), dma((2, HALF)), dma((2, HALF)),
            dma((2, HALF)), dma((2, HALF)), dma((2, HALF)), dma((2, HALF)),
            dma((HALF,)), dma((HALF,)), dma((5,)), dma((5,)),
        ],
        compiler_params=pltpu.CompilerParams(
            collective_id=0, has_side_effects=True, vmem_limit_bytes=56 << 20
        ),
        name="dilated_attention",
    )(queries, key_rows, value_rows, document_ids, dilation_offsets)


def solution(mesh):
    placed = (P("dp", "ctx", None), P("dp", "ctx", None), P("dp", "ctx", None), P("dp", "ctx"), P())
    return jax.shard_map(
        on_device, mesh=mesh, in_specs=placed, out_specs=P("dp", "ctx", None), check_vma=False
    )
```

```python
import math

import jax
import jax.numpy as jnp
from jax import lax
from jax.experimental import pallas as pl
from jax.experimental.pallas import tpu as pltpu
from jax.sharding import PartitionSpec as P

MESH = pl.DeviceIdType.MESH
F32, BF16, I32 = jnp.float32, jnp.bfloat16, jnp.int32
HEADS, HALF, ROWS, DIM, CHUNK = 16, 8, 512, 128, 256
SEL, FAR, FAR3 = 240, 112, 48
REGIONS = ((0, 128, 1), (128, 64, 2), (192, 32, 3), (224, 16, 4))
NEG = -1e30
SCALE2 = math.log2(math.e) / math.sqrt(DIM)


def nt(a, b):
    return lax.dot_general(a, b, (((1,), (1,)), ((), ())), preferred_element_type=F32)


def nn(a, b):
    return jnp.dot(a, b, preferred_element_type=F32)


def split3(x):
    first = x.astype(BF16)
    rest = x - first.astype(F32)
    second = rest.astype(BF16)
    third = (rest - second.astype(F32)).astype(BF16)
    return jnp.concatenate([first, second, third], axis=0)


def fold3(x):
    n = x.shape[0] // 3
    return (x[2 * n :] + x[n : 2 * n]) + x[:n]


def iota(shape, dim):
    return lax.broadcasted_iota(I32, shape, dim)


def attend(problems):
    scores = [nt(q, k) if bias is None else bias(nt(q, k)) for q, k, _, bias in problems]
    tops = [jnp.max(s, axis=1, keepdims=True) for s in scores]
    weights = [jnp.exp2((s - top) * SCALE2).astype(BF16) for s, top in zip(scores, tops)]
    sums = [nn(w, jnp.concatenate([v, jnp.ones_like(v)], axis=1)) for w, (_, _, v, _) in zip(weights, problems)]
    return [(x[:, :DIM] / x[:, DIM:], top * SCALE2 + jnp.log2(x[:, DIM:])) for x, top in zip(sums, tops)]


def far_pieces(chip):
    return (
        (chip % 4 == 3, ((0, FAR),)),
        (chip % 4 == 2, ((64, FAR),)),
        (chip == 1, ((0, 64),)),
        (chip == 5, ((0, 64), (96, FAR))),
        (chip == 4, ((96, FAR),)),
    )


def next_pieces(chip):
    return ((chip % 4 < 2, ((0, FAR3),)), ((chip == 2) | (chip == 3), ((32, FAR3),)))


def kernel(
    q_hbm, k_hbm, v_hbm, docs_ref, off_ref,
    loc_out, far_out, lse_out, lsef_out,
    qv, kv, vv,
    cq, ck, cv, sq, sk, sv, q1in, kp, vp, dqs, dks, dps, pbuf,
    ob, oo_in, os1, o0, loc,
    st_own, st1, lse0, ls_own, ls1, lo_in, lse_loc,
    docs_all, ot_q, ot_k, base_m, causal, bias0, al_own, a0,
    load_sem, store_sem, lse_sem, d_send, d_recv, x_send, x_recv,
    q_send, q_recv, k_send, k_recv, v_send, v_recv, o_send, o_recv,
    oo_send, oo_recv, l_send, l_recv,
):
    me = lax.axis_index("ctx")
    dp = lax.axis_index("dp")
    c = me // 2
    j = me % 2

    def device(steps, core):
        return (dp, ((c + steps + 8) % 8) * 2 + core)

    def remote(src, dst, send, recv, to):
        return pltpu.make_async_remote_copy(
            src_ref=src, dst_ref=dst, send_sem=send, recv_sem=recv, device_id=to, device_id_type=MESH
        )

    def loads(u):
        copies = []
        for half in range(2):
            first = HALF * (1 - j) if half == 0 else HALF * j
            span = pl.ds(pl.multiple_of((first + 2 * u) * DIM, DIM), 2 * DIM)
            for i, (src, dst) in enumerate(((q_hbm, qv), (k_hbm, kv), (v_hbm, vv))):
                copies.append(pltpu.make_async_copy(src.at[0, :, span], dst.at[:, span], load_sem.at[u, half, i]))
        return copies

    for u in range(4):
        for copy in loads(u):
            copy.start()

    for first, count, bits in REGIONS:
        base_m[first : first + count] = iota((count, CHUNK), 1) - (iota((count, CHUNK), 0) << bits)

    barrier = pltpu.get_barrier_semaphore()
    greeted = [(0, 1 - j)] + [(g, core) for g in (-1, 1) for core in (0, 1)]
    for g, core in greeted:
        pl.semaphore_signal(barrier, inc=1, device_id=device(g, core), device_id_type=MESH)
    pl.semaphore_wait(barrier, len(greeted))

    docs_sent = [(0, 1 - j, 0)] + [(g, core, slot) for g, slot in ((-1, 2), (1, 4)) for core in (0, 1)]
    docs_copies = [
        remote(docs_ref, docs_all.at[slot + j], d_send.at[i], d_recv.at[slot + j], device(g, core))
        for i, (g, core, slot) in enumerate(docs_sent)
    ]
    for copy in docs_copies:
        copy.start()
    docs_all[j] = docs_ref[...]

    def source(staged, held, t, which):
        return staged.at[t] if which == 0 else held.at[t, pl.ds(2 * j, 2)]

    def core_of(which):
        return 1 - j if which == 0 else j

    def q_copy(t, which, piece, low, high, d):
        return remote(
            source(sq, cq, t, which).at[:, pl.ds(128 + low, high - low)],
            q1in.at[t, pl.ds(2 * d, 2), pl.ds(low, high - low)],
            q_send.at[which, piece, t], q_recv.at[d, piece, t], device(-1, core_of(which)),
        )

    def kv_copies(t, which, low, high, d):
        return [
            remote(
                source(staged, held, t, which).at[:, pl.ds(192 + low, high - low)],
                dst.at[t, pl.ds(2 * d, 2), pl.ds(low, high - low)],
                send.at[which, t], recv.at[d, t], device(1, core_of(which)),
            )
            for staged, held, dst, send, recv in ((sk, ck, kp, k_send, k_recv), (sv, cv, vp, v_send, v_recv))
        ]

    def each_q(t, which, do):
        for present, pieces in far_pieces(c):

            @pl.when(present)
            def _():
                for piece, (low, high) in enumerate(pieces):
                    do(q_copy(t, which, piece, low, high, j))

    def each_kv(t, which, do):
        for present, pieces in next_pieces(c):

            @pl.when(present)
            def _():
                for low, high in pieces:
                    for copy in kv_copies(t, which, low, high, j):
                        do(copy)

    def exchange(t):
        return [
            remote(src.at[t], dst.at[t, pl.ds(2 * j, 2)], x_send.at[i, t], x_recv.at[i, t], device(0, 1 - j))
            for i, (src, dst) in enumerate(((sq, cq), (sk, ck), (sv, cv)))
        ]

    def picker(h):
        parts = []
        for level, (first, count, bits) in enumerate(REGIONS):
            shift = off_ref[level, h] & ((1 << bits) - 1)
            parts.append(jnp.where(base_m[first : first + count] == shift, 1.0, 0.0))
        return jnp.concatenate(parts, axis=0).astype(BF16)

    def columns(ref, h):
        return ref[:, pl.ds(pl.multiple_of(h * DIM, DIM), DIM)]

    def select(pick, ref, h):
        x = columns(ref, h)
        both = nn(pick, jnp.concatenate([x[:CHUNK], x[CHUNK:]], axis=1)).astype(BF16)
        return both[:, :DIM], both[:, DIM:]

    def start(copy):
        copy.start()

    def select_head(t, _):
        @pl.when(t % 2 == 0)
        def _():
            for copy in loads(t // 2):
                copy.wait()

        for which in range(2):
            h = HALF * (1 - j) + t if which == 0 else HALF * j + t
            pick = picker(h)
            if which == 1:
                pbuf[t] = pick
            for ref, mine, theirs in ((qv, cq, sq), (kv, ck, sk), (vv, cv, sv)):
                for b, part in enumerate(select(pick, ref, h)):
                    if which == 0:
                        theirs[t, b] = part
                    else:
                        mine[t, 2 * j + b] = part
            each_q(t, which, start)
            each_kv(t, which, start)
            if which == 0:
                for copy in exchange(t):
                    copy.start()
        return 0

    lax.fori_loop(0, HALF, select_head, 0)

    def clear_pads(t, _):
        for b in range(2):
            oo_in[t, b, SEL:] = jnp.zeros((CHUNK - SEL, DIM), BF16)
            for d in range(2):
                ob[d, t, b, SEL:] = jnp.zeros((CHUNK - SEL, DIM), BF16)
        return 0

    lax.fori_loop(0, HALF, clear_pads, 0)

    causal[...] = jnp.where(iota((CHUNK, CHUNK), 1) <= iota((CHUNK, CHUNK), 0), 0.0, NEG)
    eye = jnp.where(iota((CHUNK, CHUNK), 1) == iota((CHUNK, CHUNK), 0), 1.0, 0.0).astype(BF16)
    for b in range(2):
        same = docs_ref[:, b * CHUNK : (b + 1) * CHUNK] == iota((DIM, CHUNK), 0)
        q_one = nt(eye, jnp.where(same, 1.0, 0.0).astype(BF16)).astype(BF16)
        k_one = nt(eye, jnp.where(same, 0.0, NEG).astype(BF16)).astype(BF16)
        bias0[b] = nt(q_one, k_one) + causal[...]

    for i, slot in enumerate((1 - j, 2, 3, 4, 5)):
        remote(docs_ref, docs_all.at[slot], d_send.at[i], d_recv.at[slot], device(0, 1 - j)).wait_recv()
    for b in range(2):
        span = slice(b * CHUNK, (b + 1) * CHUNK)
        ones = [jnp.where(docs_all[g, :, span] == iota((8, CHUNK), 0), 1.0, 0.0) for g in range(4)]
        ones.append(jnp.zeros((DIM - 32, CHUNK), F32))
        ot_q[b * DIM : (b + 1) * DIM] = jnp.concatenate(ones, axis=0).astype(BF16)
        for i, slot in enumerate((0, 1, 4, 5)):
            same = docs_all[slot, :, span] == (iota((DIM, CHUNK), 0) & 7)
            ot_k[i, b * DIM : (b + 1) * DIM] = jnp.where(same, 0.0, NEG).astype(BF16)

    lane = iota((1, DIM), 1)

    def keep(ref, index, rows, t, value):
        old = ref[index + (rows,)]
        ref[index + (rows,)] = jnp.where(lane == t, value, old)

    def join(piece):
        return jnp.concatenate([piece(d, b) for d in range(2) for b in range(2)], axis=0)

    def with_docs(q, g, level, t):
        first, count, _ = REGIONS[level]

        def piece(d, b):
            mark = jnp.where((lane >> 3) == 2 * g + d, 1.0, 0.0).astype(BF16)
            return dqs[t, first : first + count, b * DIM : (b + 1) * DIM] * mark

        return jnp.concatenate([q, join(piece)], axis=1)

    def own_q(t, level):
        first, count, _ = REGIONS[level]
        return with_docs(join(lambda d, b: cq[t, 2 * d + b, first : first + count]), 0, level, t)

    def guest_q(t, level):
        first, count, _ = REGIONS[level]
        return with_docs(join(lambda d, b: q1in[t, 2 * d + b, first - 128 : first - 128 + count]), 1, level, t)

    def own_kv(t, level):
        first, count, _ = REGIONS[level]
        span = slice(first, first + count)
        k = join(lambda d, b: ck[t, 2 * d + b, span])
        kd = join(lambda d, b: dks[d, t, span, b * DIM : (b + 1) * DIM])
        return jnp.concatenate([k, kd], axis=1), join(lambda d, b: cv[t, 2 * d + b, span])

    def both_kv(t, level):
        first, count, _ = REGIONS[level]
        span = slice(first - 192, first - 192 + count)
        k = join(lambda d, b: kp[t, 2 * d + b, span])
        kd = join(lambda d, b: dps[d, t, span, b * DIM : (b + 1) * DIM])
        v = join(lambda d, b: vp[t, 2 * d + b, span])
        own_k, own_v = own_kv(t, level)
        return (
            jnp.concatenate([own_k, jnp.concatenate([k, kd], axis=1)], axis=0),
            jnp.concatenate([own_v, v], axis=0),
        )

    def put(t, level, result, out, stats, shift):
        o, lse = result
        first, count, _ = REGIONS[level]
        spot = slice(first - shift, first - shift + count)
        for d in range(2):
            for b in range(2):
                rows = slice((2 * d + b) * count, (2 * d + b + 1) * count)
                out[d, t, b, spot] = o[rows].astype(BF16)
                keep(stats, (d, b), spot, t, lse[rows])

    def near(n):
        return lambda s: s + causal[:n, :n]

    def near_half(n):
        def bias(s):
            return jnp.concatenate([s[:, :n] + causal[:n, :n], s[:, n:]], axis=1)

        return bias

    def partner_out(t):
        return remote(
            ob.at[1 - j, t, :, pl.ds(0, SEL)], oo_in.at[t, :, pl.ds(0, SEL)],
            oo_send.at[t], oo_recv.at[t], device(0, 1 - j),
        )

    def ret_copy(t, piece, low, high, d):
        return remote(
            os1.at[d, t, :, pl.ds(low, high - low)], far_out.at[HALF * j + t, :, pl.ds(low, high - low)],
            o_send.at[d, piece, t], o_recv.at[j, piece, t], device(1, d),
        )

    def own_head(t, _):
        for copy in exchange(t):
            copy.wait_recv()
        pick = pbuf[t]
        dqs[t] = nt(pick, ot_q[...]).astype(BF16)
        for d in range(2):
            dks[d, t] = nt(pick, ot_k[d]).astype(BF16)
            dps[d, t] = nt(pick[192:], ot_k[2 + d]).astype(BF16)

        problems = []
        q = own_q(t, 0)
        k, v = own_kv(t, 0)
        problems.append((q[:CHUNK], k[:CHUNK], v[:CHUNK], near(CHUNK)))
        late = lambda s: jnp.concatenate([s[:, :CHUNK], s[:, CHUNK:] + causal[...]], axis=1)
        problems.append((q[CHUNK:], k, v, late))
        for level in (1, 2, 3):
            problems.append((own_q(t, level),) + own_kv(t, level) + (near(4 * REGIONS[level][1]),))
        for h in (2 * t, 2 * t + 1):
            q, k, v = columns(qv, h), columns(kv, h), columns(vv, h)
            for b in range(2):
                span = slice(b * CHUNK, (b + 1) * CHUNK)
                problems.append((q[span], k[span], v[span], lambda s, b=b: s + bias0[b]))
        results = attend(problems)
        first = tuple(jnp.concatenate(pair, axis=0) for pair in zip(results[0], results[1]))
        for level, result in enumerate([first] + results[2:5]):
            put(t, level, result, ob, st_own, 0)
        for i in range(2):
            for b in range(2):
                span = slice(b * CHUNK, (b + 1) * CHUNK)
                o, lse = results[5 + 2 * i + b]
                o0[2 * t + i, span] = o
                keep(lse0, (), span, 2 * t + i, lse)
        return 0

    lax.fori_loop(0, HALF, own_head, 0)

    plans = (
        (c == 0, "2", ""),
        (c == 1, "34", "34"),
        (c == 5, "34", "3"),
        (c % 4 == 2, "234", ""),
        (c == 3, "4", ""),
        (c == 4, "24", ""),
    )

    def guest_head(t, _):
        for present, pieces in next_pieces(c - 1):

            @pl.when(present & (c >= 1))
            def _():
                for low, high in pieces:
                    for d in range(2):
                        for copy in kv_copies(t, 0, low, high, d):
                            copy.wait_recv()

        for present, pieces in far_pieces(c + 1):

            @pl.when(present & (c <= 6))
            def _():
                for piece, (low, high) in enumerate(pieces):
                    for d in range(2):
                        q_copy(t, 0, piece, low, high, d).wait_recv()

        for present, guests, owns in plans:

            @pl.when(present)
            def _():
                problems = []
                for name in guests:
                    level = int(name) - 1
                    kv_pair = own_kv(t, level) if level == 1 else both_kv(t, level)
                    problems.append((guest_q(t, level),) + kv_pair + (None,))
                for name in owns:
                    level = int(name) - 1
                    n = 4 * REGIONS[level][1]
                    problems.append((own_q(t, level),) + both_kv(t, level) + (near_half(n),))
                results = attend(problems)
                for name, result in zip(guests, results):
                    put(t, int(name) - 1, result, os1, st1, 128)
                for name, result in zip(owns, results[len(guests) :]):
                    put(t, int(name) - 1, result, ob, st_own, 0)

        for present, pieces in far_pieces(c + 1):

            @pl.when(present & (c <= 6))
            def _():
                for piece, (low, high) in enumerate(pieces):
                    for d in range(2):
                        ret_copy(t, piece, low, high, d).start()

        partner_out(t).start()
        return 0

    lax.fori_loop(0, HALF, guest_head, 0)

    for d in range(2):
        for b in range(2):
            ls1[d, b] = st1[d, b].T[:HALF]
            ls_own[d, b] = st_own[d, b].T[:HALF]

    def far_stats(d):
        return remote(ls1.at[d], lsef_out.at[j], l_send.at[1 + d], l_recv.at[1 + j], device(1, d))

    @pl.when(c <= 6)
    def _():
        for d in range(2):
            far_stats(d).start()

    l_own = remote(ls_own.at[1 - j], lo_in, l_send.at[0], l_recv.at[0], device(0, 1 - j))
    l_own.start()
    l_own.wait_recv()

    mine = ls_own[j]
    theirs = lo_in[...]
    lower = jnp.where(j == 0, mine, theirs)
    upper = jnp.where(j == 0, theirs, mine)
    wide = iota((1, CHUNK), 1)
    own = jnp.concatenate([lower[0], upper[0], lower[1], upper[1]], axis=0)
    own = jnp.where(wide < SEL, own, NEG)
    tall = iota((CHUNK, CHUNK), 0)
    own3 = split3(own)
    zeroth = lse0[...].T
    parts = [jnp.concatenate([zeroth[:HEADS, :CHUNK], zeroth[:HEADS, CHUNK:]], axis=0)]
    spread, chosen = [], []
    for level, (first, count, bits) in enumerate(REGIONS):
        hit = ((iota((CHUNK, CHUNK), 1) >> bits) == tall - first) & (tall >= first) & (tall < first + count)
        spread.append(jnp.where(hit, 1.0, 0.0).astype(BF16))
        chosen.append(picked(off_ref, level, bits))
        parts.append(jnp.where(chosen[level], fold3(nn(own3, spread[level])), NEG))
    lse = log_sum(parts)
    back = jnp.zeros((2 * HEADS, CHUNK), F32)
    for level in range(4):
        back = back + fold3(nt(split3(jnp.where(chosen[level], lse, 0.0)), spread[level]))
    al_own[...] = jnp.exp2(own - back)
    lse_loc[...] = lse
    lse_copy = pltpu.make_async_copy(lse_loc, lse_out, lse_sem.at[0])
    lse_copy.start()
    for b in range(2):
        span = slice(b * CHUNK, (b + 1) * CHUNK)
        a0[span] = jnp.exp2(lse0[span] - upright(lse, b))

    def loc_copy(h):
        return pltpu.make_async_copy(loc.at[h], loc_out.at[h], store_sem.at[h])

    own_first = jnp.where(wide < 128, 0, jnp.where(wide < 192, 128, jnp.where(wide < 224, 192, 224)))
    own_bits = jnp.where(wide < 128, 1, jnp.where(wide < 192, 2, jnp.where(wide < 224, 3, 4)))
    own_base = tall - ((wide - own_first) << own_bits)

    def local_head(t, _):
        partner_out(t).wait_recv()
        for which in range(2):
            h = HALF * j + t if which == 0 else HALF * (1 - j) + t
            o1, o2, o3, o4 = [off_ref[i, h] & (2 << i) - 1 for i in range(4)]
            shift = jnp.where(wide < 128, o1, jnp.where(wide < 192, o2, jnp.where(wide < 224, o3, o4)))
            hit = own_base == shift
            for b in range(2):
                span = slice(b * CHUNK, (b + 1) * CHUNK)
                weight = jnp.where(hit, al_own[pl.ds(b * HEADS + h, 1), :], 0.0).astype(BF16)
                mixed = nn(weight, ob[j, t, b] if which == 0 else oo_in[t, b])
                scale = jnp.sum(jnp.where(lane == h, a0[span], 0.0), axis=1, keepdims=True)
                loc[h, span] = (mixed + scale * o0[h, span]).astype(BF16)
            loc_copy(h).start()
        return 0

    lax.fori_loop(0, HALF, local_head, 0)

    for copy in docs_copies:
        copy.wait_send()
    l_own.wait_send()
    lse_copy.wait()

    def drain(t, _):
        for which in range(2):
            each_q(t, which, lambda copy: copy.wait_send())
            each_kv(t, which, lambda copy: copy.wait_send())
        for copy in exchange(t):
            copy.wait_send()
        partner_out(t).wait_send()
        loc_copy(2 * t).wait()
        loc_copy(2 * t + 1).wait()
        return 0

    lax.fori_loop(0, HALF, drain, 0)

    def drain_far(t, _):
        for present, pieces in far_pieces(c + 1):

            @pl.when(present & (c <= 6))
            def _():
                for piece, (low, high) in enumerate(pieces):
                    for d in range(2):
                        ret_copy(t, piece, low, high, d).wait_send()

        for present, pieces in far_pieces(c):

            @pl.when(present)
            def _():
                for piece, (low, high) in enumerate(pieces):
                    for i in range(2):
                        remote(
                            os1.at[0, t, :, pl.ds(low, high - low)],
                            far_out.at[HALF * i + t, :, pl.ds(low, high - low)],
                            o_send.at[0, piece, t], o_recv.at[i, piece, t], device(1, 0),
                        ).wait_recv()

        return 0

    lax.fori_loop(0, HALF, drain_far, 0)

    @pl.when(c <= 6)
    def _():
        for d in range(2):
            far_stats(d).wait_send()

    @pl.when(c >= 1)
    def _():
        for i in range(2):
            remote(ls1.at[0], lsef_out.at[i], l_send.at[1], l_recv.at[1 + i], device(1, 0)).wait_recv()


def picked(off_ref, level, bits):
    head = iota((HEADS, CHUNK), 0)
    shifts = jnp.zeros((HEADS, CHUNK), I32)
    for h in range(HEADS):
        shifts = jnp.where(head == h, off_ref[level, h] & ((1 << bits) - 1), shifts)
    pick = (iota((HEADS, CHUNK), 1) & ((1 << bits) - 1)) == shifts
    return jnp.concatenate([pick, pick], axis=0)


def log_sum(parts):
    top = parts[0]
    for part in parts[1:]:
        top = jnp.maximum(top, part)
    total = jnp.exp2(parts[0] - top)
    for part in parts[1:]:
        total = total + jnp.exp2(part - top)
    return top + jnp.log2(total)


def upright(dense, b):
    pad = jnp.zeros((DIM - HEADS, CHUNK), F32)
    return jnp.concatenate([dense[b * HEADS : (b + 1) * HEADS], pad], axis=0).T


GROUP = 4


def join_kernel(loc_ref, far_ref, lse_ref, lsef_ref, off_ref, out_ref, al_far, a_loc):
    c = lax.axis_index("ctx") // 2
    lane = iota((1, DIM), 1)

    def valid(x):
        return ((x < 64) & (c % 2 == 1)) | ((x >= 64) & (x < 96) & (c % 4 >= 2)) | ((x >= 96) & (x < FAR) & (c >= 2))

    @pl.when(pl.program_id(0) == 0)
    def _():
        far = jnp.concatenate([lsef_ref[0, 0], lsef_ref[1, 0], lsef_ref[0, 1], lsef_ref[1, 1]], axis=0)
        far = jnp.where(valid(lane), far, NEG)
        far3 = split3(far)
        tall = iota((DIM, CHUNK), 0) + DIM
        parts, spread, chosen = [lse_ref[...]], [], []
        for level, (first, count, bits) in enumerate(REGIONS):
            if level > 0:
                hit = ((iota((DIM, CHUNK), 1) >> bits) == tall - first) & (tall >= first) & (tall < first + count)
                spread.append(jnp.where(hit, 1.0, 0.0).astype(BF16))
                chosen.append(picked(off_ref, level, bits))
                parts.append(jnp.where(chosen[-1], fold3(nn(far3, spread[-1])), NEG))
        lse = log_sum(parts)
        back = jnp.zeros((2 * HEADS, DIM), F32)
        for pick, wide in zip(chosen, spread):
            back = back + fold3(nt(split3(jnp.where(pick, lse, 0.0)), wide))
        al_far[...] = jnp.exp2(far - back)
        share = jnp.exp2(lse_ref[...] - lse)
        for b in range(2):
            a_loc[b * CHUNK : (b + 1) * CHUNK] = upright(share, b)

    row = lane + DIM
    first = jnp.where(row < 192, 128, jnp.where(row < 224, 192, 224))
    bits = jnp.where(row < 192, 2, jnp.where(row < 224, 3, 4))
    base = iota((CHUNK, DIM), 0) - ((row - first) << bits)
    sent = valid(iota((DIM, DIM), 0))
    for i in range(GROUP):
        h = pl.program_id(0) * GROUP + i
        o2, o3, o4 = [off_ref[level, h] & (2 << level) - 1 for level in (1, 2, 3)]
        hit = base == jnp.where(row < 192, o2, jnp.where(row < 224, o3, o4))
        for b in range(2):
            span = slice(b * CHUNK, (b + 1) * CHUNK)
            weight = jnp.where(hit, al_far[pl.ds(b * HEADS + h, 1), :], 0.0).astype(BF16)
            mixed = nn(weight, jnp.where(sent, far_ref[i, b], jnp.zeros((DIM, DIM), BF16)))
            scale = jnp.sum(jnp.where(lane == h, a_loc[span], 0.0), axis=1, keepdims=True)
            out_ref[0, span, i * DIM : (i + 1) * DIM] = (mixed + scale * loc_ref[i, span].astype(F32)).astype(BF16)


def on_device(queries, key_rows, value_rows, document_ids, dilation_offsets):
    any_space = pl.BlockSpec(memory_space=pl.ANY)
    smem = pl.BlockSpec(memory_space=pltpu.SMEM)
    dma = pltpu.SemaphoreType.DMA

    def vmem(*shape, kind=BF16):
        return pltpu.VMEM(shape, kind)

    local, far, lse, lse_far = pl.pallas_call(
        kernel,
        out_shape=(
            jax.ShapeDtypeStruct((HEADS, ROWS, DIM), BF16),
            jax.ShapeDtypeStruct((HEADS, 2, DIM, DIM), BF16),
            jax.ShapeDtypeStruct((2 * HEADS, CHUNK), F32),
            jax.ShapeDtypeStruct((2, 2, HALF, DIM), F32),
        ),
        in_specs=[any_space, any_space, any_space, pl.BlockSpec(memory_space=pltpu.VMEM), smem],
        out_specs=(any_space,) * 4,
        scratch_shapes=[
            vmem(ROWS, HEADS * DIM), vmem(ROWS, HEADS * DIM), vmem(ROWS, HEADS * DIM),
            vmem(HALF, 4, SEL, DIM), vmem(HALF, 4, SEL, DIM), vmem(HALF, 4, SEL, DIM),
            vmem(HALF, 2, SEL, DIM), vmem(HALF, 2, SEL, DIM), vmem(HALF, 2, SEL, DIM),
            vmem(HALF, 4, FAR, DIM), vmem(HALF, 4, FAR3, DIM), vmem(HALF, 4, FAR3, DIM),
            vmem(HALF, SEL, CHUNK), vmem(2, HALF, SEL, CHUNK), vmem(2, HALF, FAR3, CHUNK), vmem(HALF, SEL, CHUNK),
            vmem(2, HALF, 2, CHUNK, DIM), vmem(HALF, 2, CHUNK, DIM), vmem(2, HALF, 2, FAR, DIM),
            vmem(HEADS, ROWS, DIM, kind=F32), vmem(HEADS, ROWS, DIM),
            vmem(2, 2, CHUNK, DIM, kind=F32), vmem(2, 2, DIM, DIM, kind=F32), vmem(ROWS, DIM, kind=F32),
            vmem(2, 2, HALF, CHUNK, kind=F32), vmem(2, 2, HALF, DIM, kind=F32), vmem(2, HALF, CHUNK, kind=F32),
            vmem(2 * HEADS, CHUNK, kind=F32),
            vmem(6, 1, ROWS, kind=I32), vmem(2 * DIM, CHUNK), vmem(4, 2 * DIM, CHUNK),
            vmem(SEL, CHUNK, kind=I32), vmem(CHUNK, CHUNK, kind=F32), vmem(2, CHUNK, CHUNK, kind=F32),
            vmem(2 * HEADS, CHUNK, kind=F32), vmem(ROWS, DIM, kind=F32),
            dma((4, 2, 3)), dma((HEADS,)), dma((1,)), dma((5,)), dma((6,)), dma((3, HALF)), dma((3, HALF)),
            dma((2, 2, HALF)), dma((2, 2, HALF)), dma((2, HALF)), dma((2, HALF)), dma((2, HALF)), dma((2, HALF)),
            dma((2, 2, HALF)), dma((2, 2, HALF)), dma((HALF,)), dma((HALF,)), dma((3,)), dma((3,)),
        ],
        compiler_params=pltpu.CompilerParams(collective_id=0, has_side_effects=True, vmem_limit_bytes=56 << 20),
        name="dilated_attention",
    )(queries, key_rows, value_rows, document_ids, dilation_offsets)
    return pl.pallas_call(
        join_kernel,
        grid=(HEADS // GROUP,),
        out_shape=jax.ShapeDtypeStruct((1, ROWS, HEADS * DIM), BF16),
        in_specs=[
            pl.BlockSpec((GROUP, ROWS, DIM), lambda i: (i, 0, 0)),
            pl.BlockSpec((GROUP, 2, DIM, DIM), lambda i: (i, 0, 0, 0)),
            pl.BlockSpec(memory_space=pltpu.VMEM),
            pl.BlockSpec(memory_space=pltpu.VMEM),
            smem,
        ],
        out_specs=pl.BlockSpec((1, ROWS, GROUP * DIM), lambda i: (0, 0, i)),
        scratch_shapes=[vmem(2 * HEADS, DIM, kind=F32), vmem(ROWS, DIM, kind=F32)],
        compiler_params=pltpu.CompilerParams(vmem_limit_bytes=60 << 20),
        name="join_far",
    )(local, far, lse, lse_far, dilation_offsets)


def solution(mesh):
    placed = (P("dp", "ctx", None), P("dp", "ctx", None), P("dp", "ctx", None), P("dp", "ctx"), P())
    return jax.shard_map(
        on_device, mesh=mesh, in_specs=placed, out_specs=P("dp", "ctx", None), check_vma=False
    )
```

```python
import math

import jax
import jax.numpy as jnp
from jax import lax
from jax.experimental import pallas as pl
from jax.experimental.pallas import tpu as pltpu
from jax.sharding import PartitionSpec as P

MESH = pl.DeviceIdType.MESH
F32, BF16, I32 = jnp.float32, jnp.bfloat16, jnp.int32
HEADS, HALF, ROWS, DIM, CHUNK = 16, 8, 512, 128, 256
SEL, FAR, FAR3 = 240, 112, 48
REGIONS = ((0, 128, 1), (128, 64, 2), (192, 32, 3), (224, 16, 4))
NEG = -1e30
SCALE2 = math.log2(math.e) / math.sqrt(DIM)


def nt(a, b):
    return lax.dot_general(a, b, (((1,), (1,)), ((), ())), preferred_element_type=F32)


def nn(a, b):
    return jnp.dot(a, b, preferred_element_type=F32)


def split3(x):
    first = x.astype(BF16)
    rest = x - first.astype(F32)
    second = rest.astype(BF16)
    third = (rest - second.astype(F32)).astype(BF16)
    return jnp.concatenate([first, second, third], axis=0)


def fold3(x):
    n = x.shape[0] // 3
    return (x[2 * n :] + x[n : 2 * n]) + x[:n]


def iota(shape, dim):
    return lax.broadcasted_iota(I32, shape, dim)


def attend(problems):
    scores = [nt(q, k) if bias is None else bias(nt(q, k)) for q, k, _, bias in problems]
    tops = [jnp.max(s, axis=1, keepdims=True) for s in scores]
    weights = [jnp.exp2((s - top) * SCALE2).astype(BF16) for s, top in zip(scores, tops)]
    sums = [nn(w, jnp.concatenate([v, jnp.ones_like(v)], axis=1)) for w, (_, _, v, _) in zip(weights, problems)]
    return [(x[:, :DIM] / x[:, DIM:], top * SCALE2 + jnp.log2(x[:, DIM:])) for x, top in zip(sums, tops)]


def far_pieces(chip):
    return (
        (chip % 4 == 3, ((0, FAR),)),
        (chip % 4 == 2, ((64, FAR),)),
        (chip == 1, ((0, 64),)),
        (chip == 5, ((0, 64), (96, FAR))),
        (chip == 4, ((96, FAR),)),
    )


def next_pieces(chip):
    return ((chip % 4 < 2, (0, FAR3)), ((chip == 2) | (chip == 3), (32, FAR3)))


def kernel(
    q_hbm, k_hbm, v_hbm, docs_hbm, off_hbm,
    loc_out, far_out, lse_out, lsef_out,
    docs_ref, off_ref, xv, cx, sx, q1in, kvp, dqs, dks, dps, pbuf,
    ob, oo_in, os1, o0, loc,
    st_own, st1, lse0, ls_own, ls1, lo_in, lse_loc,
    docs_all, ot_q, ot_k, base_m, causal, bias0, al_own, a0,
    load_sem, once, d_recv, x_recv, q_recv, k_recv, l_recv,
):
    me = lax.axis_index("ctx")
    dp = lax.axis_index("dp")
    c = me // 2
    j = me % 2

    def device(steps, core):
        return (dp, ((c + steps + 8) % 8) * 2 + core)

    def remote(src, dst, send, recv, to):
        return pltpu.make_async_remote_copy(
            src_ref=src, dst_ref=dst, send_sem=send, recv_sem=recv, device_id=to, device_id_type=MESH
        )

    store_sem, lse_sem, d_send, x_send, q_send, k_send, o_send, o_recv, oo_send, oo_recv, l_send, l_own_send = [
        once.at[i] for i in range(12)
    ]

    def load_start(u):
        for half in range(2):
            first = HALF * (1 - j) if half == 0 else HALF * j
            span = pl.ds(pl.multiple_of((first + 2 * u) * DIM, DIM), 2 * DIM)
            for i, src in enumerate((q_hbm, k_hbm, v_hbm)):
                pltpu.make_async_copy(src.at[0, :, span], xv.at[i, :, span], load_sem.at[u]).start()

    def load_wait(u):
        part = xv.at[:, :, pl.ds(0, 4 * DIM)]
        pltpu.make_async_copy(part, part, load_sem.at[u]).wait()

    docs_load = pltpu.make_async_copy(docs_hbm, docs_ref, load_sem.at[4])
    off_load = pltpu.make_async_copy(off_hbm, off_ref, load_sem.at[5])
    docs_load.start()
    off_load.start()
    for u in range(4):
        load_start(u)

    for first, count, bits in REGIONS:
        base_m[first : first + count] = iota((count, CHUNK), 1) - (iota((count, CHUNK), 0) << bits)

    near_chips = ((1, c <= 6), (-1, c >= 1))
    barrier = pltpu.get_barrier_semaphore()
    pl.semaphore_signal(barrier, inc=1, device_id=device(0, 1 - j), device_id_type=MESH)
    for g, present in near_chips:

        @pl.when(present)
        def _():
            for core in (0, 1):
                pl.semaphore_signal(barrier, inc=1, device_id=device(g, core), device_id_type=MESH)

    docs_load.wait()
    off_load.wait()
    pl.semaphore_wait(barrier, 1 + jnp.where(c <= 6, 2, 0) + jnp.where(c >= 1, 2, 0))

    def docs_copy(g, core, slot):
        return remote(docs_ref, docs_all.at[slot], d_send, d_recv.at[slot], device(g, core))

    def each_docs(do):
        do(docs_copy(0, 1 - j, j))
        for (g, present), first in zip(near_chips, (4, 2)):

            @pl.when(present)
            def _():
                for core in (0, 1):
                    do(docs_copy(g, core, first + j))

    each_docs(lambda copy: copy.start())
    docs_all[j] = docs_ref[...]

    def core_of(which):
        return 1 - j if which == 0 else j

    def q_copy(t, which, low, high):
        rows = pl.ds(128 + low, high - low)
        return remote(
            sx.at[t, 0, :, rows] if which == 0 else cx.at[t, 0, pl.ds(2 * j, 2), rows],
            q1in.at[t, pl.ds(2 * j, 2), pl.ds(low, high - low)],
            q_send, q_recv.at[t], device(-1, core_of(which)),
        )

    def kv_copy(t, which, low, high):
        rows = pl.ds(192 + low, high - low)
        return remote(
            sx.at[t, pl.ds(1, 2), :, rows] if which == 0 else cx.at[t, pl.ds(1, 2), pl.ds(2 * j, 2), rows],
            kvp.at[t, :, pl.ds(2 * j, 2), pl.ds(low, high - low)],
            k_send, k_recv.at[t], device(1, core_of(which)),
        )

    def each_q(t, which):
        for present, pieces in far_pieces(c):

            @pl.when(present)
            def _():
                for low, high in pieces:
                    q_copy(t, which, low, high).start()

    def each_kv(t, which):
        for present, (low, high) in next_pieces(c):

            @pl.when(present)
            def _():
                kv_copy(t, which, low, high).start()

    def exchange(t):
        return remote(sx.at[t], cx.at[t, :, pl.ds(2 * j, 2)], x_send, x_recv.at[t], device(0, 1 - j))

    def size_of(pieces):
        return sum(high - low for low, high in pieces)

    def got(part, sem):
        remote(part, part, once.at[0], sem, device(0, 1 - j)).wait_recv()

    def sent(part, sem):
        remote(part, part, sem, once.at[0], device(0, 1 - j)).wait_send()

    def picker(h):
        parts = []
        for level, (first, count, bits) in enumerate(REGIONS):
            shift = off_ref[level, h] & ((1 << bits) - 1)
            parts.append(jnp.where(base_m[first : first + count] == shift, 1.0, 0.0))
        return jnp.concatenate(parts, axis=0).astype(BF16)

    def columns(i, h):
        return xv[i, :, pl.ds(pl.multiple_of(h * DIM, DIM), DIM)]

    def select(pick, i, h):
        x = columns(i, h)
        both = nn(pick, jnp.concatenate([x[:CHUNK], x[CHUNK:]], axis=1)).astype(BF16)
        return both[:, :DIM], both[:, DIM:]

    def select_head(t, _):
        @pl.when(t % 2 == 0)
        def _():
            load_wait(t // 2)

        for which in range(2):
            h = HALF * (1 - j) + t if which == 0 else HALF * j + t
            pick = picker(h)
            if which == 1:
                pbuf[t] = pick
            for i in range(3):
                for b, part in enumerate(select(pick, i, h)):
                    if which == 0:
                        sx[t, i, b] = part
                    else:
                        cx[t, i, 2 * j + b] = part
            each_q(t, which)
            each_kv(t, which)
            if which == 0:
                exchange(t).start()
        return 0

    lax.fori_loop(0, HALF, select_head, 0)

    def clear_pads(t, _):
        for b in range(2):
            oo_in[t, b, SEL:] = jnp.zeros((CHUNK - SEL, DIM), BF16)
            for d in range(2):
                ob[d, t, b, SEL:] = jnp.zeros((CHUNK - SEL, DIM), BF16)
        return 0

    lax.fori_loop(0, HALF, clear_pads, 0)

    causal[...] = jnp.where(iota((CHUNK, CHUNK), 1) <= iota((CHUNK, CHUNK), 0), 0.0, NEG)
    eye = jnp.where(iota((CHUNK, CHUNK), 1) == iota((CHUNK, CHUNK), 0), 1.0, 0.0).astype(BF16)
    for b in range(2):
        same = docs_ref[:, b * CHUNK : (b + 1) * CHUNK] == iota((DIM, CHUNK), 0)
        q_one = nt(eye, jnp.where(same, 1.0, 0.0).astype(BF16)).astype(BF16)
        k_one = nt(eye, jnp.where(same, 0.0, NEG).astype(BF16)).astype(BF16)
        bias0[b] = nt(q_one, k_one) + causal[...]

    docs_copy(0, 1 - j, 1 - j).wait_recv()
    for (g, present), first in zip(near_chips, (2, 4)):

        @pl.when(present)
        def _():
            for core in (0, 1):
                docs_copy(g, core, first + core).wait_recv()

        @pl.when(jnp.logical_not(present))
        def _():
            for core in (0, 1):
                docs_all[first + core] = docs_ref[...]

    for b in range(2):
        span = slice(b * CHUNK, (b + 1) * CHUNK)
        ones = [jnp.where(docs_all[g, :, span] == iota((8, CHUNK), 0), 1.0, 0.0) for g in range(4)]
        ones.append(jnp.zeros((DIM - 32, CHUNK), F32))
        ot_q[b * DIM : (b + 1) * DIM] = jnp.concatenate(ones, axis=0).astype(BF16)
        for i, slot in enumerate((0, 1, 4, 5)):
            same = docs_all[slot, :, span] == (iota((DIM, CHUNK), 0) & 7)
            ot_k[i, b * DIM : (b + 1) * DIM] = jnp.where(same, 0.0, NEG).astype(BF16)

    lane = iota((1, DIM), 1)

    def keep(ref, index, rows, t, value):
        old = ref[index + (rows,)]
        ref[index + (rows,)] = jnp.where(lane == t, value, old)

    def join(piece):
        return jnp.concatenate([piece(d, b) for d in range(2) for b in range(2)], axis=0)

    def with_docs(q, g, level, t):
        first, count, _ = REGIONS[level]

        def piece(d, b):
            mark = jnp.where((lane >> 3) == 2 * g + d, 1.0, 0.0).astype(BF16)
            return dqs[t, first : first + count, b * DIM : (b + 1) * DIM] * mark

        return jnp.concatenate([q, join(piece)], axis=1)

    def own_q(t, level):
        first, count, _ = REGIONS[level]
        return with_docs(join(lambda d, b: cx[t, 0, 2 * d + b, first : first + count]), 0, level, t)

    def guest_q(t, level):
        first, count, _ = REGIONS[level]
        return with_docs(join(lambda d, b: q1in[t, 2 * d + b, first - 128 : first - 128 + count]), 1, level, t)

    def own_kv(t, level):
        first, count, _ = REGIONS[level]
        span = slice(first, first + count)
        k = join(lambda d, b: cx[t, 1, 2 * d + b, span])
        kd = join(lambda d, b: dks[d, t, span, b * DIM : (b + 1) * DIM])
        return jnp.concatenate([k, kd], axis=1), join(lambda d, b: cx[t, 2, 2 * d + b, span])

    def both_kv(t, level):
        first, count, _ = REGIONS[level]
        span = slice(first - 192, first - 192 + count)
        k = join(lambda d, b: kvp[t, 0, 2 * d + b, span])
        kd = join(lambda d, b: dps[d, t, span, b * DIM : (b + 1) * DIM])
        v = join(lambda d, b: kvp[t, 1, 2 * d + b, span])
        own_k, own_v = own_kv(t, level)
        return (
            jnp.concatenate([own_k, jnp.concatenate([k, kd], axis=1)], axis=0),
            jnp.concatenate([own_v, v], axis=0),
        )

    def put(t, level, result, out, stats, shift):
        o, lse = result
        first, count, _ = REGIONS[level]
        spot = slice(first - shift, first - shift + count)
        for d in range(2):
            for b in range(2):
                rows = slice((2 * d + b) * count, (2 * d + b + 1) * count)
                out[d, t, b, spot] = o[rows].astype(BF16)
                keep(stats, (d, b), spot, t, lse[rows])

    def near(n):
        return lambda s: s + causal[:n, :n]

    def near_half(n):
        def bias(s):
            return jnp.concatenate([s[:, :n] + causal[:n, :n], s[:, n:]], axis=1)

        return bias

    def partner_out(t):
        return remote(
            ob.at[1 - j, t, :, pl.ds(0, SEL)], oo_in.at[t, :, pl.ds(0, SEL)],
            oo_send, oo_recv, device(0, 1 - j),
        )

    def ret_copy(t, low, high, d):
        return remote(
            os1.at[d, t, :, pl.ds(low, high - low)], far_out.at[HALF * j + t, :, pl.ds(low, high - low)],
            o_send, o_recv, device(1, d),
        )

    plans = (
        (c == 0, "2", ""),
        (c == 1, "34", "34"),
        (c == 5, "34", "3"),
        (c % 4 == 2, "234", ""),
        (c == 3, "4", ""),
        (c == 4, "24", ""),
    )

    def level_head(t, _):
        exchange(t).wait_recv()
        pick = pbuf[t]
        dqs[t] = nt(pick, ot_q[...]).astype(BF16)
        for d in range(2):
            dks[d, t] = nt(pick, ot_k[d]).astype(BF16)
            dps[d, t] = nt(pick[192:], ot_k[2 + d]).astype(BF16)

        problems = []
        q = own_q(t, 0)
        k, v = own_kv(t, 0)
        problems.append((q[:CHUNK], k[:CHUNK], v[:CHUNK], near(CHUNK)))
        late = lambda s: jnp.concatenate([s[:, :CHUNK], s[:, CHUNK:] + causal[...]], axis=1)
        problems.append((q[CHUNK:], k, v, late))
        for level in (1, 2, 3):
            problems.append((own_q(t, level),) + own_kv(t, level) + (near(4 * REGIONS[level][1]),))
        for h in (2 * t, 2 * t + 1):
            q, k, v = columns(0, h), columns(1, h), columns(2, h)
            for b in range(2):
                span = slice(b * CHUNK, (b + 1) * CHUNK)
                problems.append((q[span], k[span], v[span], lambda s, b=b: s + bias0[b]))
        results = attend(problems)
        first = tuple(jnp.concatenate(pair, axis=0) for pair in zip(results[0], results[1]))
        for level, result in enumerate([first] + results[2:5]):
            put(t, level, result, ob, st_own, 0)
        for i in range(2):
            for b in range(2):
                span = slice(b * CHUNK, (b + 1) * CHUNK)
                o, lse = results[5 + 2 * i + b]
                o0[2 * t + i, span] = o
                keep(lse0, (), span, 2 * t + i, lse)

        for present, (low, high) in next_pieces(c - 1):

            @pl.when(present & (c >= 1))
            def _():
                got(kvp.at[t, :, :, pl.ds(low, high - low)], k_recv.at[t])

        for present, pieces in far_pieces(c + 1):

            @pl.when(present & (c <= 6))
            def _():
                got(q1in.at[t, :, pl.ds(0, size_of(pieces))], q_recv.at[t])

        for present, guests, owns in plans:

            @pl.when(present)
            def _():
                problems = []
                for name in guests:
                    level = int(name) - 1
                    kv_pair = own_kv(t, level) if level == 1 else both_kv(t, level)
                    problems.append((guest_q(t, level),) + kv_pair + (None,))
                for name in owns:
                    level = int(name) - 1
                    n = 4 * REGIONS[level][1]
                    problems.append((own_q(t, level),) + both_kv(t, level) + (near_half(n),))
                results = attend(problems)
                for name, result in zip(guests, results):
                    put(t, int(name) - 1, result, os1, st1, 128)
                for name, result in zip(owns, results[len(guests) :]):
                    put(t, int(name) - 1, result, ob, st_own, 0)

        for present, pieces in far_pieces(c + 1):

            @pl.when(present & (c <= 6))
            def _():
                for low, high in pieces:
                    for d in range(2):
                        ret_copy(t, low, high, d).start()

        partner_out(t).start()
        return 0

    lax.fori_loop(0, HALF, level_head, 0)

    for d in range(2):
        for b in range(2):
            ls1[d, b] = st1[d, b].T[:HALF]
            ls_own[d, b] = st_own[d, b].T[:HALF]

    def far_stats(d):
        return remote(ls1.at[d], lsef_out.at[j], l_send, l_recv.at[1 + j], device(1, d))

    @pl.when(c <= 6)
    def _():
        for d in range(2):
            far_stats(d).start()

    l_own = remote(ls_own.at[1 - j], lo_in, l_own_send, l_recv.at[0], device(0, 1 - j))
    l_own.start()
    l_own.wait_recv()

    mine = ls_own[j]
    theirs = lo_in[...]
    lower = jnp.where(j == 0, mine, theirs)
    upper = jnp.where(j == 0, theirs, mine)
    wide = iota((1, CHUNK), 1)
    own = jnp.concatenate([lower[0], upper[0], lower[1], upper[1]], axis=0)
    own = jnp.where(wide < SEL, own, NEG)
    tall = iota((CHUNK, CHUNK), 0)
    own3 = split3(own)
    zeroth = lse0[...].T
    parts = [jnp.concatenate([zeroth[:HEADS, :CHUNK], zeroth[:HEADS, CHUNK:]], axis=0)]
    spread, chosen = [], []
    for level, (first, count, bits) in enumerate(REGIONS):
        hit = ((iota((CHUNK, CHUNK), 1) >> bits) == tall - first) & (tall >= first) & (tall < first + count)
        spread.append(jnp.where(hit, 1.0, 0.0).astype(BF16))
        chosen.append(picked(off_ref, level, bits))
        parts.append(jnp.where(chosen[level], fold3(nn(own3, spread[level])), NEG))
    lse = log_sum(parts)
    back = jnp.zeros((2 * HEADS, CHUNK), F32)
    for level in range(4):
        back = back + fold3(nt(split3(jnp.where(chosen[level], lse, 0.0)), spread[level]))
    al_own[...] = jnp.exp2(own - back)
    lse_loc[...] = lse
    lse_copy = pltpu.make_async_copy(lse_loc, lse_out, lse_sem)
    lse_copy.start()
    for b in range(2):
        span = slice(b * CHUNK, (b + 1) * CHUNK)
        a0[span] = jnp.exp2(lse0[span] - upright(lse, b))

    def loc_copy(h):
        return pltpu.make_async_copy(loc.at[h], loc_out.at[h], store_sem)

    own_first = jnp.where(wide < 128, 0, jnp.where(wide < 192, 128, jnp.where(wide < 224, 192, 224)))
    own_bits = jnp.where(wide < 128, 1, jnp.where(wide < 192, 2, jnp.where(wide < 224, 3, 4)))
    own_base = tall - ((wide - own_first) << own_bits)

    got(oo_in.at[:, :, pl.ds(0, SEL)], oo_recv)

    def local_head(t, _):
        for which in range(2):
            h = HALF * j + t if which == 0 else HALF * (1 - j) + t
            o1, o2, o3, o4 = [off_ref[i, h] & (2 << i) - 1 for i in range(4)]
            shift = jnp.where(wide < 128, o1, jnp.where(wide < 192, o2, jnp.where(wide < 224, o3, o4)))
            hit = own_base == shift
            for b in range(2):
                span = slice(b * CHUNK, (b + 1) * CHUNK)
                weight = jnp.where(hit, al_own[pl.ds(b * HEADS + h, 1), :], 0.0).astype(BF16)
                mixed = nn(weight, ob[j, t, b] if which == 0 else oo_in[t, b])
                scale = jnp.sum(jnp.where(lane == h, a0[span], 0.0), axis=1, keepdims=True)
                loc[h, span] = (mixed + scale * o0[h, span]).astype(BF16)
            loc_copy(h).start()
        return 0

    lax.fori_loop(0, HALF, local_head, 0)

    for present, slots in ((near_chips[0][1] & near_chips[1][1], 5), (c == 0, 3), (c == 7, 3)):

        @pl.when(present)
        def _():
            part = docs_all.at[pl.ds(0, slots)]
            remote(part, part, d_send, d_recv.at[0], device(0, 1 - j)).wait_send()

    l_own.wait_send()
    lse_copy.wait()

    sent(sx, x_send)
    sent(oo_in.at[:, :, pl.ds(0, SEL)], oo_send)
    pltpu.make_async_copy(loc, loc_out, store_sem).wait()
    for present, pieces in far_pieces(c):

        @pl.when(present)
        def _():
            sent(q1in.at[:, :, pl.ds(0, size_of(pieces))], q_send)

    for present, (low, high) in next_pieces(c):

        @pl.when(present)
        def _():
            sent(kvp.at[:, :, :, pl.ds(0, high - low)], k_send)

    for present, pieces in far_pieces(c + 1):

        @pl.when(present & (c <= 6))
        def _():
            sent(os1.at[:, :, :, pl.ds(0, size_of(pieces))], o_send)
            sent(ls1, l_send)

    for present, pieces in far_pieces(c):

        @pl.when(present)
        def _():
            got(far_out.at[:, :, pl.ds(0, size_of(pieces))], o_recv)
            for i in range(2):
                got(lsef_out.at[i], l_recv.at[1 + i])


def picked(off_ref, level, bits):
    head = iota((HEADS, CHUNK), 0)
    shifts = jnp.zeros((HEADS, CHUNK), I32)
    for h in range(HEADS):
        shifts = jnp.where(head == h, off_ref[level, h] & ((1 << bits) - 1), shifts)
    pick = (iota((HEADS, CHUNK), 1) & ((1 << bits) - 1)) == shifts
    return jnp.concatenate([pick, pick], axis=0)


def log_sum(parts):
    top = parts[0]
    for part in parts[1:]:
        top = jnp.maximum(top, part)
    total = jnp.exp2(parts[0] - top)
    for part in parts[1:]:
        total = total + jnp.exp2(part - top)
    return top + jnp.log2(total)


def upright(dense, b):
    pad = jnp.zeros((DIM - HEADS, CHUNK), F32)
    return jnp.concatenate([dense[b * HEADS : (b + 1) * HEADS], pad], axis=0).T


GROUP = 8


def join_kernel(loc_ref, far_ref, lse_ref, lsef_ref, off_ref, out_ref, al_far, a_loc):
    c = lax.axis_index("ctx") // 2
    lane = iota((1, DIM), 1)

    def valid(x):
        return ((x < 64) & (c % 2 == 1)) | ((x >= 64) & (x < 96) & (c % 4 >= 2)) | ((x >= 96) & (x < FAR) & (c >= 2))

    @pl.when(pl.program_id(0) == 0)
    def _():
        far = jnp.concatenate([lsef_ref[0, 0], lsef_ref[1, 0], lsef_ref[0, 1], lsef_ref[1, 1]], axis=0)
        far = jnp.where(valid(lane), far, NEG)
        far3 = split3(far)
        tall = iota((DIM, CHUNK), 0) + DIM
        parts, spread, chosen = [lse_ref[...]], [], []
        for level, (first, count, bits) in enumerate(REGIONS):
            if level > 0:
                hit = ((iota((DIM, CHUNK), 1) >> bits) == tall - first) & (tall >= first) & (tall < first + count)
                spread.append(jnp.where(hit, 1.0, 0.0).astype(BF16))
                chosen.append(picked(off_ref, level, bits))
                parts.append(jnp.where(chosen[-1], fold3(nn(far3, spread[-1])), NEG))
        lse = log_sum(parts)
        back = jnp.zeros((2 * HEADS, DIM), F32)
        for pick, wide in zip(chosen, spread):
            back = back + fold3(nt(split3(jnp.where(pick, lse, 0.0)), wide))
        al_far[...] = jnp.exp2(far - back)
        share = jnp.exp2(lse_ref[...] - lse)
        for b in range(2):
            a_loc[b * CHUNK : (b + 1) * CHUNK] = upright(share, b)

    row = lane + DIM
    first = jnp.where(row < 192, 128, jnp.where(row < 224, 192, 224))
    bits = jnp.where(row < 192, 2, jnp.where(row < 224, 3, 4))
    base = iota((CHUNK, DIM), 0) - ((row - first) << bits)
    sent = valid(iota((DIM, DIM), 0))
    for i in range(GROUP):
        h = pl.program_id(0) * GROUP + i
        o2, o3, o4 = [off_ref[level, h] & (2 << level) - 1 for level in (1, 2, 3)]
        hit = base == jnp.where(row < 192, o2, jnp.where(row < 224, o3, o4))
        for b in range(2):
            span = slice(b * CHUNK, (b + 1) * CHUNK)
            weight = jnp.where(hit, al_far[pl.ds(b * HEADS + h, 1), :], 0.0).astype(BF16)
            mixed = nn(weight, jnp.where(sent, far_ref[i, b], jnp.zeros((DIM, DIM), BF16)))
            scale = jnp.sum(jnp.where(lane == h, a_loc[span], 0.0), axis=1, keepdims=True)
            out_ref[0, span, i * DIM : (i + 1) * DIM] = (mixed + scale * loc_ref[i, span].astype(F32)).astype(BF16)


def on_device(queries, key_rows, value_rows, document_ids, dilation_offsets):
    any_space = pl.BlockSpec(memory_space=pl.ANY)
    smem = pl.BlockSpec(memory_space=pltpu.SMEM)
    dma = pltpu.SemaphoreType.DMA

    def vmem(*shape, kind=BF16):
        return pltpu.VMEM(shape, kind)

    local, far, lse, lse_far = pl.pallas_call(
        kernel,
        out_shape=(
            jax.ShapeDtypeStruct((HEADS, ROWS, DIM), BF16),
            jax.ShapeDtypeStruct((HEADS, 2, DIM, DIM), BF16),
            jax.ShapeDtypeStruct((2 * HEADS, CHUNK), F32),
            jax.ShapeDtypeStruct((2, 2, HALF, DIM), F32),
        ),
        in_specs=[any_space] * 5,
        out_specs=(any_space,) * 4,
        scratch_shapes=[
            vmem(1, ROWS, kind=I32), pltpu.SMEM((4, HEADS), I32), vmem(3, ROWS, HEADS * DIM),
            vmem(HALF, 3, 4, SEL, DIM), vmem(HALF, 3, 2, SEL, DIM), vmem(HALF, 4, FAR, DIM), vmem(HALF, 2, 4, FAR3, DIM),
            vmem(HALF, SEL, CHUNK), vmem(2, HALF, SEL, CHUNK), vmem(2, HALF, FAR3, CHUNK), vmem(HALF, SEL, CHUNK),
            vmem(2, HALF, 2, CHUNK, DIM), vmem(HALF, 2, CHUNK, DIM), vmem(2, HALF, 2, FAR, DIM),
            vmem(HEADS, ROWS, DIM, kind=F32), vmem(HEADS, ROWS, DIM),
            vmem(2, 2, CHUNK, DIM, kind=F32), vmem(2, 2, DIM, DIM, kind=F32), vmem(ROWS, DIM, kind=F32),
            vmem(2, 2, HALF, CHUNK, kind=F32), vmem(2, 2, HALF, DIM, kind=F32), vmem(2, HALF, CHUNK, kind=F32),
            vmem(2 * HEADS, CHUNK, kind=F32),
            vmem(6, 1, ROWS, kind=I32), vmem(2 * DIM, CHUNK), vmem(4, 2 * DIM, CHUNK),
            vmem(SEL, CHUNK, kind=I32), vmem(CHUNK, CHUNK, kind=F32), vmem(2, CHUNK, CHUNK, kind=F32),
            vmem(2 * HEADS, CHUNK, kind=F32), vmem(ROWS, DIM, kind=F32),
            dma((6,)), dma((12,)), dma((6,)), dma((HALF,)), dma((HALF,)), dma((HALF,)), dma((3,)),
        ],
        compiler_params=pltpu.CompilerParams(collective_id=0, has_side_effects=True, vmem_limit_bytes=56 << 20),
        name="dilated_attention",
    )(queries, key_rows, value_rows, document_ids, dilation_offsets)
    return pl.pallas_call(
        join_kernel,
        grid=(HEADS // GROUP,),
        out_shape=jax.ShapeDtypeStruct((1, ROWS, HEADS * DIM), BF16),
        in_specs=[
            pl.BlockSpec((GROUP, ROWS, DIM), lambda i: (i, 0, 0)),
            pl.BlockSpec((GROUP, 2, DIM, DIM), lambda i: (i, 0, 0, 0)),
            pl.BlockSpec(memory_space=pltpu.VMEM),
            pl.BlockSpec(memory_space=pltpu.VMEM),
            smem,
        ],
        out_specs=pl.BlockSpec((1, ROWS, GROUP * DIM), lambda i: (0, 0, i)),
        scratch_shapes=[vmem(2 * HEADS, DIM, kind=F32), vmem(ROWS, DIM, kind=F32)],
        compiler_params=pltpu.CompilerParams(vmem_limit_bytes=60 << 20),
        name="join_far",
    )(local, far, lse, lse_far, dilation_offsets)


def solution(mesh):
    placed = (P("dp", "ctx", None), P("dp", "ctx", None), P("dp", "ctx", None), P("dp", "ctx"), P())
    return jax.shard_map(
        on_device, mesh=mesh, in_specs=placed, out_specs=P("dp", "ctx", None), check_vma=False
    )
```

```python
import math

import jax
import jax.numpy as jnp
from jax import lax
from jax.experimental import pallas as pl
from jax.experimental.pallas import tpu as pltpu
from jax.sharding import PartitionSpec as P

MESH = pl.DeviceIdType.MESH
F32, BF16, I32 = jnp.float32, jnp.bfloat16, jnp.int32
HEADS, HALF, ROWS, DIM, CHUNK = 16, 8, 512, 128, 256
SEL, FAR, FAR3 = 240, 112, 48
REGIONS = ((0, 128, 1), (128, 64, 2), (192, 32, 3), (224, 16, 4))
NEG = -1e30
SCALE2 = math.log2(math.e) / math.sqrt(DIM)


def nt(a, b):
    return lax.dot_general(a, b, (((1,), (1,)), ((), ())), preferred_element_type=F32)


def nn(a, b):
    return jnp.dot(a, b, preferred_element_type=F32)


def split3(x):
    first = x.astype(BF16)
    rest = x - first.astype(F32)
    second = rest.astype(BF16)
    third = (rest - second.astype(F32)).astype(BF16)
    return jnp.concatenate([first, second, third], axis=0)


def fold3(x):
    n = x.shape[0] // 3
    return (x[2 * n :] + x[n : 2 * n]) + x[:n]


def iota(shape, dim):
    return lax.broadcasted_iota(I32, shape, dim)


def attend(problems):
    scores = [nt(q, k) if bias is None else bias(nt(q, k)) for q, k, _, bias in problems]
    tops = [jnp.max(s, axis=1, keepdims=True) for s in scores]
    weights = [jnp.exp2((s - top) * SCALE2).astype(BF16) for s, top in zip(scores, tops)]
    sums = [nn(w, jnp.concatenate([v, jnp.ones_like(v)], axis=1)) for w, (_, _, v, _) in zip(weights, problems)]
    return [(x[:, :DIM] / x[:, DIM:], top * SCALE2 + jnp.log2(x[:, DIM:])) for x, top in zip(sums, tops)]


def far_pieces(chip):
    return (
        (chip % 4 == 3, ((0, FAR),)),
        (chip % 4 == 2, ((64, FAR),)),
        (chip % 4 == 1, ((0, 64),)),
        (chip == 4, ((96, FAR),)),
    )


def next_pieces(chip):
    return ((chip % 4 < 2, (0, FAR3)), (chip == 2, (32, FAR3)))


def kernel(
    q_hbm, k_hbm, v_hbm, docs_hbm, off_hbm,
    loc_out, far_out, lse_out, lsef_out, lsef2_out,
    docs_ref, off_ref, xv, cx, sx, q1in, q2in, kvp, dqs, dks, dps, pbuf,
    ob, oo_in, os1, os2, o0, loc,
    st_own, st1, st2, lse0, ls_own, ls1, ls2, lo_in, lse_loc,
    docs_all, ot_q, ot_k, base_m, causal, bias0, al_own, a0,
    load_sem, once, d_recv, x_recv, q_recv, k_recv, l_recv,
):
    me = lax.axis_index("ctx")
    dp = lax.axis_index("dp")
    c = me // 2
    j = me % 2

    def device(steps, core):
        return (dp, ((c + steps + 8) % 8) * 2 + core)

    def remote(src, dst, send, recv, to):
        return pltpu.make_async_remote_copy(
            src_ref=src, dst_ref=dst, send_sem=send, recv_sem=recv, device_id=to, device_id_type=MESH
        )

    store_sem, lse_sem, d_send, x_send, q_send, k_send, o_send, o_recv, oo_send, oo_recv, l_send, l_own_send, two_send, two_recv, o_two_send, o_two_recv, l_two_send = [
        once.at[i] for i in range(17)
    ]

    def load_start(u):
        for half in range(2):
            first = HALF * (1 - j) if half == 0 else HALF * j
            span = pl.ds(pl.multiple_of((first + 2 * u) * DIM, DIM), 2 * DIM)
            for i, src in enumerate((q_hbm, k_hbm, v_hbm)):
                pltpu.make_async_copy(src.at[0, :, span], xv.at[i, :, span], load_sem.at[u]).start()

    def load_wait(u):
        part = xv.at[:, :, pl.ds(0, 4 * DIM)]
        pltpu.make_async_copy(part, part, load_sem.at[u]).wait()

    docs_load = pltpu.make_async_copy(docs_hbm, docs_ref, load_sem.at[4])
    off_load = pltpu.make_async_copy(off_hbm, off_ref, load_sem.at[5])
    docs_load.start()
    off_load.start()
    for u in range(4):
        load_start(u)

    for first, count, bits in REGIONS:
        base_m[first : first + count] = iota((count, CHUNK), 1) - (iota((count, CHUNK), 0) << bits)

    near_chips = ((1, c <= 6), (-1, c >= 1))
    barrier = pltpu.get_barrier_semaphore()
    pl.semaphore_signal(barrier, inc=1, device_id=device(0, 1 - j), device_id_type=MESH)
    for g, present in near_chips:

        @pl.when(present)
        def _():
            for core in (0, 1):
                pl.semaphore_signal(barrier, inc=1, device_id=device(g, core), device_id_type=MESH)

    guest_of_two = ((c == 5, -2), (c == 3, 2))
    for present, g in guest_of_two:

        @pl.when(present)
        def _():
            for core in (0, 1):
                pl.semaphore_signal(barrier, inc=1, device_id=device(g, core), device_id_type=MESH)

    docs_load.wait()
    off_load.wait()
    pl.semaphore_wait(barrier, 1 + jnp.where(c <= 6, 2, 0) + jnp.where(c >= 1, 2, 0) + jnp.where((c == 3) | (c == 5), 2, 0))

    def docs_copy(g, core, slot):
        return remote(docs_ref, docs_all.at[slot], d_send, d_recv.at[slot], device(g, core))

    def each_docs(do):
        do(docs_copy(0, 1 - j, j))
        for (g, present), first in zip(near_chips, (4, 2)):

            @pl.when(present)
            def _():
                for core in (0, 1):
                    do(docs_copy(g, core, first + j))

        @pl.when(c == 5)
        def _():
            for core in (0, 1):
                do(docs_copy(-2, core, 6 + j))

    each_docs(lambda copy: copy.start())
    docs_all[j] = docs_ref[...]

    def core_of(which):
        return 1 - j if which == 0 else j

    def q_copy(t, which, low, high):
        rows = pl.ds(128 + low, high - low)
        return remote(
            sx.at[t, 0, :, rows] if which == 0 else cx.at[t, 0, pl.ds(2 * j, 2), rows],
            q1in.at[t, pl.ds(2 * j, 2), pl.ds(low, high - low)],
            q_send, q_recv.at[t], device(-1, core_of(which)),
        )

    def kv_copy(t, which, low, high):
        rows = pl.ds(192 + low, high - low)
        return remote(
            sx.at[t, pl.ds(1, 2), :, rows] if which == 0 else cx.at[t, pl.ds(1, 2), pl.ds(2 * j, 2), rows],
            kvp.at[t, :, pl.ds(2 * j, 2), pl.ds(low, high - low)],
            k_send, k_recv.at[t], device(1, core_of(which)),
        )

    def two_copy(t, which):
        rows = pl.ds(224, 16)
        return remote(
            sx.at[t, 0, :, rows] if which == 0 else cx.at[t, 0, pl.ds(2 * j, 2), rows],
            q2in.at[t, pl.ds(2 * j, 2)], two_send, two_recv, device(-2, core_of(which)),
        )

    def each_q(t, which):
        @pl.when(c == 5)
        def _():
            two_copy(t, which).start()

        for present, pieces in far_pieces(c):

            @pl.when(present)
            def _():
                for low, high in pieces:
                    q_copy(t, which, low, high).start()

    def each_kv(t, which):
        for present, (low, high) in next_pieces(c):

            @pl.when(present)
            def _():
                kv_copy(t, which, low, high).start()

    def exchange(t):
        return remote(sx.at[t], cx.at[t, :, pl.ds(2 * j, 2)], x_send, x_recv.at[t], device(0, 1 - j))

    def size_of(pieces):
        return sum(high - low for low, high in pieces)

    def got(part, sem):
        remote(part, part, once.at[0], sem, device(0, 1 - j)).wait_recv()

    def sent(part, sem):
        remote(part, part, sem, once.at[0], device(0, 1 - j)).wait_send()

    def picker(h):
        parts = []
        for level, (first, count, bits) in enumerate(REGIONS):
            shift = off_ref[level, h] & ((1 << bits) - 1)
            parts.append(jnp.where(base_m[first : first + count] == shift, 1.0, 0.0))
        return jnp.concatenate(parts, axis=0).astype(BF16)

    def columns(i, h):
        return xv[i, :, pl.ds(pl.multiple_of(h * DIM, DIM), DIM)]

    def select(pick, i, h):
        x = columns(i, h)
        both = nn(pick, jnp.concatenate([x[:CHUNK], x[CHUNK:]], axis=1)).astype(BF16)
        return both[:, :DIM], both[:, DIM:]

    def select_head(t, _):
        @pl.when(t % 2 == 0)
        def _():
            load_wait(t // 2)

        for which in range(2):
            h = HALF * (1 - j) + t if which == 0 else HALF * j + t
            pick = picker(h)
            if which == 1:
                pbuf[t] = pick
            for i in range(3):
                for b, part in enumerate(select(pick, i, h)):
                    if which == 0:
                        sx[t, i, b] = part
                    else:
                        cx[t, i, 2 * j + b] = part
            each_q(t, which)
            each_kv(t, which)
            if which == 0:
                exchange(t).start()
        return 0

    lax.fori_loop(0, HALF, select_head, 0)

    def clear_pads(t, _):
        for b in range(2):
            oo_in[t, b, SEL:] = jnp.zeros((CHUNK - SEL, DIM), BF16)
            for d in range(2):
                ob[d, t, b, SEL:] = jnp.zeros((CHUNK - SEL, DIM), BF16)
        return 0

    lax.fori_loop(0, HALF, clear_pads, 0)

    causal[...] = jnp.where(iota((CHUNK, CHUNK), 1) <= iota((CHUNK, CHUNK), 0), 0.0, NEG)
    eye = jnp.where(iota((CHUNK, CHUNK), 1) == iota((CHUNK, CHUNK), 0), 1.0, 0.0).astype(BF16)
    for b in range(2):
        same = docs_ref[:, b * CHUNK : (b + 1) * CHUNK] == iota((DIM, CHUNK), 0)
        q_one = nt(eye, jnp.where(same, 1.0, 0.0).astype(BF16)).astype(BF16)
        k_one = nt(eye, jnp.where(same, 0.0, NEG).astype(BF16)).astype(BF16)
        bias0[b] = nt(q_one, k_one) + causal[...]

    docs_copy(0, 1 - j, 1 - j).wait_recv()
    for (g, present), first in zip(near_chips, (2, 4)):

        @pl.when(present)
        def _():
            for core in (0, 1):
                docs_copy(g, core, first + core).wait_recv()

        @pl.when(jnp.logical_not(present))
        def _():
            for core in (0, 1):
                docs_all[first + core] = docs_ref[...]

    @pl.when(c == 3)
    def _():
        for core in (0, 1):
            docs_copy(-2, core, 6 + core).wait_recv()

    @pl.when(c != 3)
    def _():
        for core in (0, 1):
            docs_all[6 + core] = docs_ref[...]

    for b in range(2):
        span = slice(b * CHUNK, (b + 1) * CHUNK)
        ones = [jnp.where(docs_all[g, :, span] == iota((8, CHUNK), 0), 1.0, 0.0) for g in (0, 1, 2, 3, 6, 7)]
        ones.append(jnp.zeros((DIM - 48, CHUNK), F32))
        ot_q[b * DIM : (b + 1) * DIM] = jnp.concatenate(ones, axis=0).astype(BF16)
        for i, slot in enumerate((0, 1, 4, 5)):
            same = docs_all[slot, :, span] == (iota((DIM, CHUNK), 0) & 7)
            ot_k[i, b * DIM : (b + 1) * DIM] = jnp.where(same, 0.0, NEG).astype(BF16)

    lane = iota((1, DIM), 1)

    def keep(ref, index, rows, t, value):
        old = ref[index + (rows,)]
        ref[index + (rows,)] = jnp.where(lane == t, value, old)

    def join(piece):
        return jnp.concatenate([piece(d, b) for d in range(2) for b in range(2)], axis=0)

    def with_docs(q, g, level, t):
        first, count, _ = REGIONS[level]

        def piece(d, b):
            mark = jnp.where((lane >> 3) == 2 * g + d, 1.0, 0.0).astype(BF16)
            return dqs[t, first : first + count, b * DIM : (b + 1) * DIM] * mark

        return jnp.concatenate([q, join(piece)], axis=1)

    def own_q(t, level):
        first, count, _ = REGIONS[level]
        return with_docs(join(lambda d, b: cx[t, 0, 2 * d + b, first : first + count]), 0, level, t)

    def guest_q(t, level):
        first, count, _ = REGIONS[level]
        return with_docs(join(lambda d, b: q1in[t, 2 * d + b, first - 128 : first - 128 + count]), 1, level, t)

    def own_kv(t, level):
        first, count, _ = REGIONS[level]
        span = slice(first, first + count)
        k = join(lambda d, b: cx[t, 1, 2 * d + b, span])
        kd = join(lambda d, b: dks[d, t, span, b * DIM : (b + 1) * DIM])
        return jnp.concatenate([k, kd], axis=1), join(lambda d, b: cx[t, 2, 2 * d + b, span])

    def both_kv(t, level):
        first, count, _ = REGIONS[level]
        span = slice(first - 192, first - 192 + count)
        k = join(lambda d, b: kvp[t, 0, 2 * d + b, span])
        kd = join(lambda d, b: dps[d, t, span, b * DIM : (b + 1) * DIM])
        v = join(lambda d, b: kvp[t, 1, 2 * d + b, span])
        own_k, own_v = own_kv(t, level)
        return (
            jnp.concatenate([own_k, jnp.concatenate([k, kd], axis=1)], axis=0),
            jnp.concatenate([own_v, v], axis=0),
        )

    def put(t, level, result, out, stats, shift):
        o, lse = result
        first, count, _ = REGIONS[level]
        spot = slice(first - shift, first - shift + count)
        for d in range(2):
            for b in range(2):
                rows = slice((2 * d + b) * count, (2 * d + b + 1) * count)
                out[d, t, b, spot] = o[rows].astype(BF16)
                keep(stats, (d, b), spot, t, lse[rows])

    def near(n):
        return lambda s: s + causal[:n, :n]

    def near_half(n):
        def bias(s):
            return jnp.concatenate([s[:, :n] + causal[:n, :n], s[:, n:]], axis=1)

        return bias

    def partner_out(t):
        return remote(
            ob.at[1 - j, t, :, pl.ds(0, SEL)], oo_in.at[t, :, pl.ds(0, SEL)],
            oo_send, oo_recv, device(0, 1 - j),
        )

    def ret_copy(t, low, high, d):
        return remote(
            os1.at[d, t, :, pl.ds(low, high - low)], far_out.at[HALF * j + t, :, pl.ds(low, high - low)],
            o_send, o_recv, device(1, d),
        )

    plans = (
        (c % 4 == 0, "2", ""),
        (c % 4 == 1, "34", "34"),
        (c % 4 == 2, "234", ""),
        (c == 3, "4", ""),
    )

    def level_head(t, _):
        exchange(t).wait_recv()
        pick = pbuf[t]
        dqs[t] = nt(pick, ot_q[...]).astype(BF16)
        for d in range(2):
            dks[d, t] = nt(pick, ot_k[d]).astype(BF16)
            dps[d, t] = nt(pick[192:], ot_k[2 + d]).astype(BF16)

        problems = []
        q = own_q(t, 0)
        k, v = own_kv(t, 0)
        problems.append((q[:CHUNK], k[:CHUNK], v[:CHUNK], near(CHUNK)))
        late = lambda s: jnp.concatenate([s[:, :CHUNK], s[:, CHUNK:] + causal[...]], axis=1)
        problems.append((q[CHUNK:], k, v, late))
        for level in (1, 2, 3):
            problems.append((own_q(t, level),) + own_kv(t, level) + (near(4 * REGIONS[level][1]),))
        for h in (2 * t, 2 * t + 1):
            q, k, v = columns(0, h), columns(1, h), columns(2, h)
            for b in range(2):
                span = slice(b * CHUNK, (b + 1) * CHUNK)
                problems.append((q[span], k[span], v[span], lambda s, b=b: s + bias0[b]))
        results = attend(problems)
        first = tuple(jnp.concatenate(pair, axis=0) for pair in zip(results[0], results[1]))
        for level, result in enumerate([first] + results[2:5]):
            put(t, level, result, ob, st_own, 0)
        for i in range(2):
            for b in range(2):
                span = slice(b * CHUNK, (b + 1) * CHUNK)
                o, lse = results[5 + 2 * i + b]
                o0[2 * t + i, span] = o
                keep(lse0, (), span, 2 * t + i, lse)

        for present, (low, high) in next_pieces(c - 1):

            @pl.when(present & (c >= 1))
            def _():
                got(kvp.at[t, :, :, pl.ds(low, high - low)], k_recv.at[t])

        for present, pieces in far_pieces(c + 1):

            @pl.when(present & (c <= 6))
            def _():
                got(q1in.at[t, :, pl.ds(0, size_of(pieces))], q_recv.at[t])

        for present, guests, owns in plans:

            @pl.when(present)
            def _():
                problems = []
                for name in guests:
                    level = int(name) - 1
                    kv_pair = own_kv(t, level) if level == 1 else both_kv(t, level)
                    problems.append((guest_q(t, level),) + kv_pair + (None,))
                for name in owns:
                    level = int(name) - 1
                    n = 4 * REGIONS[level][1]
                    problems.append((own_q(t, level),) + both_kv(t, level) + (near_half(n),))
                results = attend(problems)
                for name, result in zip(guests, results):
                    put(t, int(name) - 1, result, os1, st1, 128)
                for name, result in zip(owns, results[len(guests) :]):
                    put(t, int(name) - 1, result, ob, st_own, 0)

        for present, pieces in far_pieces(c + 1):

            @pl.when(present & (c <= 6))
            def _():
                for low, high in pieces:
                    for d in range(2):
                        ret_copy(t, low, high, d).start()

        partner_out(t).start()
        return 0

    lax.fori_loop(0, HALF, level_head, 0)

    def two_back(d):
        return remote(
            os2.at[d], far_out.at[pl.ds(pl.multiple_of(HALF * j, HALF), HALF), :, pl.ds(96, 16)],
            o_two_send, o_two_recv, device(2, d),
        )

    def two_stats(d):
        return remote(ls2.at[d], lsef2_out.at[j], l_two_send, l_recv.at[3 + j], device(2, d))

    @pl.when(c == 3)
    def _():
        got(q2in, two_recv)
        problems = []
        for t in range(HALF):
            q = with_docs(join(lambda d, b: q2in[t, 2 * d + b]), 2, 3, t)
            problems.append((q,) + own_kv(t, 3) + (None,))
        for t, (o, lse) in enumerate(attend(problems)):
            for d in range(2):
                for b in range(2):
                    rows = slice((2 * d + b) * 16, (2 * d + b + 1) * 16)
                    os2[d, t, b] = o[rows].astype(BF16)
                    keep(st2, (d, b), slice(96, FAR), t, lse[rows])
        for d in range(2):
            for b in range(2):
                ls2[d, b] = st2[d, b].T[:HALF]
        for d in range(2):
            two_back(d).start()
            two_stats(d).start()

    for d in range(2):
        for b in range(2):
            ls1[d, b] = st1[d, b].T[:HALF]
            ls_own[d, b] = st_own[d, b].T[:HALF]

    def far_stats(d):
        return remote(ls1.at[d], lsef_out.at[j], l_send, l_recv.at[1 + j], device(1, d))

    @pl.when(c <= 6)
    def _():
        for d in range(2):
            far_stats(d).start()

    l_own = remote(ls_own.at[1 - j], lo_in, l_own_send, l_recv.at[0], device(0, 1 - j))
    l_own.start()
    l_own.wait_recv()

    mine = ls_own[j]
    theirs = lo_in[...]
    lower = jnp.where(j == 0, mine, theirs)
    upper = jnp.where(j == 0, theirs, mine)
    wide = iota((1, CHUNK), 1)
    own = jnp.concatenate([lower[0], upper[0], lower[1], upper[1]], axis=0)
    own = jnp.where(wide < SEL, own, NEG)
    tall = iota((CHUNK, CHUNK), 0)
    own3 = split3(own)
    zeroth = lse0[...].T
    parts = [jnp.concatenate([zeroth[:HEADS, :CHUNK], zeroth[:HEADS, CHUNK:]], axis=0)]
    spread, chosen = [], []
    for level, (first, count, bits) in enumerate(REGIONS):
        hit = ((iota((CHUNK, CHUNK), 1) >> bits) == tall - first) & (tall >= first) & (tall < first + count)
        spread.append(jnp.where(hit, 1.0, 0.0).astype(BF16))
        chosen.append(picked(off_ref, level, bits))
        parts.append(jnp.where(chosen[level], fold3(nn(own3, spread[level])), NEG))
    lse = log_sum(parts)
    back = jnp.zeros((2 * HEADS, CHUNK), F32)
    for level in range(4):
        back = back + fold3(nt(split3(jnp.where(chosen[level], lse, 0.0)), spread[level]))
    al_own[...] = jnp.exp2(own - back)
    lse_loc[...] = lse
    lse_copy = pltpu.make_async_copy(lse_loc, lse_out, lse_sem)
    lse_copy.start()
    for b in range(2):
        span = slice(b * CHUNK, (b + 1) * CHUNK)
        a0[span] = jnp.exp2(lse0[span] - upright(lse, b))

    def loc_copy(h):
        return pltpu.make_async_copy(loc.at[h], loc_out.at[h], store_sem)

    own_first = jnp.where(wide < 128, 0, jnp.where(wide < 192, 128, jnp.where(wide < 224, 192, 224)))
    own_bits = jnp.where(wide < 128, 1, jnp.where(wide < 192, 2, jnp.where(wide < 224, 3, 4)))
    own_base = tall - ((wide - own_first) << own_bits)

    got(oo_in.at[:, :, pl.ds(0, SEL)], oo_recv)

    def local_head(t, _):
        for which in range(2):
            h = HALF * j + t if which == 0 else HALF * (1 - j) + t
            o1, o2, o3, o4 = [off_ref[i, h] & (2 << i) - 1 for i in range(4)]
            shift = jnp.where(wide < 128, o1, jnp.where(wide < 192, o2, jnp.where(wide < 224, o3, o4)))
            hit = own_base == shift
            for b in range(2):
                span = slice(b * CHUNK, (b + 1) * CHUNK)
                weight = jnp.where(hit, al_own[pl.ds(b * HEADS + h, 1), :], 0.0).astype(BF16)
                mixed = nn(weight, ob[j, t, b] if which == 0 else oo_in[t, b])
                scale = jnp.sum(jnp.where(lane == h, a0[span], 0.0), axis=1, keepdims=True)
                loc[h, span] = (mixed + scale * o0[h, span]).astype(BF16)
            loc_copy(h).start()
        return 0

    lax.fori_loop(0, HALF, local_head, 0)

    for present, slots in (((c > 0) & (c < 7) & (c != 5), 5), ((c == 0) | (c == 7), 3), (c == 5, 7)):

        @pl.when(present)
        def _():
            part = docs_all.at[pl.ds(0, slots)]
            remote(part, part, d_send, d_recv.at[0], device(0, 1 - j)).wait_send()

    l_own.wait_send()
    lse_copy.wait()

    sent(sx, x_send)
    sent(oo_in.at[:, :, pl.ds(0, SEL)], oo_send)
    pltpu.make_async_copy(loc, loc_out, store_sem).wait()
    for present, pieces in far_pieces(c):

        @pl.when(present)
        def _():
            sent(q1in.at[:, :, pl.ds(0, size_of(pieces))], q_send)

    for present, (low, high) in next_pieces(c):

        @pl.when(present)
        def _():
            sent(kvp.at[:, :, :, pl.ds(0, high - low)], k_send)

    for present, pieces in far_pieces(c + 1):

        @pl.when(present & (c <= 6))
        def _():
            sent(os1.at[:, :, :, pl.ds(0, size_of(pieces))], o_send)
            sent(ls1, l_send)

    @pl.when(c == 3)
    def _():
        sent(os2, o_two_send)
        sent(ls2, l_two_send)

    @pl.when(c == 5)
    def _():
        sent(q2in, two_send)
        got(far_out.at[:, :, pl.ds(0, 16)], o_two_recv)
        for i in range(2):
            got(lsef2_out.at[i], l_recv.at[3 + i])

    for present, pieces in far_pieces(c):

        @pl.when(present)
        def _():
            got(far_out.at[:, :, pl.ds(0, size_of(pieces))], o_recv)
            for i in range(2):
                got(lsef_out.at[i], l_recv.at[1 + i])


def picked(off_ref, level, bits):
    head = iota((HEADS, CHUNK), 0)
    shifts = jnp.zeros((HEADS, CHUNK), I32)
    for h in range(HEADS):
        shifts = jnp.where(head == h, off_ref[level, h] & ((1 << bits) - 1), shifts)
    pick = (iota((HEADS, CHUNK), 1) & ((1 << bits) - 1)) == shifts
    return jnp.concatenate([pick, pick], axis=0)


def log_sum(parts):
    top = parts[0]
    for part in parts[1:]:
        top = jnp.maximum(top, part)
    total = jnp.exp2(parts[0] - top)
    for part in parts[1:]:
        total = total + jnp.exp2(part - top)
    return top + jnp.log2(total)


def upright(dense, b):
    pad = jnp.zeros((DIM - HEADS, CHUNK), F32)
    return jnp.concatenate([dense[b * HEADS : (b + 1) * HEADS], pad], axis=0).T


GROUP = 8


def join_kernel(loc_ref, far_ref, lse_ref, lsef_ref, lsef2_ref, off_ref, out_ref, al_far, a_loc):
    c = lax.axis_index("ctx") // 2
    lane = iota((1, DIM), 1)

    def valid(x):
        return ((x < 64) & (c % 2 == 1)) | ((x >= 64) & (x < 96) & (c % 4 >= 2)) | ((x >= 96) & (x < FAR) & (c >= 2))

    @pl.when(pl.program_id(0) == 0)
    def _():
        one, two = [
            jnp.concatenate([ref[0, 0], ref[1, 0], ref[0, 1], ref[1, 1]], axis=0) for ref in (lsef_ref, lsef2_ref)
        ]
        far = jnp.where((lane >= 96) & (c == 5), two, one)
        far = jnp.where(valid(lane), far, NEG)
        far3 = split3(far)
        tall = iota((DIM, CHUNK), 0) + DIM
        parts, spread, chosen = [lse_ref[...]], [], []
        for level, (first, count, bits) in enumerate(REGIONS):
            if level > 0:
                hit = ((iota((DIM, CHUNK), 1) >> bits) == tall - first) & (tall >= first) & (tall < first + count)
                spread.append(jnp.where(hit, 1.0, 0.0).astype(BF16))
                chosen.append(picked(off_ref, level, bits))
                parts.append(jnp.where(chosen[-1], fold3(nn(far3, spread[-1])), NEG))
        lse = log_sum(parts)
        back = jnp.zeros((2 * HEADS, DIM), F32)
        for pick, wide in zip(chosen, spread):
            back = back + fold3(nt(split3(jnp.where(pick, lse, 0.0)), wide))
        al_far[...] = jnp.exp2(far - back)
        share = jnp.exp2(lse_ref[...] - lse)
        for b in range(2):
            a_loc[b * CHUNK : (b + 1) * CHUNK] = upright(share, b)

    row = lane + DIM
    first = jnp.where(row < 192, 128, jnp.where(row < 224, 192, 224))
    bits = jnp.where(row < 192, 2, jnp.where(row < 224, 3, 4))
    base = iota((CHUNK, DIM), 0) - ((row - first) << bits)
    sent = valid(iota((DIM, DIM), 0))
    for i in range(GROUP):
        h = pl.program_id(0) * GROUP + i
        o2, o3, o4 = [off_ref[level, h] & (2 << level) - 1 for level in (1, 2, 3)]
        hit = base == jnp.where(row < 192, o2, jnp.where(row < 224, o3, o4))
        for b in range(2):
            span = slice(b * CHUNK, (b + 1) * CHUNK)
            weight = jnp.where(hit, al_far[pl.ds(b * HEADS + h, 1), :], 0.0).astype(BF16)
            mixed = nn(weight, jnp.where(sent, far_ref[i, b], jnp.zeros((DIM, DIM), BF16)))
            scale = jnp.sum(jnp.where(lane == h, a_loc[span], 0.0), axis=1, keepdims=True)
            out_ref[0, span, i * DIM : (i + 1) * DIM] = (mixed + scale * loc_ref[i, span].astype(F32)).astype(BF16)


def on_device(queries, key_rows, value_rows, document_ids, dilation_offsets):
    any_space = pl.BlockSpec(memory_space=pl.ANY)
    smem = pl.BlockSpec(memory_space=pltpu.SMEM)
    dma = pltpu.SemaphoreType.DMA

    def vmem(*shape, kind=BF16):
        return pltpu.VMEM(shape, kind)

    local, far, lse, lse_far, lse_far2 = pl.pallas_call(
        kernel,
        out_shape=(
            jax.ShapeDtypeStruct((HEADS, ROWS, DIM), BF16),
            jax.ShapeDtypeStruct((HEADS, 2, DIM, DIM), BF16),
            jax.ShapeDtypeStruct((2 * HEADS, CHUNK), F32),
            jax.ShapeDtypeStruct((2, 2, HALF, DIM), F32),
            jax.ShapeDtypeStruct((2, 2, HALF, DIM), F32),
        ),
        in_specs=[any_space] * 5,
        out_specs=(any_space,) * 5,
        scratch_shapes=[
            vmem(1, ROWS, kind=I32), pltpu.SMEM((4, HEADS), I32), vmem(3, ROWS, HEADS * DIM),
            vmem(HALF, 3, 4, SEL, DIM), vmem(HALF, 3, 2, SEL, DIM), vmem(HALF, 4, FAR, DIM), vmem(HALF, 4, 16, DIM),
            vmem(HALF, 2, 4, FAR3, DIM),
            vmem(HALF, SEL, CHUNK), vmem(2, HALF, SEL, CHUNK), vmem(2, HALF, FAR3, CHUNK), vmem(HALF, SEL, CHUNK),
            vmem(2, HALF, 2, CHUNK, DIM), vmem(HALF, 2, CHUNK, DIM), vmem(2, HALF, 2, FAR, DIM), vmem(2, HALF, 2, 16, DIM),
            vmem(HEADS, ROWS, DIM, kind=F32), vmem(HEADS, ROWS, DIM),
            vmem(2, 2, CHUNK, DIM, kind=F32), vmem(2, 2, DIM, DIM, kind=F32), vmem(2, 2, DIM, DIM, kind=F32),
            vmem(ROWS, DIM, kind=F32),
            vmem(2, 2, HALF, CHUNK, kind=F32), vmem(2, 2, HALF, DIM, kind=F32), vmem(2, 2, HALF, DIM, kind=F32),
            vmem(2, HALF, CHUNK, kind=F32),
            vmem(2 * HEADS, CHUNK, kind=F32),
            vmem(8, 1, ROWS, kind=I32), vmem(2 * DIM, CHUNK), vmem(4, 2 * DIM, CHUNK),
            vmem(SEL, CHUNK, kind=I32), vmem(CHUNK, CHUNK, kind=F32), vmem(2, CHUNK, CHUNK, kind=F32),
            vmem(2 * HEADS, CHUNK, kind=F32), vmem(ROWS, DIM, kind=F32),
            dma((6,)), dma((17,)), dma((8,)), dma((HALF,)), dma((HALF,)), dma((HALF,)), dma((5,)),
        ],
        compiler_params=pltpu.CompilerParams(collective_id=0, has_side_effects=True, vmem_limit_bytes=56 << 20),
        name="dilated_attention",
    )(queries, key_rows, value_rows, document_ids, dilation_offsets)
    return pl.pallas_call(
        join_kernel,
        grid=(HEADS // GROUP,),
        out_shape=jax.ShapeDtypeStruct((1, ROWS, HEADS * DIM), BF16),
        in_specs=[
            pl.BlockSpec((GROUP, ROWS, DIM), lambda i: (i, 0, 0)),
            pl.BlockSpec((GROUP, 2, DIM, DIM), lambda i: (i, 0, 0, 0)),
            pl.BlockSpec(memory_space=pltpu.VMEM),
            pl.BlockSpec(memory_space=pltpu.VMEM),
            pl.BlockSpec(memory_space=pltpu.VMEM),
            smem,
        ],
        out_specs=pl.BlockSpec((1, ROWS, GROUP * DIM), lambda i: (0, 0, i)),
        scratch_shapes=[vmem(2 * HEADS, DIM, kind=F32), vmem(ROWS, DIM, kind=F32)],
        compiler_params=pltpu.CompilerParams(vmem_limit_bytes=60 << 20),
        name="join_far",
    )(local, far, lse, lse_far, lse_far2, dilation_offsets)


def solution(mesh):
    placed = (P("dp", "ctx", None), P("dp", "ctx", None), P("dp", "ctx", None), P("dp", "ctx"), P())
    return jax.shard_map(
        on_device, mesh=mesh, in_specs=placed, out_specs=P("dp", "ctx", None), check_vma=False
    )
```

```python
import math

import jax
import jax.numpy as jnp
from jax import lax
from jax.experimental import pallas as pl
from jax.experimental.pallas import tpu as pltpu
from jax.sharding import PartitionSpec as P

MESH = pl.DeviceIdType.MESH
F32, BF16, I32 = jnp.float32, jnp.bfloat16, jnp.int32
HEADS, HALF, ROWS, DIM, CHUNK = 16, 8, 512, 128, 256
SEL, FAR, FAR3 = 240, 112, 48
REGIONS = ((0, 128, 1), (128, 64, 2), (192, 32, 3), (224, 16, 4))
NEG = -1e30
SCALE2 = math.log2(math.e) / math.sqrt(DIM)


def nt(a, b):
    return lax.dot_general(a, b, (((1,), (1,)), ((), ())), preferred_element_type=F32)


def nn(a, b):
    return jnp.dot(a, b, preferred_element_type=F32)


def split3(x):
    first = x.astype(BF16)
    rest = x - first.astype(F32)
    second = rest.astype(BF16)
    third = (rest - second.astype(F32)).astype(BF16)
    return jnp.concatenate([first, second, third], axis=0)


def fold3(x):
    n = x.shape[0] // 3
    return (x[2 * n :] + x[n : 2 * n]) + x[:n]


def iota(shape, dim):
    return lax.broadcasted_iota(I32, shape, dim)


def attend(problems):
    scores = [nt(q, k) if bias is None else bias(nt(q, k)) for q, k, _, bias in problems]
    tops = [jnp.max(s, axis=1, keepdims=True) for s in scores]
    weights = [jnp.exp2((s - top) * SCALE2).astype(BF16) for s, top in zip(scores, tops)]
    sums = [nn(w, jnp.concatenate([v, jnp.ones_like(v)], axis=1)) for w, (_, _, v, _) in zip(weights, problems)]
    return [(x[:, :DIM] / x[:, DIM:], top * SCALE2 + jnp.log2(x[:, DIM:])) for x, top in zip(sums, tops)]


def far_pieces(chip):
    return (
        (chip % 4 == 3, ((0, FAR),)),
        (chip % 4 == 2, ((64, FAR),)),
        (chip % 4 == 1, ((0, 64),)),
        (chip == 4, ((96, FAR),)),
    )


def next_pieces(chip):
    return ((chip % 4 < 2, (0, FAR3)), (chip == 2, (32, FAR3)))


def kernel(
    q_hbm, k_hbm, v_hbm, docs_hbm, off_hbm,
    loc_out, far_out, al_out, share_out,
    docs_ref, off_ref, xv, cx, sx, q1in, q2in, kvp, dqs, dks, dps, pbuf,
    ob, oo_in, os1, os2, o0, loc,
    st_own, st1, st2, lse0, ls_own, ls1, ls2, lo_in, lr1, lr2, lse_loc,
    docs_all, ot_q, ot_k, base_m, causal, bias0, al_own, a0, al_far, share,
    load_sem, once, d_recv, x_recv, q_recv, k_recv, l_recv,
):
    me = lax.axis_index("ctx")
    dp = lax.axis_index("dp")
    c = me // 2
    j = me % 2

    def device(steps, core):
        return (dp, ((c + steps + 8) % 8) * 2 + core)

    def remote(src, dst, send, recv, to):
        return pltpu.make_async_remote_copy(
            src_ref=src, dst_ref=dst, send_sem=send, recv_sem=recv, device_id=to, device_id_type=MESH
        )

    store_sem, lse_sem, d_send, x_send, q_send, k_send, o_send, o_recv, oo_send, oo_recv, l_send, l_own_send, two_send, two_recv, o_two_send, o_two_recv, l_two_send, al_sem = [
        once.at[i] for i in range(18)
    ]

    near_chips = ((1, c <= 6), (-1, c >= 1))
    barrier = pltpu.get_barrier_semaphore()
    pl.semaphore_signal(barrier, inc=1, device_id=device(0, 1 - j), device_id_type=MESH)
    for g, present in near_chips:

        @pl.when(present)
        def _():
            for core in (0, 1):
                pl.semaphore_signal(barrier, inc=1, device_id=device(g, core), device_id_type=MESH)

    guest_of_two = ((c == 5, -2), (c == 3, 2))
    for present, g in guest_of_two:

        @pl.when(present)
        def _():
            for core in (0, 1):
                pl.semaphore_signal(barrier, inc=1, device_id=device(g, core), device_id_type=MESH)

    def load_start(u):
        for half in range(2):
            first = HALF * (1 - j) if half == 0 else HALF * j
            span = pl.ds(pl.multiple_of((first + 2 * u) * DIM, DIM), 2 * DIM)
            for i, src in enumerate((q_hbm, k_hbm, v_hbm)):
                pltpu.make_async_copy(src.at[0, :, span], xv.at[i, :, span], load_sem.at[u]).start()

    def load_wait(u):
        part = xv.at[:, :, pl.ds(0, 4 * DIM)]
        pltpu.make_async_copy(part, part, load_sem.at[u]).wait()

    docs_load = pltpu.make_async_copy(docs_hbm, docs_ref, load_sem.at[4])
    off_load = pltpu.make_async_copy(off_hbm, off_ref, load_sem.at[5])
    docs_load.start()
    off_load.start()
    for u in range(4):
        load_start(u)

    for first, count, bits in REGIONS:
        base_m[first : first + count] = iota((count, CHUNK), 1) - (iota((count, CHUNK), 0) << bits)

    docs_load.wait()
    off_load.wait()
    pl.semaphore_wait(barrier, 1 + jnp.where(c <= 6, 2, 0) + jnp.where(c >= 1, 2, 0) + jnp.where((c == 3) | (c == 5), 2, 0))

    def docs_copy(g, core, slot):
        return remote(docs_ref, docs_all.at[slot], d_send, d_recv.at[slot], device(g, core))

    def each_docs(do):
        do(docs_copy(0, 1 - j, j))
        for (g, present), first in zip(near_chips, (4, 2)):

            @pl.when(present)
            def _():
                for core in (0, 1):
                    do(docs_copy(g, core, first + j))

        @pl.when(c == 5)
        def _():
            for core in (0, 1):
                do(docs_copy(-2, core, 6 + j))

    each_docs(lambda copy: copy.start())
    docs_all[j] = docs_ref[...]

    def core_of(which):
        return 1 - j if which == 0 else j

    def q_copy(t, which, low, high):
        rows = pl.ds(128 + low, high - low)
        return remote(
            sx.at[t, 0, :, rows] if which == 0 else cx.at[t, 0, pl.ds(2 * j, 2), rows],
            q1in.at[t, pl.ds(2 * j, 2), pl.ds(low, high - low)],
            q_send, q_recv.at[t], device(-1, core_of(which)),
        )

    def kv_copy(t, which, low, high):
        rows = pl.ds(192 + low, high - low)
        return remote(
            sx.at[t, pl.ds(1, 2), :, rows] if which == 0 else cx.at[t, pl.ds(1, 2), pl.ds(2 * j, 2), rows],
            kvp.at[t, :, pl.ds(2 * j, 2), pl.ds(low, high - low)],
            k_send, k_recv.at[t], device(1, core_of(which)),
        )

    def two_copy(t, which):
        rows = pl.ds(224, 16)
        return remote(
            sx.at[t, 0, :, rows] if which == 0 else cx.at[t, 0, pl.ds(2 * j, 2), rows],
            q2in.at[t, pl.ds(2 * j, 2)], two_send, two_recv, device(-2, core_of(which)),
        )

    def each_q(t, which):
        @pl.when(c == 5)
        def _():
            two_copy(t, which).start()

        for present, pieces in far_pieces(c):

            @pl.when(present)
            def _():
                for low, high in pieces:
                    q_copy(t, which, low, high).start()

    def each_kv(t, which):
        for present, (low, high) in next_pieces(c):

            @pl.when(present)
            def _():
                kv_copy(t, which, low, high).start()

    def exchange(t):
        return remote(sx.at[t], cx.at[t, :, pl.ds(2 * j, 2)], x_send, x_recv.at[t], device(0, 1 - j))

    def size_of(pieces):
        return sum(high - low for low, high in pieces)

    def got(part, sem):
        remote(part, part, once.at[0], sem, device(0, 1 - j)).wait_recv()

    def sent(part, sem):
        remote(part, part, sem, once.at[0], device(0, 1 - j)).wait_send()

    def picker(h):
        parts = []
        for level, (first, count, bits) in enumerate(REGIONS):
            shift = off_ref[level, h] & ((1 << bits) - 1)
            parts.append(jnp.where(base_m[first : first + count] == shift, 1.0, 0.0))
        return jnp.concatenate(parts, axis=0).astype(BF16)

    def columns(i, h):
        return xv[i, :, pl.ds(pl.multiple_of(h * DIM, DIM), DIM)]

    def select(pick, i, h):
        x = columns(i, h)
        both = nn(pick, jnp.concatenate([x[:CHUNK], x[CHUNK:]], axis=1)).astype(BF16)
        return both[:, :DIM], both[:, DIM:]

    def select_head(t, _):
        @pl.when(t % 2 == 0)
        def _():
            load_wait(t // 2)

        for which in range(2):
            h = HALF * (1 - j) + t if which == 0 else HALF * j + t
            pick = picker(h)
            if which == 1:
                pbuf[t] = pick
            for i in range(3):
                for b, part in enumerate(select(pick, i, h)):
                    if which == 0:
                        sx[t, i, b] = part
                    else:
                        cx[t, i, 2 * j + b] = part
            each_q(t, which)
            each_kv(t, which)
            if which == 0:
                exchange(t).start()
        return 0

    lax.fori_loop(0, HALF, select_head, 0)

    def clear_pads(t, _):
        for b in range(2):
            oo_in[t, b, SEL:] = jnp.zeros((CHUNK - SEL, DIM), BF16)
            for d in range(2):
                ob[d, t, b, SEL:] = jnp.zeros((CHUNK - SEL, DIM), BF16)
        return 0

    lax.fori_loop(0, HALF, clear_pads, 0)

    causal[...] = jnp.where(iota((CHUNK, CHUNK), 1) <= iota((CHUNK, CHUNK), 0), 0.0, NEG)
    eye = jnp.where(iota((CHUNK, CHUNK), 1) == iota((CHUNK, CHUNK), 0), 1.0, 0.0).astype(BF16)
    for b in range(2):
        same = docs_ref[:, b * CHUNK : (b + 1) * CHUNK] == iota((DIM, CHUNK), 0)
        q_one = nt(eye, jnp.where(same, 1.0, 0.0).astype(BF16)).astype(BF16)
        k_one = nt(eye, jnp.where(same, 0.0, NEG).astype(BF16)).astype(BF16)
        bias0[b] = nt(q_one, k_one) + causal[...]

    docs_copy(0, 1 - j, 1 - j).wait_recv()
    for (g, present), first in zip(near_chips, (2, 4)):

        @pl.when(present)
        def _():
            for core in (0, 1):
                docs_copy(g, core, first + core).wait_recv()

        @pl.when(jnp.logical_not(present))
        def _():
            for core in (0, 1):
                docs_all[first + core] = docs_ref[...]

    @pl.when(c == 3)
    def _():
        for core in (0, 1):
            docs_copy(-2, core, 6 + core).wait_recv()

    @pl.when(c != 3)
    def _():
        for core in (0, 1):
            docs_all[6 + core] = docs_ref[...]

    for b in range(2):
        span = slice(b * CHUNK, (b + 1) * CHUNK)
        ones = [jnp.where(docs_all[g, :, span] == iota((8, CHUNK), 0), 1.0, 0.0) for g in (0, 1, 2, 3, 6, 7)]
        ones.append(jnp.zeros((DIM - 48, CHUNK), F32))
        ot_q[b * DIM : (b + 1) * DIM] = jnp.concatenate(ones, axis=0).astype(BF16)
        for i, slot in enumerate((0, 1, 4, 5)):
            same = docs_all[slot, :, span] == (iota((DIM, CHUNK), 0) & 7)
            ot_k[i, b * DIM : (b + 1) * DIM] = jnp.where(same, 0.0, NEG).astype(BF16)

    lane = iota((1, DIM), 1)

    def keep(ref, index, rows, t, value):
        old = ref[index + (rows,)]
        ref[index + (rows,)] = jnp.where(lane == t, value, old)

    def join(piece):
        return jnp.concatenate([piece(d, b) for d in range(2) for b in range(2)], axis=0)

    def with_docs(q, g, level, t):
        first, count, _ = REGIONS[level]

        def piece(d, b):
            mark = jnp.where((lane >> 3) == 2 * g + d, 1.0, 0.0).astype(BF16)
            return dqs[t, first : first + count, b * DIM : (b + 1) * DIM] * mark

        return jnp.concatenate([q, join(piece)], axis=1)

    def own_q(t, level):
        first, count, _ = REGIONS[level]
        return with_docs(join(lambda d, b: cx[t, 0, 2 * d + b, first : first + count]), 0, level, t)

    def guest_q(t, level):
        first, count, _ = REGIONS[level]
        return with_docs(join(lambda d, b: q1in[t, 2 * d + b, first - 128 : first - 128 + count]), 1, level, t)

    def own_kv(t, level):
        first, count, _ = REGIONS[level]
        span = slice(first, first + count)
        k = join(lambda d, b: cx[t, 1, 2 * d + b, span])
        kd = join(lambda d, b: dks[d, t, span, b * DIM : (b + 1) * DIM])
        return jnp.concatenate([k, kd], axis=1), join(lambda d, b: cx[t, 2, 2 * d + b, span])

    def both_kv(t, level):
        first, count, _ = REGIONS[level]
        span = slice(first - 192, first - 192 + count)
        k = join(lambda d, b: kvp[t, 0, 2 * d + b, span])
        kd = join(lambda d, b: dps[d, t, span, b * DIM : (b + 1) * DIM])
        v = join(lambda d, b: kvp[t, 1, 2 * d + b, span])
        own_k, own_v = own_kv(t, level)
        return (
            jnp.concatenate([own_k, jnp.concatenate([k, kd], axis=1)], axis=0),
            jnp.concatenate([own_v, v], axis=0),
        )

    def put(t, level, result, out, stats, shift):
        o, lse = result
        first, count, _ = REGIONS[level]
        spot = slice(first - shift, first - shift + count)
        for d in range(2):
            for b in range(2):
                rows = slice((2 * d + b) * count, (2 * d + b + 1) * count)
                out[d, t, b, spot] = o[rows].astype(BF16)
                keep(stats, (d, b), spot, t, lse[rows])

    def near(n):
        return lambda s: s + causal[:n, :n]

    def near_half(n):
        def bias(s):
            return jnp.concatenate([s[:, :n] + causal[:n, :n], s[:, n:]], axis=1)

        return bias

    def partner_out(t):
        return remote(
            ob.at[1 - j, t, :, pl.ds(0, SEL)], oo_in.at[t, :, pl.ds(0, SEL)],
            oo_send, oo_recv, device(0, 1 - j),
        )

    def ret_copy(t, low, high, d):
        return remote(
            os1.at[d, t, :, pl.ds(low, high - low)], far_out.at[HALF * j + t, :, pl.ds(low, high - low)],
            o_send, o_recv, device(1, d),
        )

    plans = (
        (c % 4 == 0, "2", ""),
        (c % 4 == 1, "34", "34"),
        (c % 4 == 2, "234", ""),
        (c == 3, "4", ""),
    )

    def each_return(t, more):
        for present, pieces in far_pieces(c + 1):

            @pl.when(present & (c <= 6) & more)
            def _():
                for low, high in pieces:
                    for d in range(2):
                        ret_copy(t, low, high, d).start()

    def level_head(t, _):
        exchange(t).wait_recv()
        pick = pbuf[t]
        dqs[t] = nt(pick, ot_q[...]).astype(BF16)
        for d in range(2):
            dks[d, t] = nt(pick, ot_k[d]).astype(BF16)
            dps[d, t] = nt(pick[192:], ot_k[2 + d]).astype(BF16)

        problems = []
        q = own_q(t, 0)
        k, v = own_kv(t, 0)
        problems.append((q[:CHUNK], k[:CHUNK], v[:CHUNK], near(CHUNK)))
        late = lambda s: jnp.concatenate([s[:, :CHUNK], s[:, CHUNK:] + causal[...]], axis=1)
        problems.append((q[CHUNK:], k, v, late))
        for level in (1, 2, 3):
            problems.append((own_q(t, level),) + own_kv(t, level) + (near(4 * REGIONS[level][1]),))
        for h in (2 * t, 2 * t + 1):
            q, k, v = columns(0, h), columns(1, h), columns(2, h)
            for b in range(2):
                span = slice(b * CHUNK, (b + 1) * CHUNK)
                problems.append((q[span], k[span], v[span], lambda s, b=b: s + bias0[b]))
        results = attend(problems)
        first = tuple(jnp.concatenate(pair, axis=0) for pair in zip(results[0], results[1]))
        for level, result in enumerate([first] + results[2:5]):
            put(t, level, result, ob, st_own, 0)
        for i in range(2):
            for b in range(2):
                span = slice(b * CHUNK, (b + 1) * CHUNK)
                o, lse = results[5 + 2 * i + b]
                o0[2 * t + i, span] = o
                keep(lse0, (), span, 2 * t + i, lse)

        for present, (low, high) in next_pieces(c - 1):

            @pl.when(present & (c >= 1))
            def _():
                got(kvp.at[t, :, :, pl.ds(low, high - low)], k_recv.at[t])

        for present, pieces in far_pieces(c + 1):

            @pl.when(present & (c <= 6))
            def _():
                got(q1in.at[t, :, pl.ds(0, size_of(pieces))], q_recv.at[t])

        for present, guests, owns in plans:

            @pl.when(present)
            def _():
                problems = []
                for name in guests:
                    level = int(name) - 1
                    kv_pair = own_kv(t, level) if level == 1 else both_kv(t, level)
                    problems.append((guest_q(t, level),) + kv_pair + (None,))
                for name in owns:
                    level = int(name) - 1
                    n = 4 * REGIONS[level][1]
                    problems.append((own_q(t, level),) + both_kv(t, level) + (near_half(n),))
                results = attend(problems)
                for name, result in zip(guests, results):
                    put(t, int(name) - 1, result, os1, st1, 128)
                for name, result in zip(owns, results[len(guests) :]):
                    put(t, int(name) - 1, result, ob, st_own, 0)

        each_return(t, t < HALF - jnp.where(c % 4 == 0, 3, 1))
        partner_out(t).start()
        return 0

    lax.fori_loop(0, HALF, level_head, 0)

    for d in range(2):
        for b in range(2):
            ls1[d, b] = st1[d, b].T[:HALF]
            ls_own[d, b] = st_own[d, b].T[:HALF]

    def far_stats(d):
        return remote(ls1.at[d], lr1.at[j], l_send, l_recv.at[1 + j], device(1, d))

    @pl.when(c <= 6)
    def _():
        for d in range(2):
            far_stats(d).start()

    each_return(HALF - 3, c % 4 == 0)
    each_return(HALF - 2, c % 4 == 0)
    each_return(HALF - 1, True)

    def two_back(d):
        return remote(
            os2.at[d], far_out.at[pl.ds(pl.multiple_of(HALF * j, HALF), HALF), :, pl.ds(96, 16)],
            o_two_send, o_two_recv, device(2, d),
        )

    def two_stats(d):
        return remote(ls2.at[d], lr2.at[j], l_two_send, l_recv.at[3 + j], device(2, d))

    @pl.when(c == 3)
    def _():
        got(q2in, two_recv)
        problems = []
        for t in range(HALF):
            q = with_docs(join(lambda d, b: q2in[t, 2 * d + b]), 2, 3, t)
            problems.append((q,) + own_kv(t, 3) + (None,))
        for t, (o, lse) in enumerate(attend(problems)):
            for d in range(2):
                for b in range(2):
                    rows = slice((2 * d + b) * 16, (2 * d + b + 1) * 16)
                    os2[d, t, b] = o[rows].astype(BF16)
                    keep(st2, (d, b), slice(96, FAR), t, lse[rows])
        for d in range(2):
            for b in range(2):
                ls2[d, b] = st2[d, b].T[:HALF]
        for d in range(2):
            two_stats(d).start()
        for d in range(2):
            two_back(d).start()

    l_own = remote(ls_own.at[1 - j], lo_in, l_own_send, l_recv.at[0], device(0, 1 - j))
    l_own.start()
    l_own.wait_recv()

    mine = ls_own[j]
    theirs = lo_in[...]
    lower = jnp.where(j == 0, mine, theirs)
    upper = jnp.where(j == 0, theirs, mine)
    wide = iota((1, CHUNK), 1)
    own = jnp.concatenate([lower[0], upper[0], lower[1], upper[1]], axis=0)
    own = jnp.where(wide < SEL, own, NEG)
    tall = iota((CHUNK, CHUNK), 0)
    own3 = split3(own)
    zeroth = lse0[...].T
    parts = [jnp.concatenate([zeroth[:HEADS, :CHUNK], zeroth[:HEADS, CHUNK:]], axis=0)]
    spread, chosen = [], []
    for level, (first, count, bits) in enumerate(REGIONS):
        hit = ((iota((CHUNK, CHUNK), 1) >> bits) == tall - first) & (tall >= first) & (tall < first + count)
        spread.append(jnp.where(hit, 1.0, 0.0).astype(BF16))
        chosen.append(picked(off_ref, level, bits))
        parts.append(jnp.where(chosen[level], fold3(nn(own3, spread[level])), NEG))
    lse = log_sum(parts)
    back = jnp.zeros((2 * HEADS, CHUNK), F32)
    for level in range(4):
        back = back + fold3(nt(split3(jnp.where(chosen[level], lse, 0.0)), spread[level]))
    al_own[...] = jnp.exp2(own - back)
    lse_loc[...] = lse
    for b in range(2):
        span = slice(b * CHUNK, (b + 1) * CHUNK)
        a0[span] = jnp.exp2(lse0[span] - upright(lse, b))

    def loc_copy(h):
        return pltpu.make_async_copy(loc.at[h], loc_out.at[h], store_sem)

    own_first = jnp.where(wide < 128, 0, jnp.where(wide < 192, 128, jnp.where(wide < 224, 192, 224)))
    own_bits = jnp.where(wide < 128, 1, jnp.where(wide < 192, 2, jnp.where(wide < 224, 3, 4)))
    own_base = tall - ((wide - own_first) << own_bits)

    got(oo_in.at[:, :, pl.ds(0, SEL)], oo_recv)

    def local_head(t, _):
        for which in range(2):
            h = HALF * j + t if which == 0 else HALF * (1 - j) + t
            o1, o2, o3, o4 = [off_ref[i, h] & (2 << i) - 1 for i in range(4)]
            shift = jnp.where(wide < 128, o1, jnp.where(wide < 192, o2, jnp.where(wide < 224, o3, o4)))
            hit = own_base == shift
            for b in range(2):
                span = slice(b * CHUNK, (b + 1) * CHUNK)
                weight = jnp.where(hit, al_own[pl.ds(b * HEADS + h, 1), :], 0.0).astype(BF16)
                mixed = nn(weight, ob[j, t, b] if which == 0 else oo_in[t, b])
                scale = jnp.sum(jnp.where(lane == h, a0[span], 0.0), axis=1, keepdims=True)
                loc[h, span] = (mixed + scale * o0[h, span]).astype(BF16)
            loc_copy(h).start()
        return 0

    lax.fori_loop(0, HALF, local_head, 0)

    @pl.when(c >= 1)
    def _():
        for i in range(2):
            got(lr1.at[i], l_recv.at[1 + i])

    @pl.when(c == 5)
    def _():
        for i in range(2):
            got(lr2.at[i], l_recv.at[3 + i])

    one, two = [
        jnp.concatenate([ref[0, 0], ref[1, 0], ref[0, 1], ref[1, 1]], axis=0) for ref in (lr1, lr2)
    ]
    far = jnp.where((lane >= 96) & (c == 5), two, one)
    far = jnp.where(valid_row(lane, c), far, NEG)
    far3 = split3(far)
    tall = iota((DIM, CHUNK), 0) + DIM
    parts, spread, chosen = [lse_loc[...]], [], []
    for level, (first, count, bits) in enumerate(REGIONS):
        if level > 0:
            hit = ((iota((DIM, CHUNK), 1) >> bits) == tall - first) & (tall >= first) & (tall < first + count)
            spread.append(jnp.where(hit, 1.0, 0.0).astype(BF16))
            chosen.append(picked(off_ref, level, bits))
            parts.append(jnp.where(chosen[-1], fold3(nn(far3, spread[-1])), NEG))
    lse = log_sum(parts)
    back = jnp.zeros((2 * HEADS, DIM), F32)
    for pick, wide in zip(chosen, spread):
        back = back + fold3(nt(split3(jnp.where(pick, lse, 0.0)), wide))
    al_far[...] = jnp.exp2(far - back)
    portion = jnp.exp2(lse_loc[...] - lse)
    for b in range(2):
        share[b * CHUNK : (b + 1) * CHUNK] = upright(portion, b)
    al_copy = pltpu.make_async_copy(al_far, al_out, al_sem)
    share_copy = pltpu.make_async_copy(share, share_out, lse_sem)
    al_copy.start()
    share_copy.start()

    for present, slots in (((c > 0) & (c < 7) & (c != 5), 5), ((c == 0) | (c == 7), 3), (c == 5, 7)):

        @pl.when(present)
        def _():
            part = docs_all.at[pl.ds(0, slots)]
            remote(part, part, d_send, d_recv.at[0], device(0, 1 - j)).wait_send()

    l_own.wait_send()

    al_copy.wait()
    share_copy.wait()
    sent(sx, x_send)
    sent(oo_in.at[:, :, pl.ds(0, SEL)], oo_send)
    pltpu.make_async_copy(loc, loc_out, store_sem).wait()
    for present, pieces in far_pieces(c):

        @pl.when(present)
        def _():
            sent(q1in.at[:, :, pl.ds(0, size_of(pieces))], q_send)

    for present, (low, high) in next_pieces(c):

        @pl.when(present)
        def _():
            sent(kvp.at[:, :, :, pl.ds(0, high - low)], k_send)

    for present, pieces in far_pieces(c + 1):

        @pl.when(present & (c <= 6))
        def _():
            sent(os1.at[:, :, :, pl.ds(0, size_of(pieces))], o_send)
            sent(ls1, l_send)

    @pl.when(c == 3)
    def _():
        sent(os2, o_two_send)
        sent(ls2, l_two_send)

    @pl.when(c == 5)
    def _():
        sent(q2in, two_send)
        got(far_out.at[:, :, pl.ds(0, 16)], o_two_recv)

    for present, pieces in far_pieces(c):

        @pl.when(present)
        def _():
            got(far_out.at[:, :, pl.ds(0, size_of(pieces))], o_recv)


def valid_row(x, c):
    return ((x < 64) & (c % 2 == 1)) | ((x >= 64) & (x < 96) & (c % 4 >= 2)) | ((x >= 96) & (x < FAR) & (c >= 2))


def picked(off_ref, level, bits):
    head = iota((HEADS, CHUNK), 0)
    shifts = jnp.zeros((HEADS, CHUNK), I32)
    for h in range(HEADS):
        shifts = jnp.where(head == h, off_ref[level, h] & ((1 << bits) - 1), shifts)
    pick = (iota((HEADS, CHUNK), 1) & ((1 << bits) - 1)) == shifts
    return jnp.concatenate([pick, pick], axis=0)


def log_sum(parts):
    top = parts[0]
    for part in parts[1:]:
        top = jnp.maximum(top, part)
    total = jnp.exp2(parts[0] - top)
    for part in parts[1:]:
        total = total + jnp.exp2(part - top)
    return top + jnp.log2(total)


def upright(dense, b):
    pad = jnp.zeros((DIM - HEADS, CHUNK), F32)
    return jnp.concatenate([dense[b * HEADS : (b + 1) * HEADS], pad], axis=0).T


GROUP = 8


def join_kernel(loc_ref, far_ref, al_far, a_loc, off_ref, out_ref):
    c = lax.axis_index("ctx") // 2
    lane = iota((1, DIM), 1)

    sent = valid_row(iota((DIM, DIM), 0), c)
    row = lane + DIM
    first = jnp.where(row < 192, 128, jnp.where(row < 224, 192, 224))
    bits = jnp.where(row < 192, 2, jnp.where(row < 224, 3, 4))
    base = iota((CHUNK, DIM), 0) - ((row - first) << bits)
    for i in range(GROUP):
        h = pl.program_id(0) * GROUP + i
        o2, o3, o4 = [off_ref[level, h] & (2 << level) - 1 for level in (1, 2, 3)]
        hit = base == jnp.where(row < 192, o2, jnp.where(row < 224, o3, o4))
        for b in range(2):
            span = slice(b * CHUNK, (b + 1) * CHUNK)
            weight = jnp.where(hit, al_far[pl.ds(b * HEADS + h, 1), :], 0.0).astype(BF16)
            mixed = nn(weight, jnp.where(sent, far_ref[i, b], jnp.zeros((DIM, DIM), BF16)))
            scale = jnp.sum(jnp.where(lane == h, a_loc[span], 0.0), axis=1, keepdims=True)
            out_ref[0, span, i * DIM : (i + 1) * DIM] = (mixed + scale * loc_ref[i, span].astype(F32)).astype(BF16)


def on_device(queries, key_rows, value_rows, document_ids, dilation_offsets):
    any_space = pl.BlockSpec(memory_space=pl.ANY)
    smem = pl.BlockSpec(memory_space=pltpu.SMEM)
    dma = pltpu.SemaphoreType.DMA

    def vmem(*shape, kind=BF16):
        return pltpu.VMEM(shape, kind)

    local, far, far_share, local_share = pl.pallas_call(
        kernel,
        out_shape=(
            jax.ShapeDtypeStruct((HEADS, ROWS, DIM), BF16),
            jax.ShapeDtypeStruct((HEADS, 2, DIM, DIM), BF16),
            jax.ShapeDtypeStruct((2 * HEADS, DIM), F32),
            jax.ShapeDtypeStruct((ROWS, DIM), F32),
        ),
        in_specs=[any_space] * 5,
        out_specs=(any_space,) * 4,
        scratch_shapes=[
            vmem(1, ROWS, kind=I32), pltpu.SMEM((4, HEADS), I32), vmem(3, ROWS, HEADS * DIM),
            vmem(HALF, 3, 4, SEL, DIM), vmem(HALF, 3, 2, SEL, DIM), vmem(HALF, 4, FAR, DIM), vmem(HALF, 4, 16, DIM),
            vmem(HALF, 2, 4, FAR3, DIM),
            vmem(HALF, SEL, CHUNK), vmem(2, HALF, SEL, CHUNK), vmem(2, HALF, FAR3, CHUNK), vmem(HALF, SEL, CHUNK),
            vmem(2, HALF, 2, CHUNK, DIM), vmem(HALF, 2, CHUNK, DIM), vmem(2, HALF, 2, FAR, DIM), vmem(2, HALF, 2, 16, DIM),
            vmem(HEADS, ROWS, DIM, kind=F32), vmem(HEADS, ROWS, DIM),
            vmem(2, 2, CHUNK, DIM, kind=F32), vmem(2, 2, DIM, DIM, kind=F32), vmem(2, 2, DIM, DIM, kind=F32),
            vmem(ROWS, DIM, kind=F32),
            vmem(2, 2, HALF, CHUNK, kind=F32), vmem(2, 2, HALF, DIM, kind=F32), vmem(2, 2, HALF, DIM, kind=F32),
            vmem(2, HALF, CHUNK, kind=F32), vmem(2, 2, HALF, DIM, kind=F32), vmem(2, 2, HALF, DIM, kind=F32),
            vmem(2 * HEADS, CHUNK, kind=F32),
            vmem(8, 1, ROWS, kind=I32), vmem(2 * DIM, CHUNK), vmem(4, 2 * DIM, CHUNK),
            vmem(SEL, CHUNK, kind=I32), vmem(CHUNK, CHUNK, kind=F32), vmem(2, CHUNK, CHUNK, kind=F32),
            vmem(2 * HEADS, CHUNK, kind=F32), vmem(ROWS, DIM, kind=F32),
            vmem(2 * HEADS, DIM, kind=F32), vmem(ROWS, DIM, kind=F32),
            dma((6,)), dma((18,)), dma((8,)), dma((HALF,)), dma((HALF,)), dma((HALF,)), dma((5,)),
        ],
        compiler_params=pltpu.CompilerParams(collective_id=0, has_side_effects=True, vmem_limit_bytes=56 << 20),
        name="dilated_attention",
    )(queries, key_rows, value_rows, document_ids, dilation_offsets)
    return pl.pallas_call(
        join_kernel,
        grid=(HEADS // GROUP,),
        out_shape=jax.ShapeDtypeStruct((1, ROWS, HEADS * DIM), BF16),
        in_specs=[
            pl.BlockSpec((GROUP, ROWS, DIM), lambda i: (i, 0, 0)),
            pl.BlockSpec((GROUP, 2, DIM, DIM), lambda i: (i, 0, 0, 0)),
            pl.BlockSpec(memory_space=pltpu.VMEM),
            pl.BlockSpec(memory_space=pltpu.VMEM),
            smem,
        ],
        out_specs=pl.BlockSpec((1, ROWS, GROUP * DIM), lambda i: (0, 0, i)),
        compiler_params=pltpu.CompilerParams(vmem_limit_bytes=60 << 20),
        name="join_far",
    )(local, far, far_share, local_share, dilation_offsets)


def solution(mesh):
    placed = (P("dp", "ctx", None), P("dp", "ctx", None), P("dp", "ctx", None), P("dp", "ctx"), P())
    return jax.shard_map(
        on_device, mesh=mesh, in_specs=placed, out_specs=P("dp", "ctx", None), check_vma=False
    )
```

```python
import math

import jax
import jax.numpy as jnp
from jax import lax
from jax.experimental import pallas as pl
from jax.experimental.pallas import tpu as pltpu
from jax.sharding import PartitionSpec as P

MESH = pl.DeviceIdType.MESH
F32, BF16, I32 = jnp.float32, jnp.bfloat16, jnp.int32
HEADS, HALF, ROWS, DIM, CHUNK = 16, 8, 512, 128, 256
SEL, FAR, FAR3 = 240, 112, 48
REGIONS = ((0, 128, 1), (128, 64, 2), (192, 32, 3), (224, 16, 4))
NEG = -1e30
SCALE2 = math.log2(math.e) / math.sqrt(DIM)


def nt(a, b):
    return lax.dot_general(a, b, (((1,), (1,)), ((), ())), preferred_element_type=F32)


def nn(a, b):
    return jnp.dot(a, b, preferred_element_type=F32)


def split3(x):
    first = x.astype(BF16)
    rest = x - first.astype(F32)
    second = rest.astype(BF16)
    third = (rest - second.astype(F32)).astype(BF16)
    return jnp.concatenate([first, second, third], axis=0)


def fold3(x):
    n = x.shape[0] // 3
    return (x[2 * n :] + x[n : 2 * n]) + x[:n]


def iota(shape, dim):
    return lax.broadcasted_iota(I32, shape, dim)


def attend(problems):
    scores = [nt(q, k) if bias is None else bias(nt(q, k)) for q, k, _, bias in problems]
    tops = [jnp.max(s, axis=1, keepdims=True) for s in scores]
    weights = [jnp.exp2((s - top) * SCALE2).astype(BF16) for s, top in zip(scores, tops)]
    sums = [nn(w, jnp.concatenate([v, jnp.ones_like(v)], axis=1)) for w, (_, _, v, _) in zip(weights, problems)]
    return [(x[:, :DIM] / x[:, DIM:], top * SCALE2 + jnp.log2(x[:, DIM:])) for x, top in zip(sums, tops)]


def far_pieces(chip):
    return (
        (chip % 4 == 3, ((0, FAR),)),
        (chip % 4 == 2, ((64, FAR),)),
        (chip % 4 == 1, ((0, 64),)),
        (chip == 4, ((96, FAR),)),
    )


def next_pieces(chip):
    return ((chip % 4 < 2, (0, FAR3)), (chip == 2, (32, FAR3)))


def kernel(
    q_hbm, k_hbm, v_hbm, docs_hbm, off_hbm,
    loc_out, far_out, al_out, share_out,
    docs_ref, off_ref, xv, cx, sx, q1in, q2in, kvp, dqs, dks, dps, pbuf,
    ob, oo_in, os1, os2, o0, loc,
    st_own, st1, st2, lse0, ls_own, ls1, ls2, lo_in, lr1, lr2, lse_loc,
    docs_all, ot_q, ot_k, base_m, causal, bias0, al_own, a0, al_far, share,
    load_sem, once, d_recv, x_recv, q_recv, k_recv, l_recv,
):
    me = lax.axis_index("ctx")
    dp = lax.axis_index("dp")
    c = me // 2
    j = me % 2

    def device(steps, core):
        return (dp, ((c + steps + 8) % 8) * 2 + core)

    def remote(src, dst, send, recv, to):
        return pltpu.make_async_remote_copy(
            src_ref=src, dst_ref=dst, send_sem=send, recv_sem=recv, device_id=to, device_id_type=MESH
        )

    store_sem, lse_sem, d_send, x_send, q_send, k_send, o_send, o_recv, oo_send, oo_recv, l_send, l_own_send, two_send, two_recv, o_two_send, o_two_recv, l_two_send, al_sem = [
        once.at[i] for i in range(18)
    ]

    near_chips = ((1, c <= 6), (-1, c >= 1))
    barrier = pltpu.get_barrier_semaphore()
    pl.semaphore_signal(barrier, inc=1, device_id=device(0, 1 - j), device_id_type=MESH)
    for g, present in near_chips:

        @pl.when(present)
        def _():
            for core in (0, 1):
                pl.semaphore_signal(barrier, inc=1, device_id=device(g, core), device_id_type=MESH)

    guest_of_two = ((c == 5, -2), (c == 3, 2))
    for present, g in guest_of_two:

        @pl.when(present)
        def _():
            for core in (0, 1):
                pl.semaphore_signal(barrier, inc=1, device_id=device(g, core), device_id_type=MESH)

    def load_start(u):
        for half in range(2):
            first = HALF * (1 - j) if half == 0 else HALF * j
            span = pl.ds(pl.multiple_of((first + 2 * u) * DIM, DIM), 2 * DIM)
            for i, src in enumerate((q_hbm, k_hbm, v_hbm)):
                pltpu.make_async_copy(src.at[0, :, span], xv.at[i, :, span], load_sem.at[u]).start()

    def load_wait(u):
        part = xv.at[:, :, pl.ds(0, 4 * DIM)]
        pltpu.make_async_copy(part, part, load_sem.at[u]).wait()

    docs_load = pltpu.make_async_copy(docs_hbm, docs_ref, load_sem.at[4])
    off_load = pltpu.make_async_copy(off_hbm, off_ref, load_sem.at[5])
    docs_load.start()
    off_load.start()
    for u in range(4):
        load_start(u)

    for first, count, bits in REGIONS:
        base_m[first : first + count] = iota((count, CHUNK), 1) - (iota((count, CHUNK), 0) << bits)

    docs_load.wait()
    off_load.wait()
    pl.semaphore_wait(barrier, 1 + jnp.where(c <= 6, 2, 0) + jnp.where(c >= 1, 2, 0) + jnp.where((c == 3) | (c == 5), 2, 0))

    def docs_copy(g, core, slot):
        return remote(docs_ref, docs_all.at[slot], d_send, d_recv.at[slot], device(g, core))

    def each_docs(do):
        do(docs_copy(0, 1 - j, j))
        for (g, present), first in zip(near_chips, (4, 2)):

            @pl.when(present)
            def _():
                for core in (0, 1):
                    do(docs_copy(g, core, first + j))

        @pl.when(c == 5)
        def _():
            for core in (0, 1):
                do(docs_copy(-2, core, 6 + j))

    each_docs(lambda copy: copy.start())
    docs_all[j] = docs_ref[...]

    def core_of(which):
        return 1 - j if which == 0 else j

    def q_copy(t, which, low, high):
        rows = pl.ds(128 + low, high - low)
        return remote(
            sx.at[t, 0, :, rows] if which == 0 else cx.at[t, 0, pl.ds(2 * j, 2), rows],
            q1in.at[t, pl.ds(2 * j, 2), pl.ds(low, high - low)],
            q_send, q_recv.at[t], device(-1, core_of(which)),
        )

    def kv_copy(t, which, low, high):
        rows = pl.ds(192 + low, high - low)
        return remote(
            sx.at[t, pl.ds(1, 2), :, rows] if which == 0 else cx.at[t, pl.ds(1, 2), pl.ds(2 * j, 2), rows],
            kvp.at[t, :, pl.ds(2 * j, 2), pl.ds(low, high - low)],
            k_send, k_recv.at[t], device(1, core_of(which)),
        )

    def two_copy(t, which):
        rows = pl.ds(224, 16)
        return remote(
            sx.at[t, 0, :, rows] if which == 0 else cx.at[t, 0, pl.ds(2 * j, 2), rows],
            q2in.at[t, pl.ds(2 * j, 2)], two_send, two_recv, device(-2, core_of(which)),
        )

    def each_q(t, which):
        @pl.when(c == 5)
        def _():
            two_copy(t, which).start()

        for present, pieces in far_pieces(c):

            @pl.when(present)
            def _():
                for low, high in pieces:
                    q_copy(t, which, low, high).start()

    def each_kv(t, which):
        for present, (low, high) in next_pieces(c):

            @pl.when(present)
            def _():
                kv_copy(t, which, low, high).start()

    def exchange(t):
        return remote(sx.at[t], cx.at[t, :, pl.ds(2 * j, 2)], x_send, x_recv.at[t], device(0, 1 - j))

    def size_of(pieces):
        return sum(high - low for low, high in pieces)

    def got(part, sem):
        remote(part, part, once.at[0], sem, device(0, 1 - j)).wait_recv()

    def sent(part, sem):
        remote(part, part, sem, once.at[0], device(0, 1 - j)).wait_send()

    def picker(h):
        parts = []
        for level, (first, count, bits) in enumerate(REGIONS):
            shift = off_ref[level, h] & ((1 << bits) - 1)
            parts.append(jnp.where(base_m[first : first + count] == shift, 1.0, 0.0))
        return jnp.concatenate(parts, axis=0).astype(BF16)

    def columns(i, h):
        return xv[i, :, pl.ds(pl.multiple_of(h * DIM, DIM), DIM)]

    def select(pick, i, h):
        x = columns(i, h)
        both = nn(pick, jnp.concatenate([x[:CHUNK], x[CHUNK:]], axis=1)).astype(BF16)
        return both[:, :DIM], both[:, DIM:]

    def select_head(t, _):
        @pl.when(t % 2 == 0)
        def _():
            load_wait(t // 2)

        for which in range(2):
            h = HALF * (1 - j) + t if which == 0 else HALF * j + t
            pick = picker(h)
            if which == 1:
                pbuf[t] = pick
            for i in range(3):
                for b, part in enumerate(select(pick, i, h)):
                    if which == 0:
                        sx[t, i, b] = part
                    else:
                        cx[t, i, 2 * j + b] = part
            each_q(t, which)
            each_kv(t, which)
            if which == 0:
                exchange(t).start()
        return 0

    lax.fori_loop(0, HALF, select_head, 0)

    def clear_pads(t, _):
        for b in range(2):
            oo_in[t, b, SEL:] = jnp.zeros((CHUNK - SEL, DIM), BF16)
            for d in range(2):
                ob[d, t, b, SEL:] = jnp.zeros((CHUNK - SEL, DIM), BF16)
        return 0

    lax.fori_loop(0, HALF, clear_pads, 0)

    causal[...] = jnp.where(iota((CHUNK, CHUNK), 1) <= iota((CHUNK, CHUNK), 0), 0.0, NEG)
    eye = jnp.where(iota((CHUNK, CHUNK), 1) == iota((CHUNK, CHUNK), 0), 1.0, 0.0).astype(BF16)
    for b in range(2):
        same = docs_ref[:, b * CHUNK : (b + 1) * CHUNK] == iota((DIM, CHUNK), 0)
        q_one = nt(eye, jnp.where(same, 1.0, 0.0).astype(BF16)).astype(BF16)
        k_one = nt(eye, jnp.where(same, 0.0, NEG).astype(BF16)).astype(BF16)
        bias0[b] = nt(q_one, k_one) + causal[...]

    docs_copy(0, 1 - j, 1 - j).wait_recv()
    for (g, present), first in zip(near_chips, (2, 4)):

        @pl.when(present)
        def _():
            for core in (0, 1):
                docs_copy(g, core, first + core).wait_recv()

        @pl.when(jnp.logical_not(present))
        def _():
            for core in (0, 1):
                docs_all[first + core] = docs_ref[...]

    @pl.when(c == 3)
    def _():
        for core in (0, 1):
            docs_copy(-2, core, 6 + core).wait_recv()

    @pl.when(c != 3)
    def _():
        for core in (0, 1):
            docs_all[6 + core] = docs_ref[...]

    for b in range(2):
        span = slice(b * CHUNK, (b + 1) * CHUNK)
        ones = [jnp.where(docs_all[g, :, span] == iota((8, CHUNK), 0), 1.0, 0.0) for g in (0, 1, 2, 3, 6, 7)]
        ones.append(jnp.zeros((DIM - 48, CHUNK), F32))
        ot_q[b * DIM : (b + 1) * DIM] = jnp.concatenate(ones, axis=0).astype(BF16)
        for i, slot in enumerate((0, 1, 4, 5)):
            same = docs_all[slot, :, span] == (iota((DIM, CHUNK), 0) & 7)
            ot_k[i, b * DIM : (b + 1) * DIM] = jnp.where(same, 0.0, NEG).astype(BF16)

    lane = iota((1, DIM), 1)

    def keep(ref, index, rows, t, value):
        old = ref[index + (rows,)]
        ref[index + (rows,)] = jnp.where(lane == t, value, old)

    def join(piece):
        return jnp.concatenate([piece(d, b) for d in range(2) for b in range(2)], axis=0)

    def with_docs(q, g, level, t):
        first, count, _ = REGIONS[level]

        def piece(d, b):
            mark = jnp.where((lane >> 3) == 2 * g + d, 1.0, 0.0).astype(BF16)
            return dqs[t, first : first + count, b * DIM : (b + 1) * DIM] * mark

        return jnp.concatenate([q, join(piece)], axis=1)

    def own_q(t, level):
        first, count, _ = REGIONS[level]
        return with_docs(join(lambda d, b: cx[t, 0, 2 * d + b, first : first + count]), 0, level, t)

    def guest_q(t, level):
        first, count, _ = REGIONS[level]
        return with_docs(join(lambda d, b: q1in[t, 2 * d + b, first - 128 : first - 128 + count]), 1, level, t)

    def own_kv(t, level):
        first, count, _ = REGIONS[level]
        span = slice(first, first + count)
        k = join(lambda d, b: cx[t, 1, 2 * d + b, span])
        kd = join(lambda d, b: dks[d, t, span, b * DIM : (b + 1) * DIM])
        return jnp.concatenate([k, kd], axis=1), join(lambda d, b: cx[t, 2, 2 * d + b, span])

    def both_kv(t, level):
        first, count, _ = REGIONS[level]
        span = slice(first - 192, first - 192 + count)
        k = join(lambda d, b: kvp[t, 0, 2 * d + b, span])
        kd = join(lambda d, b: dps[d, t, span, b * DIM : (b + 1) * DIM])
        v = join(lambda d, b: kvp[t, 1, 2 * d + b, span])
        own_k, own_v = own_kv(t, level)
        return (
            jnp.concatenate([own_k, jnp.concatenate([k, kd], axis=1)], axis=0),
            jnp.concatenate([own_v, v], axis=0),
        )

    def put(t, level, result, out, stats, shift):
        o, lse = result
        first, count, _ = REGIONS[level]
        spot = slice(first - shift, first - shift + count)
        for d in range(2):
            for b in range(2):
                rows = slice((2 * d + b) * count, (2 * d + b + 1) * count)
                out[d, t, b, spot] = o[rows].astype(BF16)
                keep(stats, (d, b), spot, t, lse[rows])

    def near(n):
        return lambda s: s + causal[:n, :n]

    def near_half(n):
        def bias(s):
            return jnp.concatenate([s[:, :n] + causal[:n, :n], s[:, n:]], axis=1)

        return bias

    def partner_out(t):
        return remote(
            ob.at[1 - j, t, :, pl.ds(0, SEL)], oo_in.at[t, :, pl.ds(0, SEL)],
            oo_send, oo_recv, device(0, 1 - j),
        )

    def ret_copy(t, low, high, d):
        return remote(
            os1.at[d, t, :, pl.ds(low, high - low)], far_out.at[HALF * j + t, :, pl.ds(low, high - low)],
            o_send, o_recv, device(1, d),
        )

    plans = (
        (c % 4 == 0, "2", ""),
        (c % 4 == 1, "34", "34"),
        (c % 4 == 2, "234", ""),
        (c == 3, "4", ""),
    )

    def each_return(t, more):
        for present, pieces in far_pieces(c + 1):

            @pl.when(present & (c <= 6) & more)
            def _():
                for low, high in pieces:
                    for d in range(2):
                        ret_copy(t, low, high, d).start()

    def level_head(t, _):
        exchange(t).wait_recv()
        pick = pbuf[t]
        dqs[t] = nt(pick, ot_q[...]).astype(BF16)
        for d in range(2):
            dks[d, t] = nt(pick, ot_k[d]).astype(BF16)
            dps[d, t] = nt(pick[192:], ot_k[2 + d]).astype(BF16)

        problems = []
        q = own_q(t, 0)
        k, v = own_kv(t, 0)
        problems.append((q[:CHUNK], k[:CHUNK], v[:CHUNK], near(CHUNK)))
        late = lambda s: jnp.concatenate([s[:, :CHUNK], s[:, CHUNK:] + causal[...]], axis=1)
        problems.append((q[CHUNK:], k, v, late))
        for level in (1, 2, 3):
            problems.append((own_q(t, level),) + own_kv(t, level) + (near(4 * REGIONS[level][1]),))
        for h in (2 * t, 2 * t + 1):
            q, k, v = columns(0, h), columns(1, h), columns(2, h)
            for b in range(2):
                span = slice(b * CHUNK, (b + 1) * CHUNK)
                problems.append((q[span], k[span], v[span], lambda s, b=b: s + bias0[b]))
        results = attend(problems)
        first = tuple(jnp.concatenate(pair, axis=0) for pair in zip(results[0], results[1]))
        for level, result in enumerate([first] + results[2:5]):
            put(t, level, result, ob, st_own, 0)
        for i in range(2):
            for b in range(2):
                span = slice(b * CHUNK, (b + 1) * CHUNK)
                o, lse = results[5 + 2 * i + b]
                o0[2 * t + i, span] = o
                keep(lse0, (), span, 2 * t + i, lse)

        for present, (low, high) in next_pieces(c - 1):

            @pl.when(present & (c >= 1))
            def _():
                got(kvp.at[t, :, :, pl.ds(low, high - low)], k_recv.at[t])

        for present, pieces in far_pieces(c + 1):

            @pl.when(present & (c <= 6))
            def _():
                got(q1in.at[t, :, pl.ds(0, size_of(pieces))], q_recv.at[t])

        for present, guests, owns in plans:

            @pl.when(present)
            def _():
                problems = []
                for name in guests:
                    level = int(name) - 1
                    kv_pair = own_kv(t, level) if level == 1 else both_kv(t, level)
                    problems.append((guest_q(t, level),) + kv_pair + (None,))
                for name in owns:
                    level = int(name) - 1
                    n = 4 * REGIONS[level][1]
                    problems.append((own_q(t, level),) + both_kv(t, level) + (near_half(n),))
                results = attend(problems)
                for name, result in zip(guests, results):
                    put(t, int(name) - 1, result, os1, st1, 128)
                for name, result in zip(owns, results[len(guests) :]):
                    put(t, int(name) - 1, result, ob, st_own, 0)

        each_return(t, t < HALF - jnp.where(c % 4 == 0, 3, 1))
        partner_out(t).start()
        return 0

    lax.fori_loop(0, HALF, level_head, 0)

    for d in range(2):
        for b in range(2):
            ls1[d, b] = st1[d, b].T[:HALF]
            ls_own[d, b] = st_own[d, b].T[:HALF]

    def far_stats(d):
        return remote(ls1.at[d], lr1.at[j], l_send, l_recv.at[1 + j], device(1, d))

    @pl.when(c <= 6)
    def _():
        for d in range(2):
            far_stats(d).start()

    each_return(HALF - 3, c % 4 == 0)
    each_return(HALF - 2, c % 4 == 0)
    each_return(HALF - 1, True)

    def two_back(d):
        return remote(
            os2.at[d], far_out.at[pl.ds(pl.multiple_of(HALF * j, HALF), HALF), :, pl.ds(96, 16)],
            o_two_send, o_two_recv, device(2, d),
        )

    def two_stats(d):
        return remote(ls2.at[d], lr2.at[j], l_two_send, l_recv.at[3 + j], device(2, d))

    @pl.when(c == 3)
    def _():
        got(q2in, two_recv)
        problems = []
        for t in range(HALF):
            q = with_docs(join(lambda d, b: q2in[t, 2 * d + b]), 2, 3, t)
            problems.append((q,) + own_kv(t, 3) + (None,))
        for t, (o, lse) in enumerate(attend(problems)):
            for d in range(2):
                for b in range(2):
                    rows = slice((2 * d + b) * 16, (2 * d + b + 1) * 16)
                    os2[d, t, b] = o[rows].astype(BF16)
                    keep(st2, (d, b), slice(96, FAR), t, lse[rows])
        for d in range(2):
            for b in range(2):
                ls2[d, b] = st2[d, b].T[:HALF]
        for d in range(2):
            two_stats(d).start()
        for d in range(2):
            two_back(d).start()

    l_own = remote(ls_own.at[1 - j], lo_in, l_own_send, l_recv.at[0], device(0, 1 - j))
    l_own.start()
    l_own.wait_recv()

    mine = ls_own[j]
    theirs = lo_in[...]
    lower = jnp.where(j == 0, mine, theirs)
    upper = jnp.where(j == 0, theirs, mine)
    wide = iota((1, CHUNK), 1)
    own = jnp.concatenate([lower[0], upper[0], lower[1], upper[1]], axis=0)
    own = jnp.where(wide < SEL, own, NEG)
    tall = iota((CHUNK, CHUNK), 0)
    own3 = split3(own)
    zeroth = lse0[...].T
    parts = [jnp.concatenate([zeroth[:HEADS, :CHUNK], zeroth[:HEADS, CHUNK:]], axis=0)]
    spread, chosen = [], []
    for level, (first, count, bits) in enumerate(REGIONS):
        hit = ((iota((CHUNK, CHUNK), 1) >> bits) == tall - first) & (tall >= first) & (tall < first + count)
        spread.append(jnp.where(hit, 1.0, 0.0).astype(BF16))
        chosen.append(picked(off_ref, level, bits))
        parts.append(jnp.where(chosen[level], fold3(nn(own3, spread[level])), NEG))
    lse = log_sum(parts)
    back = jnp.zeros((2 * HEADS, CHUNK), F32)
    for level in range(4):
        back = back + fold3(nt(split3(jnp.where(chosen[level], lse, 0.0)), spread[level]))
    al_own[...] = jnp.exp2(own - back)
    lse_loc[...] = lse
    for b in range(2):
        span = slice(b * CHUNK, (b + 1) * CHUNK)
        a0[span] = jnp.exp2(lse0[span] - upright(lse, b))

    def loc_copy(h):
        return pltpu.make_async_copy(loc.at[h], loc_out.at[h], store_sem)

    own_first = jnp.where(wide < 128, 0, jnp.where(wide < 192, 128, jnp.where(wide < 224, 192, 224)))
    own_bits = jnp.where(wide < 128, 1, jnp.where(wide < 192, 2, jnp.where(wide < 224, 3, 4)))
    own_base = tall - ((wide - own_first) << own_bits)

    got(oo_in.at[:, :, pl.ds(0, SEL)], oo_recv)

    def local_head(t, _):
        for which in range(2):
            h = HALF * j + t if which == 0 else HALF * (1 - j) + t
            o1, o2, o3, o4 = [off_ref[i, h] & (2 << i) - 1 for i in range(4)]
            shift = jnp.where(wide < 128, o1, jnp.where(wide < 192, o2, jnp.where(wide < 224, o3, o4)))
            hit = own_base == shift
            for b in range(2):
                span = slice(b * CHUNK, (b + 1) * CHUNK)
                weight = jnp.where(hit, al_own[pl.ds(b * HEADS + h, 1), :], 0.0).astype(BF16)
                mixed = nn(weight, ob[j, t, b] if which == 0 else oo_in[t, b])
                scale = jnp.sum(jnp.where(lane == h, a0[span], 0.0), axis=1, keepdims=True)
                loc[h, span] = (mixed + scale * o0[h, span]).astype(BF16)
            loc_copy(h).start()
        return 0

    lax.fori_loop(0, HALF, local_head, 0)

    @pl.when(c >= 1)
    def _():
        for i in range(2):
            got(lr1.at[i], l_recv.at[1 + i])

    @pl.when(c == 5)
    def _():
        for i in range(2):
            got(lr2.at[i], l_recv.at[3 + i])

    one, two = [
        jnp.concatenate([ref[0, 0], ref[1, 0], ref[0, 1], ref[1, 1]], axis=0) for ref in (lr1, lr2)
    ]
    far = jnp.where((lane >= 96) & (c == 5), two, one)
    far = jnp.where(valid_row(lane, c), far, NEG)
    far3 = split3(far)
    tall = iota((DIM, CHUNK), 0) + DIM
    parts, spread, chosen = [lse_loc[...]], [], []
    for level, (first, count, bits) in enumerate(REGIONS):
        if level > 0:
            hit = ((iota((DIM, CHUNK), 1) >> bits) == tall - first) & (tall >= first) & (tall < first + count)
            spread.append(jnp.where(hit, 1.0, 0.0).astype(BF16))
            chosen.append(picked(off_ref, level, bits))
            parts.append(jnp.where(chosen[-1], fold3(nn(far3, spread[-1])), NEG))
    lse = log_sum(parts)
    back = jnp.zeros((2 * HEADS, DIM), F32)
    for pick, wide in zip(chosen, spread):
        back = back + fold3(nt(split3(jnp.where(pick, lse, 0.0)), wide))
    al_far[...] = jnp.exp2(far - back)
    portion = jnp.exp2(lse_loc[...] - lse)
    pad = jnp.zeros((DIM - GROUP, CHUNK), F32)
    for g in range(HEADS // GROUP):
        for b in range(2):
            first = b * HEADS + g * GROUP
            share[g, b * CHUNK : (b + 1) * CHUNK] = jnp.concatenate([portion[first : first + GROUP], pad], axis=0).T
    al_copy = pltpu.make_async_copy(al_far, al_out, al_sem)
    share_copy = pltpu.make_async_copy(share, share_out, lse_sem)
    al_copy.start()
    share_copy.start()

    for present, slots in (((c > 0) & (c < 7) & (c != 5), 5), ((c == 0) | (c == 7), 3), (c == 5, 7)):

        @pl.when(present)
        def _():
            part = docs_all.at[pl.ds(0, slots)]
            remote(part, part, d_send, d_recv.at[0], device(0, 1 - j)).wait_send()

    l_own.wait_send()

    al_copy.wait()
    share_copy.wait()
    sent(sx, x_send)
    sent(oo_in.at[:, :, pl.ds(0, SEL)], oo_send)
    pltpu.make_async_copy(loc, loc_out, store_sem).wait()
    for present, pieces in far_pieces(c):

        @pl.when(present)
        def _():
            sent(q1in.at[:, :, pl.ds(0, size_of(pieces))], q_send)

    for present, (low, high) in next_pieces(c):

        @pl.when(present)
        def _():
            sent(kvp.at[:, :, :, pl.ds(0, high - low)], k_send)

    for present, pieces in far_pieces(c + 1):

        @pl.when(present & (c <= 6))
        def _():
            sent(os1.at[:, :, :, pl.ds(0, size_of(pieces))], o_send)
            sent(ls1, l_send)

    @pl.when(c == 3)
    def _():
        sent(os2, o_two_send)
        sent(ls2, l_two_send)

    @pl.when(c == 5)
    def _():
        sent(q2in, two_send)
        got(far_out.at[:, :, pl.ds(0, 16)], o_two_recv)

    for present, pieces in far_pieces(c):

        @pl.when(present)
        def _():
            got(far_out.at[:, :, pl.ds(0, size_of(pieces))], o_recv)


def valid_row(x, c):
    return ((x < 64) & (c % 2 == 1)) | ((x >= 64) & (x < 96) & (c % 4 >= 2)) | ((x >= 96) & (x < FAR) & (c >= 2))


def picked(off_ref, level, bits):
    head = iota((HEADS, CHUNK), 0)
    shifts = jnp.zeros((HEADS, CHUNK), I32)
    for h in range(HEADS):
        shifts = jnp.where(head == h, off_ref[level, h] & ((1 << bits) - 1), shifts)
    pick = (iota((HEADS, CHUNK), 1) & ((1 << bits) - 1)) == shifts
    return jnp.concatenate([pick, pick], axis=0)


def log_sum(parts):
    top = parts[0]
    for part in parts[1:]:
        top = jnp.maximum(top, part)
    total = jnp.exp2(parts[0] - top)
    for part in parts[1:]:
        total = total + jnp.exp2(part - top)
    return top + jnp.log2(total)


def upright(dense, b):
    pad = jnp.zeros((DIM - HEADS, CHUNK), F32)
    return jnp.concatenate([dense[b * HEADS : (b + 1) * HEADS], pad], axis=0).T


GROUP = 8


def join_kernel(loc_ref, far_ref, al_far, a_loc, off_ref, out_ref):
    c = lax.axis_index("ctx") // 2
    lane = iota((1, DIM), 1)

    sent = valid_row(iota((DIM, DIM), 0), c)
    row = lane + DIM
    first = jnp.where(row < 192, 128, jnp.where(row < 224, 192, 224))
    bits = jnp.where(row < 192, 2, jnp.where(row < 224, 3, 4))
    base = iota((CHUNK, DIM), 0) - ((row - first) << bits)
    for i in range(GROUP):
        h = pl.program_id(0) * GROUP + i
        o2, o3, o4 = [off_ref[level, h] & (2 << level) - 1 for level in (1, 2, 3)]
        hit = base == jnp.where(row < 192, o2, jnp.where(row < 224, o3, o4))
        for b in range(2):
            span = slice(b * CHUNK, (b + 1) * CHUNK)
            weight = jnp.where(hit, al_far[pl.ds(b * HEADS + h, 1), :], 0.0).astype(BF16)
            mixed = nn(weight, jnp.where(sent, far_ref[i, b], jnp.zeros((DIM, DIM), BF16)))
            scale = a_loc[0, span, i : i + 1]
            out_ref[0, span, i * DIM : (i + 1) * DIM] = (mixed + scale * loc_ref[i, span].astype(F32)).astype(BF16)


def on_device(queries, key_rows, value_rows, document_ids, dilation_offsets):
    any_space = pl.BlockSpec(memory_space=pl.ANY)
    smem = pl.BlockSpec(memory_space=pltpu.SMEM)
    dma = pltpu.SemaphoreType.DMA

    def vmem(*shape, kind=BF16):
        return pltpu.VMEM(shape, kind)

    local, far, far_share, local_share = pl.pallas_call(
        kernel,
        out_shape=(
            jax.ShapeDtypeStruct((HEADS, ROWS, DIM), BF16),
            jax.ShapeDtypeStruct((HEADS, 2, DIM, DIM), BF16),
            jax.ShapeDtypeStruct((2 * HEADS, DIM), F32),
            jax.ShapeDtypeStruct((HEADS // GROUP, ROWS, DIM), F32),
        ),
        in_specs=[any_space] * 5,
        out_specs=(any_space,) * 4,
        scratch_shapes=[
            vmem(1, ROWS, kind=I32), pltpu.SMEM((4, HEADS), I32), vmem(3, ROWS, HEADS * DIM),
            vmem(HALF, 3, 4, SEL, DIM), vmem(HALF, 3, 2, SEL, DIM), vmem(HALF, 4, FAR, DIM), vmem(HALF, 4, 16, DIM),
            vmem(HALF, 2, 4, FAR3, DIM),
            vmem(HALF, SEL, CHUNK), vmem(2, HALF, SEL, CHUNK), vmem(2, HALF, FAR3, CHUNK), vmem(HALF, SEL, CHUNK),
            vmem(2, HALF, 2, CHUNK, DIM), vmem(HALF, 2, CHUNK, DIM), vmem(2, HALF, 2, FAR, DIM), vmem(2, HALF, 2, 16, DIM),
            vmem(HEADS, ROWS, DIM, kind=F32), vmem(HEADS, ROWS, DIM),
            vmem(2, 2, CHUNK, DIM, kind=F32), vmem(2, 2, DIM, DIM, kind=F32), vmem(2, 2, DIM, DIM, kind=F32),
            vmem(ROWS, DIM, kind=F32),
            vmem(2, 2, HALF, CHUNK, kind=F32), vmem(2, 2, HALF, DIM, kind=F32), vmem(2, 2, HALF, DIM, kind=F32),
            vmem(2, HALF, CHUNK, kind=F32), vmem(2, 2, HALF, DIM, kind=F32), vmem(2, 2, HALF, DIM, kind=F32),
            vmem(2 * HEADS, CHUNK, kind=F32),
            vmem(8, 1, ROWS, kind=I32), vmem(2 * DIM, CHUNK), vmem(4, 2 * DIM, CHUNK),
            vmem(SEL, CHUNK, kind=I32), vmem(CHUNK, CHUNK, kind=F32), vmem(2, CHUNK, CHUNK, kind=F32),
            vmem(2 * HEADS, CHUNK, kind=F32), vmem(ROWS, DIM, kind=F32),
            vmem(2 * HEADS, DIM, kind=F32), vmem(HEADS // GROUP, ROWS, DIM, kind=F32),
            dma((6,)), dma((18,)), dma((8,)), dma((HALF,)), dma((HALF,)), dma((HALF,)), dma((5,)),
        ],
        compiler_params=pltpu.CompilerParams(collective_id=0, has_side_effects=True, vmem_limit_bytes=56 << 20),
        name="dilated_attention",
    )(queries, key_rows, value_rows, document_ids, dilation_offsets)
    return pl.pallas_call(
        join_kernel,
        grid=(HEADS // GROUP,),
        out_shape=jax.ShapeDtypeStruct((1, ROWS, HEADS * DIM), BF16),
        in_specs=[
            pl.BlockSpec((GROUP, ROWS, DIM), lambda i: (i, 0, 0)),
            pl.BlockSpec((GROUP, 2, DIM, DIM), lambda i: (i, 0, 0, 0)),
            pl.BlockSpec(memory_space=pltpu.VMEM),
            pl.BlockSpec((1, ROWS, DIM), lambda i: (i, 0, 0)),
            smem,
        ],
        out_specs=pl.BlockSpec((1, ROWS, GROUP * DIM), lambda i: (0, 0, i)),
        compiler_params=pltpu.CompilerParams(vmem_limit_bytes=60 << 20),
        name="join_far",
    )(local, far, far_share, local_share, dilation_offsets)


def solution(mesh):
    placed = (P("dp", "ctx", None), P("dp", "ctx", None), P("dp", "ctx", None), P("dp", "ctx"), P())
    return jax.shard_map(
        on_device, mesh=mesh, in_specs=placed, out_specs=P("dp", "ctx", None), check_vma=False
    )
```

```python
import math

import jax
import jax.numpy as jnp
from jax import lax
from jax.experimental import pallas as pl
from jax.experimental.pallas import tpu as pltpu
from jax.sharding import PartitionSpec as P

MESH = pl.DeviceIdType.MESH
F32, BF16, I32 = jnp.float32, jnp.bfloat16, jnp.int32
HEADS, HALF, ROWS, DIM, CHUNK = 16, 8, 512, 128, 256
SEL, FAR, FAR3 = 240, 112, 48
REGIONS = ((0, 128, 1), (128, 64, 2), (192, 32, 3), (224, 16, 4))
NEG = -1e30
SCALE2 = math.log2(math.e) / math.sqrt(DIM)


def nt(a, b):
    return lax.dot_general(a, b, (((1,), (1,)), ((), ())), preferred_element_type=F32)


def nn(a, b):
    return jnp.dot(a, b, preferred_element_type=F32)


def split3(x):
    first = x.astype(BF16)
    rest = x - first.astype(F32)
    second = rest.astype(BF16)
    third = (rest - second.astype(F32)).astype(BF16)
    return jnp.concatenate([first, second, third], axis=0)


def fold3(x):
    n = x.shape[0] // 3
    return (x[2 * n :] + x[n : 2 * n]) + x[:n]


def iota(shape, dim):
    return lax.broadcasted_iota(I32, shape, dim)


def attend(problems):
    scores = [nt(q, k) if bias is None else bias(nt(q, k)) for q, k, _, bias in problems]
    tops = [jnp.max(s, axis=1, keepdims=True) for s in scores]
    weights = [jnp.exp2((s - top) * SCALE2).astype(BF16) for s, top in zip(scores, tops)]
    sums = [nn(w, jnp.concatenate([v, jnp.ones_like(v)], axis=1)) for w, (_, _, v, _) in zip(weights, problems)]
    return [(x[:, :DIM] / x[:, DIM:], top * SCALE2 + jnp.log2(x[:, DIM:])) for x, top in zip(sums, tops)]


def far_pieces(chip):
    return (
        (chip % 4 == 3, ((0, FAR),)),
        (chip % 4 == 2, ((64, FAR),)),
        (chip % 4 == 1, ((0, 64),)),
        (chip == 4, ((96, FAR),)),
    )


def next_pieces(chip):
    return ((chip % 4 < 2, (0, FAR3)), (chip == 2, (32, FAR3)))


def kernel(
    q_hbm, k_hbm, v_hbm, docs_hbm, off_hbm,
    loc_out, far_out, al_out, share_out,
    docs_ref, off_ref, xv, cx, sx, q1in, q2in, kvp, dqs, dks, dps, pbuf,
    ob, oo_in, os1, os2, o0, loc,
    st_own, st1, st2, lse0, ls_own, ls1, ls2, lo_in, lr1, lr2, lse_loc,
    docs_all, ot_q, ot_k, base_m, causal, bias0, al_own, a0, al_far, share,
    load_sem, once, d_recv, x_recv, q_recv, k_recv, l_recv,
):
    me = lax.axis_index("ctx")
    dp = lax.axis_index("dp")
    c = me // 2
    j = me % 2

    def device(steps, core):
        return (dp, ((c + steps + 8) % 8) * 2 + core)

    def remote(src, dst, send, recv, to):
        return pltpu.make_async_remote_copy(
            src_ref=src, dst_ref=dst, send_sem=send, recv_sem=recv, device_id=to, device_id_type=MESH
        )

    store_sem, lse_sem, d_send, x_send, q_send, k_send, o_send, o_recv, oo_send, oo_recv, l_send, l_own_send, two_send, two_recv, o_two_send, o_two_recv, l_two_send, al_sem = [
        once.at[i] for i in range(18)
    ]

    near_chips = ((1, c <= 6), (-1, c >= 1))
    barrier = pltpu.get_barrier_semaphore()
    pl.semaphore_signal(barrier, inc=1, device_id=device(0, 1 - j), device_id_type=MESH)
    for g, present in near_chips:

        @pl.when(present)
        def _():
            for core in (0, 1):
                pl.semaphore_signal(barrier, inc=1, device_id=device(g, core), device_id_type=MESH)

    guest_of_two = ((c == 5, -2), (c == 3, 2))
    for present, g in guest_of_two:

        @pl.when(present)
        def _():
            for core in (0, 1):
                pl.semaphore_signal(barrier, inc=1, device_id=device(g, core), device_id_type=MESH)

    def load_start(u):
        for half in range(2):
            first = HALF * (1 - j) if half == 0 else HALF * j
            span = pl.ds(pl.multiple_of((first + 2 * u) * DIM, DIM), 2 * DIM)
            for i, src in enumerate((q_hbm, k_hbm, v_hbm)):
                pltpu.make_async_copy(src.at[0, :, span], xv.at[i, :, span], load_sem.at[u]).start()

    def load_wait(u):
        part = xv.at[:, :, pl.ds(0, 4 * DIM)]
        pltpu.make_async_copy(part, part, load_sem.at[u]).wait()

    docs_load = pltpu.make_async_copy(docs_hbm, docs_ref, load_sem.at[4])
    off_load = pltpu.make_async_copy(off_hbm, off_ref, load_sem.at[5])
    docs_load.start()
    off_load.start()
    load_start(0)

    for first, count, bits in REGIONS:
        base_m[first : first + count] = iota((count, CHUNK), 1) - (iota((count, CHUNK), 0) << bits)

    docs_load.wait()
    off_load.wait()
    pl.semaphore_wait(barrier, 1 + jnp.where(c <= 6, 2, 0) + jnp.where(c >= 1, 2, 0) + jnp.where((c == 3) | (c == 5), 2, 0))

    def docs_copy(g, core, slot):
        return remote(docs_ref, docs_all.at[slot], d_send, d_recv.at[slot], device(g, core))

    def each_docs(do):
        do(docs_copy(0, 1 - j, j))
        for (g, present), first in zip(near_chips, (4, 2)):

            @pl.when(present)
            def _():
                for core in (0, 1):
                    do(docs_copy(g, core, first + j))

        @pl.when(c == 5)
        def _():
            for core in (0, 1):
                do(docs_copy(-2, core, 6 + j))

    each_docs(lambda copy: copy.start())
    docs_all[j] = docs_ref[...]

    def core_of(which):
        return 1 - j if which == 0 else j

    def q_copy(t, which, low, high):
        rows = pl.ds(128 + low, high - low)
        return remote(
            sx.at[t, 0, :, rows] if which == 0 else cx.at[t, 0, pl.ds(2 * j, 2), rows],
            q1in.at[t, pl.ds(2 * j, 2), pl.ds(low, high - low)],
            q_send, q_recv.at[t], device(-1, core_of(which)),
        )

    def kv_copy(t, which, low, high):
        rows = pl.ds(192 + low, high - low)
        return remote(
            sx.at[t, pl.ds(1, 2), :, rows] if which == 0 else cx.at[t, pl.ds(1, 2), pl.ds(2 * j, 2), rows],
            kvp.at[t, :, pl.ds(2 * j, 2), pl.ds(low, high - low)],
            k_send, k_recv.at[t], device(1, core_of(which)),
        )

    def two_copy(t, which):
        rows = pl.ds(224, 16)
        return remote(
            sx.at[t, 0, :, rows] if which == 0 else cx.at[t, 0, pl.ds(2 * j, 2), rows],
            q2in.at[t, pl.ds(2 * j, 2)], two_send, two_recv, device(-2, core_of(which)),
        )

    def each_q(t, which):
        @pl.when(c == 5)
        def _():
            two_copy(t, which).start()

        for present, pieces in far_pieces(c):

            @pl.when(present)
            def _():
                for low, high in pieces:
                    q_copy(t, which, low, high).start()

    def each_kv(t, which):
        for present, (low, high) in next_pieces(c):

            @pl.when(present)
            def _():
                kv_copy(t, which, low, high).start()

    def exchange(t):
        return remote(sx.at[t], cx.at[t, :, pl.ds(2 * j, 2)], x_send, x_recv.at[t], device(0, 1 - j))

    def size_of(pieces):
        return sum(high - low for low, high in pieces)

    def got(part, sem):
        remote(part, part, once.at[0], sem, device(0, 1 - j)).wait_recv()

    def sent(part, sem):
        remote(part, part, sem, once.at[0], device(0, 1 - j)).wait_send()

    def picker(h):
        parts = []
        for level, (first, count, bits) in enumerate(REGIONS):
            shift = off_ref[level, h] & ((1 << bits) - 1)
            parts.append(jnp.where(base_m[first : first + count] == shift, 1.0, 0.0))
        return jnp.concatenate(parts, axis=0).astype(BF16)

    def columns(i, h):
        return xv[i, :, pl.ds(pl.multiple_of(h * DIM, DIM), DIM)]

    def select(pick, i, h):
        x = columns(i, h)
        both = nn(pick, jnp.concatenate([x[:CHUNK], x[CHUNK:]], axis=1)).astype(BF16)
        return both[:, :DIM], both[:, DIM:]

    def select_head(t, _):
        @pl.when(t % 2 == 0)
        def _():
            load_wait(t // 2)

            @pl.when(t < 6)
            def _():
                load_start(t // 2 + 1)

        for which in range(2):
            h = HALF * (1 - j) + t if which == 0 else HALF * j + t
            pick = picker(h)
            if which == 1:
                pbuf[t] = pick
            for i in range(3):
                for b, part in enumerate(select(pick, i, h)):
                    if which == 0:
                        sx[t, i, b] = part
                    else:
                        cx[t, i, 2 * j + b] = part
            each_q(t, which)
            each_kv(t, which)
            if which == 0:
                exchange(t).start()
        return 0

    lax.fori_loop(0, HALF, select_head, 0)

    def clear_pads(t, _):
        for b in range(2):
            oo_in[t, b, SEL:] = jnp.zeros((CHUNK - SEL, DIM), BF16)
            for d in range(2):
                ob[d, t, b, SEL:] = jnp.zeros((CHUNK - SEL, DIM), BF16)
        return 0

    lax.fori_loop(0, HALF, clear_pads, 0)

    causal[...] = jnp.where(iota((CHUNK, CHUNK), 1) <= iota((CHUNK, CHUNK), 0), 0.0, NEG)
    eye = jnp.where(iota((CHUNK, CHUNK), 1) == iota((CHUNK, CHUNK), 0), 1.0, 0.0).astype(BF16)
    for b in range(2):
        same = docs_ref[:, b * CHUNK : (b + 1) * CHUNK] == iota((DIM, CHUNK), 0)
        q_one = nt(eye, jnp.where(same, 1.0, 0.0).astype(BF16)).astype(BF16)
        k_one = nt(eye, jnp.where(same, 0.0, NEG).astype(BF16)).astype(BF16)
        bias0[b] = nt(q_one, k_one) + causal[...]

    docs_copy(0, 1 - j, 1 - j).wait_recv()
    for (g, present), first in zip(near_chips, (2, 4)):

        @pl.when(present)
        def _():
            for core in (0, 1):
                docs_copy(g, core, first + core).wait_recv()

        @pl.when(jnp.logical_not(present))
        def _():
            for core in (0, 1):
                docs_all[first + core] = docs_ref[...]

    @pl.when(c == 3)
    def _():
        for core in (0, 1):
            docs_copy(-2, core, 6 + core).wait_recv()

    @pl.when(c != 3)
    def _():
        for core in (0, 1):
            docs_all[6 + core] = docs_ref[...]

    for b in range(2):
        span = slice(b * CHUNK, (b + 1) * CHUNK)
        ones = [jnp.where(docs_all[g, :, span] == iota((8, CHUNK), 0), 1.0, 0.0) for g in (0, 1, 2, 3, 6, 7)]
        ones.append(jnp.zeros((DIM - 48, CHUNK), F32))
        ot_q[b * DIM : (b + 1) * DIM] = jnp.concatenate(ones, axis=0).astype(BF16)
        for i, slot in enumerate((0, 1, 4, 5)):
            same = docs_all[slot, :, span] == (iota((DIM, CHUNK), 0) & 7)
            ot_k[i, b * DIM : (b + 1) * DIM] = jnp.where(same, 0.0, NEG).astype(BF16)

    lane = iota((1, DIM), 1)

    def keep(ref, index, rows, t, value):
        old = ref[index + (rows,)]
        ref[index + (rows,)] = jnp.where(lane == t, value, old)

    def join(piece):
        return jnp.concatenate([piece(d, b) for d in range(2) for b in range(2)], axis=0)

    def with_docs(q, g, level, t):
        first, count, _ = REGIONS[level]

        def piece(d, b):
            mark = jnp.where((lane >> 3) == 2 * g + d, 1.0, 0.0).astype(BF16)
            return dqs[t, first : first + count, b * DIM : (b + 1) * DIM] * mark

        return jnp.concatenate([q, join(piece)], axis=1)

    def own_q(t, level):
        first, count, _ = REGIONS[level]
        return with_docs(join(lambda d, b: cx[t, 0, 2 * d + b, first : first + count]), 0, level, t)

    def guest_q(t, level):
        first, count, _ = REGIONS[level]
        return with_docs(join(lambda d, b: q1in[t, 2 * d + b, first - 128 : first - 128 + count]), 1, level, t)

    def own_kv(t, level):
        first, count, _ = REGIONS[level]
        span = slice(first, first + count)
        k = join(lambda d, b: cx[t, 1, 2 * d + b, span])
        kd = join(lambda d, b: dks[d, t, span, b * DIM : (b + 1) * DIM])
        return jnp.concatenate([k, kd], axis=1), join(lambda d, b: cx[t, 2, 2 * d + b, span])

    def both_kv(t, level):
        first, count, _ = REGIONS[level]
        span = slice(first - 192, first - 192 + count)
        k = join(lambda d, b: kvp[t, 0, 2 * d + b, span])
        kd = join(lambda d, b: dps[d, t, span, b * DIM : (b + 1) * DIM])
        v = join(lambda d, b: kvp[t, 1, 2 * d + b, span])
        own_k, own_v = own_kv(t, level)
        return (
            jnp.concatenate([own_k, jnp.concatenate([k, kd], axis=1)], axis=0),
            jnp.concatenate([own_v, v], axis=0),
        )

    def put(t, level, result, out, stats, shift):
        o, lse = result
        first, count, _ = REGIONS[level]
        spot = slice(first - shift, first - shift + count)
        for d in range(2):
            for b in range(2):
                rows = slice((2 * d + b) * count, (2 * d + b + 1) * count)
                out[d, t, b, spot] = o[rows].astype(BF16)
                keep(stats, (d, b), spot, t, lse[rows])

    def near(n):
        return lambda s: s + causal[:n, :n]

    def near_half(n):
        def bias(s):
            return jnp.concatenate([s[:, :n] + causal[:n, :n], s[:, n:]], axis=1)

        return bias

    def partner_out(t):
        return remote(
            ob.at[1 - j, t, :, pl.ds(0, SEL)], oo_in.at[t, :, pl.ds(0, SEL)],
            oo_send, oo_recv, device(0, 1 - j),
        )

    def ret_copy(t, low, high, d):
        return remote(
            os1.at[d, t, :, pl.ds(low, high - low)], far_out.at[HALF * j + t, :, pl.ds(low, high - low)],
            o_send, o_recv, device(1, d),
        )

    plans = (
        (c % 4 == 0, "2", ""),
        (c % 4 == 1, "34", "34"),
        (c % 4 == 2, "234", ""),
        (c == 3, "4", ""),
    )

    def each_return(t, more):
        for present, pieces in far_pieces(c + 1):

            @pl.when(present & (c <= 6) & more)
            def _():
                for low, high in pieces:
                    for d in range(2):
                        ret_copy(t, low, high, d).start()

    def level_head(t, _):
        exchange(t).wait_recv()
        pick = pbuf[t]
        dqs[t] = nt(pick, ot_q[...]).astype(BF16)
        for d in range(2):
            dks[d, t] = nt(pick, ot_k[d]).astype(BF16)
            dps[d, t] = nt(pick[192:], ot_k[2 + d]).astype(BF16)

        problems = []
        q = own_q(t, 0)
        k, v = own_kv(t, 0)
        problems.append((q[:CHUNK], k[:CHUNK], v[:CHUNK], near(CHUNK)))
        late = lambda s: jnp.concatenate([s[:, :CHUNK], s[:, CHUNK:] + causal[...]], axis=1)
        problems.append((q[CHUNK:], k, v, late))
        for level in (1, 2, 3):
            problems.append((own_q(t, level),) + own_kv(t, level) + (near(4 * REGIONS[level][1]),))
        for h in (2 * t, 2 * t + 1):
            q, k, v = columns(0, h), columns(1, h), columns(2, h)
            for b in range(2):
                span = slice(b * CHUNK, (b + 1) * CHUNK)
                problems.append((q[span], k[span], v[span], lambda s, b=b: s + bias0[b]))
        results = attend(problems)
        first = tuple(jnp.concatenate(pair, axis=0) for pair in zip(results[0], results[1]))
        for level, result in enumerate([first] + results[2:5]):
            put(t, level, result, ob, st_own, 0)
        for i in range(2):
            for b in range(2):
                span = slice(b * CHUNK, (b + 1) * CHUNK)
                o, lse = results[5 + 2 * i + b]
                o0[2 * t + i, span] = o
                keep(lse0, (), span, 2 * t + i, lse)

        for present, (low, high) in next_pieces(c - 1):

            @pl.when(present & (c >= 1))
            def _():
                got(kvp.at[t, :, :, pl.ds(low, high - low)], k_recv.at[t])

        for present, pieces in far_pieces(c + 1):

            @pl.when(present & (c <= 6))
            def _():
                got(q1in.at[t, :, pl.ds(0, size_of(pieces))], q_recv.at[t])

        for present, guests, owns in plans:

            @pl.when(present)
            def _():
                problems = []
                for name in guests:
                    level = int(name) - 1
                    kv_pair = own_kv(t, level) if level == 1 else both_kv(t, level)
                    problems.append((guest_q(t, level),) + kv_pair + (None,))
                for name in owns:
                    level = int(name) - 1
                    n = 4 * REGIONS[level][1]
                    problems.append((own_q(t, level),) + both_kv(t, level) + (near_half(n),))
                results = attend(problems)
                for name, result in zip(guests, results):
                    put(t, int(name) - 1, result, os1, st1, 128)
                for name, result in zip(owns, results[len(guests) :]):
                    put(t, int(name) - 1, result, ob, st_own, 0)

        each_return(t, t < HALF - jnp.where(c % 4 == 0, 3, 1))
        partner_out(t).start()
        return 0

    lax.fori_loop(0, HALF, level_head, 0)

    for d in range(2):
        for b in range(2):
            ls1[d, b] = st1[d, b].T[:HALF]
            ls_own[d, b] = st_own[d, b].T[:HALF]

    def far_stats(d):
        return remote(ls1.at[d], lr1.at[j], l_send, l_recv.at[1 + j], device(1, d))

    @pl.when(c <= 6)
    def _():
        for d in range(2):
            far_stats(d).start()

    each_return(HALF - 3, c % 4 == 0)
    each_return(HALF - 2, c % 4 == 0)
    each_return(HALF - 1, True)

    def two_back(d):
        return remote(
            os2.at[d], far_out.at[pl.ds(pl.multiple_of(HALF * j, HALF), HALF), :, pl.ds(96, 16)],
            o_two_send, o_two_recv, device(2, d),
        )

    def two_stats(d):
        return remote(ls2.at[d], lr2.at[j], l_two_send, l_recv.at[3 + j], device(2, d))

    @pl.when(c == 3)
    def _():
        got(q2in, two_recv)
        problems = []
        for t in range(HALF):
            q = with_docs(join(lambda d, b: q2in[t, 2 * d + b]), 2, 3, t)
            problems.append((q,) + own_kv(t, 3) + (None,))
        for t, (o, lse) in enumerate(attend(problems)):
            for d in range(2):
                for b in range(2):
                    rows = slice((2 * d + b) * 16, (2 * d + b + 1) * 16)
                    os2[d, t, b] = o[rows].astype(BF16)
                    keep(st2, (d, b), slice(96, FAR), t, lse[rows])
        for d in range(2):
            for b in range(2):
                ls2[d, b] = st2[d, b].T[:HALF]
        for d in range(2):
            two_stats(d).start()
        for d in range(2):
            two_back(d).start()

    l_own = remote(ls_own.at[1 - j], lo_in, l_own_send, l_recv.at[0], device(0, 1 - j))
    l_own.start()
    l_own.wait_recv()

    mine = ls_own[j]
    theirs = lo_in[...]
    lower = jnp.where(j == 0, mine, theirs)
    upper = jnp.where(j == 0, theirs, mine)
    wide = iota((1, CHUNK), 1)
    own = jnp.concatenate([lower[0], upper[0], lower[1], upper[1]], axis=0)
    own = jnp.where(wide < SEL, own, NEG)
    tall = iota((CHUNK, CHUNK), 0)
    own3 = split3(own)
    zeroth = lse0[...].T
    parts = [jnp.concatenate([zeroth[:HEADS, :CHUNK], zeroth[:HEADS, CHUNK:]], axis=0)]
    spread, chosen = [], []
    for level, (first, count, bits) in enumerate(REGIONS):
        hit = ((iota((CHUNK, CHUNK), 1) >> bits) == tall - first) & (tall >= first) & (tall < first + count)
        spread.append(jnp.where(hit, 1.0, 0.0).astype(BF16))
        chosen.append(picked(off_ref, level, bits))
        parts.append(jnp.where(chosen[level], fold3(nn(own3, spread[level])), NEG))
    lse = log_sum(parts)
    back = jnp.zeros((2 * HEADS, CHUNK), F32)
    for level in range(4):
        back = back + fold3(nt(split3(jnp.where(chosen[level], lse, 0.0)), spread[level]))
    al_own[...] = jnp.exp2(own - back)
    lse_loc[...] = lse
    for b in range(2):
        span = slice(b * CHUNK, (b + 1) * CHUNK)
        a0[span] = jnp.exp2(lse0[span] - upright(lse, b))

    def loc_copy(h):
        return pltpu.make_async_copy(loc.at[h], loc_out.at[h], store_sem)

    own_first = jnp.where(wide < 128, 0, jnp.where(wide < 192, 128, jnp.where(wide < 224, 192, 224)))
    own_bits = jnp.where(wide < 128, 1, jnp.where(wide < 192, 2, jnp.where(wide < 224, 3, 4)))
    own_base = tall - ((wide - own_first) << own_bits)

    got(oo_in.at[:, :, pl.ds(0, SEL)], oo_recv)

    def local_head(t, _):
        for which in range(2):
            h = HALF * j + t if which == 0 else HALF * (1 - j) + t
            o1, o2, o3, o4 = [off_ref[i, h] & (2 << i) - 1 for i in range(4)]
            shift = jnp.where(wide < 128, o1, jnp.where(wide < 192, o2, jnp.where(wide < 224, o3, o4)))
            hit = own_base == shift
            for b in range(2):
                span = slice(b * CHUNK, (b + 1) * CHUNK)
                weight = jnp.where(hit, al_own[pl.ds(b * HEADS + h, 1), :], 0.0).astype(BF16)
                mixed = nn(weight, ob[j, t, b] if which == 0 else oo_in[t, b])
                scale = jnp.sum(jnp.where(lane == h, a0[span], 0.0), axis=1, keepdims=True)
                loc[h, span] = (mixed + scale * o0[h, span]).astype(BF16)
            loc_copy(h).start()
        return 0

    lax.fori_loop(0, HALF, local_head, 0)

    @pl.when(c >= 1)
    def _():
        for i in range(2):
            got(lr1.at[i], l_recv.at[1 + i])

    @pl.when(c == 5)
    def _():
        for i in range(2):
            got(lr2.at[i], l_recv.at[3 + i])

    one, two = [
        jnp.concatenate([ref[0, 0], ref[1, 0], ref[0, 1], ref[1, 1]], axis=0) for ref in (lr1, lr2)
    ]
    far = jnp.where((lane >= 96) & (c == 5), two, one)
    far = jnp.where(valid_row(lane, c), far, NEG)
    far3 = split3(far)
    tall = iota((DIM, CHUNK), 0) + DIM
    parts, spread, chosen = [lse_loc[...]], [], []
    for level, (first, count, bits) in enumerate(REGIONS):
        if level > 0:
            hit = ((iota((DIM, CHUNK), 1) >> bits) == tall - first) & (tall >= first) & (tall < first + count)
            spread.append(jnp.where(hit, 1.0, 0.0).astype(BF16))
            chosen.append(picked(off_ref, level, bits))
            parts.append(jnp.where(chosen[-1], fold3(nn(far3, spread[-1])), NEG))
    lse = log_sum(parts)
    back = jnp.zeros((2 * HEADS, DIM), F32)
    for pick, wide in zip(chosen, spread):
        back = back + fold3(nt(split3(jnp.where(pick, lse, 0.0)), wide))
    al_far[...] = jnp.exp2(far - back)
    portion = jnp.exp2(lse_loc[...] - lse)
    for b in range(2):
        share[b * CHUNK : (b + 1) * CHUNK] = upright(portion, b)
    al_copy = pltpu.make_async_copy(al_far, al_out, al_sem)
    share_copy = pltpu.make_async_copy(share, share_out, lse_sem)
    al_copy.start()
    share_copy.start()

    for present, slots in (((c > 0) & (c < 7) & (c != 5), 5), ((c == 0) | (c == 7), 3), (c == 5, 7)):

        @pl.when(present)
        def _():
            part = docs_all.at[pl.ds(0, slots)]
            remote(part, part, d_send, d_recv.at[0], device(0, 1 - j)).wait_send()

    l_own.wait_send()

    al_copy.wait()
    share_copy.wait()
    sent(sx, x_send)
    sent(oo_in.at[:, :, pl.ds(0, SEL)], oo_send)
    pltpu.make_async_copy(loc, loc_out, store_sem).wait()
    for present, pieces in far_pieces(c):

        @pl.when(present)
        def _():
            sent(q1in.at[:, :, pl.ds(0, size_of(pieces))], q_send)

    for present, (low, high) in next_pieces(c):

        @pl.when(present)
        def _():
            sent(kvp.at[:, :, :, pl.ds(0, high - low)], k_send)

    for present, pieces in far_pieces(c + 1):

        @pl.when(present & (c <= 6))
        def _():
            sent(os1.at[:, :, :, pl.ds(0, size_of(pieces))], o_send)
            sent(ls1, l_send)

    @pl.when(c == 3)
    def _():
        sent(os2, o_two_send)
        sent(ls2, l_two_send)

    @pl.when(c == 5)
    def _():
        sent(q2in, two_send)
        got(far_out.at[:, :, pl.ds(0, 16)], o_two_recv)

    for present, pieces in far_pieces(c):

        @pl.when(present)
        def _():
            got(far_out.at[:, :, pl.ds(0, size_of(pieces))], o_recv)


def valid_row(x, c):
    return ((x < 64) & (c % 2 == 1)) | ((x >= 64) & (x < 96) & (c % 4 >= 2)) | ((x >= 96) & (x < FAR) & (c >= 2))


def picked(off_ref, level, bits):
    head = iota((HEADS, CHUNK), 0)
    shifts = jnp.zeros((HEADS, CHUNK), I32)
    for h in range(HEADS):
        shifts = jnp.where(head == h, off_ref[level, h] & ((1 << bits) - 1), shifts)
    pick = (iota((HEADS, CHUNK), 1) & ((1 << bits) - 1)) == shifts
    return jnp.concatenate([pick, pick], axis=0)


def log_sum(parts):
    top = parts[0]
    for part in parts[1:]:
        top = jnp.maximum(top, part)
    total = jnp.exp2(parts[0] - top)
    for part in parts[1:]:
        total = total + jnp.exp2(part - top)
    return top + jnp.log2(total)


def upright(dense, b):
    pad = jnp.zeros((DIM - HEADS, CHUNK), F32)
    return jnp.concatenate([dense[b * HEADS : (b + 1) * HEADS], pad], axis=0).T


GROUP = 8


def join_kernel(loc_ref, far_ref, al_far, a_loc, off_ref, out_ref):
    c = lax.axis_index("ctx") // 2
    lane = iota((1, DIM), 1)

    sent = valid_row(iota((DIM, DIM), 0), c)
    row = lane + DIM
    first = jnp.where(row < 192, 128, jnp.where(row < 224, 192, 224))
    bits = jnp.where(row < 192, 2, jnp.where(row < 224, 3, 4))
    base = iota((CHUNK, DIM), 0) - ((row - first) << bits)
    for i in range(GROUP):
        h = pl.program_id(0) * GROUP + i
        o2, o3, o4 = [off_ref[level, h] & (2 << level) - 1 for level in (1, 2, 3)]
        hit = base == jnp.where(row < 192, o2, jnp.where(row < 224, o3, o4))
        for b in range(2):
            span = slice(b * CHUNK, (b + 1) * CHUNK)
            weight = jnp.where(hit, al_far[pl.ds(b * HEADS + h, 1), :], 0.0).astype(BF16)
            mixed = nn(weight, jnp.where(sent, far_ref[i, b], jnp.zeros((DIM, DIM), BF16)))
            scale = jnp.sum(jnp.where(lane == h, a_loc[span], 0.0), axis=1, keepdims=True)
            out_ref[0, span, i * DIM : (i + 1) * DIM] = (mixed + scale * loc_ref[i, span].astype(F32)).astype(BF16)


def on_device(queries, key_rows, value_rows, document_ids, dilation_offsets):
    any_space = pl.BlockSpec(memory_space=pl.ANY)
    smem = pl.BlockSpec(memory_space=pltpu.SMEM)
    dma = pltpu.SemaphoreType.DMA

    def vmem(*shape, kind=BF16):
        return pltpu.VMEM(shape, kind)

    local, far, far_share, local_share = pl.pallas_call(
        kernel,
        out_shape=(
            jax.ShapeDtypeStruct((HEADS, ROWS, DIM), BF16),
            jax.ShapeDtypeStruct((HEADS, 2, DIM, DIM), BF16),
            jax.ShapeDtypeStruct((2 * HEADS, DIM), F32),
            jax.ShapeDtypeStruct((ROWS, DIM), F32),
        ),
        in_specs=[any_space] * 5,
        out_specs=(any_space,) * 4,
        scratch_shapes=[
            vmem(1, ROWS, kind=I32), pltpu.SMEM((4, HEADS), I32), vmem(3, ROWS, HEADS * DIM),
            vmem(HALF, 3, 4, SEL, DIM), vmem(HALF, 3, 2, SEL, DIM), vmem(HALF, 4, FAR, DIM), vmem(HALF, 4, 16, DIM),
            vmem(HALF, 2, 4, FAR3, DIM),
            vmem(HALF, SEL, CHUNK), vmem(2, HALF, SEL, CHUNK), vmem(2, HALF, FAR3, CHUNK), vmem(HALF, SEL, CHUNK),
            vmem(2, HALF, 2, CHUNK, DIM), vmem(HALF, 2, CHUNK, DIM), vmem(2, HALF, 2, FAR, DIM), vmem(2, HALF, 2, 16, DIM),
            vmem(HEADS, ROWS, DIM, kind=F32), vmem(HEADS, ROWS, DIM),
            vmem(2, 2, CHUNK, DIM, kind=F32), vmem(2, 2, DIM, DIM, kind=F32), vmem(2, 2, DIM, DIM, kind=F32),
            vmem(ROWS, DIM, kind=F32),
            vmem(2, 2, HALF, CHUNK, kind=F32), vmem(2, 2, HALF, DIM, kind=F32), vmem(2, 2, HALF, DIM, kind=F32),
            vmem(2, HALF, CHUNK, kind=F32), vmem(2, 2, HALF, DIM, kind=F32), vmem(2, 2, HALF, DIM, kind=F32),
            vmem(2 * HEADS, CHUNK, kind=F32),
            vmem(8, 1, ROWS, kind=I32), vmem(2 * DIM, CHUNK), vmem(4, 2 * DIM, CHUNK),
            vmem(SEL, CHUNK, kind=I32), vmem(CHUNK, CHUNK, kind=F32), vmem(2, CHUNK, CHUNK, kind=F32),
            vmem(2 * HEADS, CHUNK, kind=F32), vmem(ROWS, DIM, kind=F32),
            vmem(2 * HEADS, DIM, kind=F32), vmem(ROWS, DIM, kind=F32),
            dma((6,)), dma((18,)), dma((8,)), dma((HALF,)), dma((HALF,)), dma((HALF,)), dma((5,)),
        ],
        compiler_params=pltpu.CompilerParams(collective_id=0, has_side_effects=True, vmem_limit_bytes=56 << 20),
        name="dilated_attention",
    )(queries, key_rows, value_rows, document_ids, dilation_offsets)
    return pl.pallas_call(
        join_kernel,
        grid=(HEADS // GROUP,),
        out_shape=jax.ShapeDtypeStruct((1, ROWS, HEADS * DIM), BF16),
        in_specs=[
            pl.BlockSpec((GROUP, ROWS, DIM), lambda i: (i, 0, 0)),
            pl.BlockSpec((GROUP, 2, DIM, DIM), lambda i: (i, 0, 0, 0)),
            pl.BlockSpec(memory_space=pltpu.VMEM),
            pl.BlockSpec(memory_space=pltpu.VMEM),
            smem,
        ],
        out_specs=pl.BlockSpec((1, ROWS, GROUP * DIM), lambda i: (0, 0, i)),
        compiler_params=pltpu.CompilerParams(vmem_limit_bytes=60 << 20),
        name="join_far",
    )(local, far, far_share, local_share, dilation_offsets)


def solution(mesh):
    placed = (P("dp", "ctx", None), P("dp", "ctx", None), P("dp", "ctx", None), P("dp", "ctx"), P())
    return jax.shard_map(
        on_device, mesh=mesh, in_specs=placed, out_specs=P("dp", "ctx", None), check_vma=False
    )
```
